128 devices in a mesh: tx: 8 (over x_hi, z), ty: 16 (over x_lo, y, core).
Axes of the slice: x: 4 (x_hi: 2, x_lo: 2; x = x_hi * 2 + x_lo), y: 4, z: 4, core: 2. Of those that a mesh axis runs over, the one named last changes fastest.
Arguments:
- reduced_heat: float32 [8, 512, 1024], P(None, 'ty', 'tx'), may hold values from 0.3 to 1.2
- substance_kind: int32 [8, 512, 1024], P(None, 'ty', 'tx'), may hold values from 0 to 3
- moment_vector: float32 [3, 8, 512, 1024], P(None, None, 'ty', 'tx'), may hold values from -4 to 4
- stray_tensor: float32 [6, 16, 1024, 2048], P(None, 'tx', None, 'ty'), may hold values from -8 to 8
- diffusivity_nodes: float32 [16], replicated, may hold values from 0.5 to 1.5
- substance_factor: float32 [4], replicated, may hold values from 0.5 to 2
- ordering_threshold: float32 [4], replicated, may hold values from 0.7 to 1.1
- beam_transverse_spot: int32 [2], replicated, may hold values from 0 to 511
- beam_downtrack_spot: int32 [2], replicated, may hold values from 0 to 1023
Outputs:
- warmed_state: float32 [8, 512, 1024], P(None, 'ty', 'tx')
- demag_field: float32 [3, 8, 512, 1024], P(None, None, 'ty', 'tx')
The draws below stay inside these ranges and needn't reach their ends.
All inputs are finite; a program needn't handle non-finite values.
Results may differ from the reference program's by a relative error of at most 0.00007.
Values sent between devices are 32-bit elements; how exact they have to be, the bound alone decides.
No kernel may reach another device: no remote copies, remote signals or barrier semaphores. Data moves between devices by JAX's collectives and lax.ppermute only.
A program may use at most 128 MiB of HBM per device.

```python
import math
import jax
import jax.numpy as jnp
from jax import lax

CX = 128
CY = 32
FILM_SHEETS = 8
SWEEPS = 2
TABLE = 16
SUBSTANCE_KINDS = 4
DOWNTRACK_SITES = 1024
TRANSVERSE_SITES = 512


def plant(values, rng, smallest, largest):
    longest = values.shape.index(max(values.shape))
    spots = []
    for shift in (0, 1):
        where = [jax.random.randint(jax.random.fold_in(rng, axis), (), 0, length) for axis, length in enumerate(values.shape)]
        where[longest] = (where[longest] + shift) % values.shape[longest]
        spots.append(tuple(where))
    return values.at[spots[0]].set(smallest).at[spots[1]].set(largest)


def levels(stream_key, shape, pieces, smallest, top_value):
    gain, own = 1.0, jax.random.fold_in(stream_key, 6)
    for axis_at, blocks in pieces:
        steps = jnp.exp(jax.random.uniform(jax.random.fold_in(own, axis_at), (blocks,), jnp.float32, smallest / len(pieces), top_value / len(pieces)))
        gain = gain * jnp.repeat(steps, shape[axis_at] // blocks).reshape([-1 if axis == axis_at else 1 for axis in range(len(shape))])
    return gain


def noise(own_key, shape, deviation, bound, cuts=(), held_as=jnp.bfloat16):
    factor_of = levels(own_key, shape, cuts, -0.22, 0.18) if cuts else 1.0
    values = jax.random.normal(own_key, shape, jnp.float32) * deviation * factor_of
    return jnp.minimum(jnp.maximum(values, -bound), bound).astype(held_as)


def setup_inputs(seed: int = 0) -> dict:
    keys = jax.random.split(jax.random.key(seed), 10)
    reduced_heat = jnp.clip(0.3 + 0.90000004 * jax.random.uniform(keys[0], (FILM_SHEETS, TRANSVERSE_SITES, DOWNTRACK_SITES), jnp.float32) ** levels(keys[0], (FILM_SHEETS, TRANSVERSE_SITES, DOWNTRACK_SITES), ((1, 16), (2, 8)), -0.2, 0.2), 0.3, 1.2)
    substance_kind = plant(jax.random.randint(keys[1], (FILM_SHEETS, TRANSVERSE_SITES, DOWNTRACK_SITES), 0, SUBSTANCE_KINDS), jax.random.fold_in(keys[1], 1), 0, SUBSTANCE_KINDS - 1).astype(jnp.int32)
    moment_vector = noise(keys[2], (3, FILM_SHEETS, TRANSVERSE_SITES, DOWNTRACK_SITES), 0.6, 4.0, ((2, 16), (3, 8)), jnp.float32)
    stray_tensor = noise(keys[3], (6, 2 * FILM_SHEETS, 2 * TRANSVERSE_SITES, 2 * DOWNTRACK_SITES), 2.0, 8.0, ((1, 8), (3, 16)), jnp.float32)
    diffusivity_nodes = jnp.clip(jnp.exp(jax.random.uniform(keys[4], (TABLE,), jnp.float32, math.log(0.5), math.log(1.5))), 0.5, 1.5)
    substance_factor = jnp.clip(jnp.exp(jax.random.uniform(keys[5], (SUBSTANCE_KINDS,), jnp.float32, math.log(0.5), math.log(2.0))), 0.5, 2.0)
    ordering_threshold = jnp.clip(jax.random.uniform(keys[6], (SUBSTANCE_KINDS,), jnp.float32, 0.7, 1.1), 0.7, 1.1)
    beam_transverse_spot = jax.random.randint(keys[7], (SWEEPS,), 0, TRANSVERSE_SITES).astype(jnp.int32)
    beam_downtrack_spot = jax.random.randint(keys[8], (SWEEPS,), 0, DOWNTRACK_SITES).astype(jnp.int32)
    return {"reduced_heat": reduced_heat, "substance_kind": substance_kind, "moment_vector": moment_vector, "stray_tensor": stray_tensor, "diffusivity_nodes": diffusivity_nodes, "substance_factor": substance_factor, "ordering_threshold": ordering_threshold, "beam_transverse_spot": beam_transverse_spot, "beam_downtrack_spot": beam_downtrack_spot}


AMBIENT_HEAT = 0.3
STEP_RATE = 0.05
LASER_POWER = 4.0
LASER_DEPTH = 4.0
ORDERING_SPREAD = 0.08
TABLE_LOW = 0.2
TABLE_SPAN = 1.6


def lookup_diffusivity(absolute, diffusivity_nodes):
    nodes = diffusivity_nodes.shape[0]
    spacing = TABLE_SPAN / (nodes - 1)
    total = jnp.zeros_like(absolute) + diffusivity_nodes[0]
    for index in range(nodes - 1):
        start_node = TABLE_LOW + index * spacing
        total = total + (diffusivity_nodes[index + 1] - diffusivity_nodes[index]) * jnp.clip((absolute - start_node) / spacing, 0.0, 1.0)
    return total


def per_particle(substance_kind, values):
    result = jnp.zeros(substance_kind.shape, jnp.float32)
    for grain in range(values.shape[0]):
        result = result + jnp.where(substance_kind == grain, values[grain], 0.0)
    return result


def laser_heating(row_ids, col_ids, sheet_indices, spot_row, spot_col, total_cols, col_width, row_width):
    along = ((col_ids - spot_col + total_cols // 2) % total_cols - total_cols // 2).astype(jnp.float32) / col_width
    across = (row_ids - spot_row).astype(jnp.float32) / row_width
    col_factor = jnp.exp(-0.5 * along * along)
    row_factor = jnp.exp(-0.5 * across * across)
    layer_factor = jnp.exp(-jnp.arange(sheet_indices, dtype=jnp.float32) / LASER_DEPTH)
    return layer_factor[:, None, None] * row_factor[None, :, None] * col_factor[None, None, :]


def heat_update(center, diffusivity, neighbours, heating):
    flux = jnp.zeros_like(center)
    for other_temp, other_cond in neighbours:
        flux = flux + 0.5 * (diffusivity + other_cond) * (other_temp - center)
    vertical = 0.5 * (diffusivity[1:] + diffusivity[:-1]) * (center[1:] - center[:-1])
    zero_layer = jnp.zeros_like(center[:1])
    flux = flux + jnp.concatenate([vertical, zero_layer], 0) - jnp.concatenate([zero_layer, vertical], 0)
    return center + STEP_RATE * (flux + LASER_POWER * heating)


def reference(reduced_heat, substance_kind, moment_vector, stray_tensor, diffusivity_nodes, substance_factor, ordering_threshold, beam_transverse_spot, beam_downtrack_spot):
    rotation_phase = reduced_heat - AMBIENT_HEAT
    site_multiplier = per_particle(substance_kind, substance_factor)
    row_ids = jnp.arange(TRANSVERSE_SITES, dtype=jnp.int32)
    col_ids = jnp.arange(DOWNTRACK_SITES, dtype=jnp.int32)
    for sweep in range(SWEEPS):
        diffusivity = site_multiplier * lookup_diffusivity(rotation_phase + AMBIENT_HEAT, diffusivity_nodes)
        padded_temp = jnp.pad(rotation_phase, ((0, 0), (1, 1), (0, 0)))
        padded_cond = jnp.pad(diffusivity, ((0, 0), (1, 1), (0, 0)))
        neighbours = [(jnp.roll(rotation_phase, 1, axis=2), jnp.roll(diffusivity, 1, axis=2)),
                      (jnp.roll(rotation_phase, -1, axis=2), jnp.roll(diffusivity, -1, axis=2)),
                      (padded_temp[:, :-2], padded_cond[:, :-2]),
                      (padded_temp[:, 2:], padded_cond[:, 2:])]
        heating = laser_heating(row_ids, col_ids, FILM_SHEETS, beam_transverse_spot[sweep], beam_downtrack_spot[sweep], DOWNTRACK_SITES, 0.5 * CX, 1.0 * CY)
        rotation_phase = heat_update(rotation_phase, diffusivity, neighbours, heating)
    warmed_state = rotation_phase + AMBIENT_HEAT
    proportion = jax.nn.sigmoid((per_particle(substance_kind, ordering_threshold) - warmed_state) / ORDERING_SPREAD)
    scaled = moment_vector * proportion[None]
    depth = jnp.fft.fft(jnp.pad(scaled, ((0, 0), (0, FILM_SHEETS), (0, 0), (0, 0))), axis=1)
    pairs = ((0, 3, 4), (3, 1, 5), (4, 5, 2))

    def one_layer(index):
        plane = lax.dynamic_index_in_dim(depth, index, 1, keepdims=False)
        taps = lax.dynamic_index_in_dim(stray_tensor, index, 1, keepdims=False)
        spectra = jnp.fft.fft2(jnp.pad(plane, ((0, 0), (0, TRANSVERSE_SITES), (0, DOWNTRACK_SITES))))
        fields = []
        for target in range(3):
            total = taps[pairs[target][0]] * spectra[0] + taps[pairs[target][1]] * spectra[1] + taps[pairs[target][2]] * spectra[2]
            fields.append(-total)
        return jnp.fft.ifft2(jnp.stack(fields))[:, :TRANSVERSE_SITES, :DOWNTRACK_SITES]

    planes = lax.map(one_layer, jnp.arange(2 * FILM_SHEETS, dtype=jnp.int32))
    demag = jnp.real(jnp.fft.ifft(planes, axis=0))[:FILM_SHEETS]
    demag_field = jnp.transpose(demag, (1, 0, 2, 3)).astype(jnp.float32)
    return warmed_state, demag_field
```

```python
import functools
import math

import jax
import jax.numpy as jnp
import ml_dtypes
import numpy as np
from jax import lax
from jax.experimental import pallas as pl
from jax.experimental.pallas import tpu as pltpu
from jax.sharding import PartitionSpec as P

SWEEPS = 2
AMBIENT_HEAT = 0.3
STEP_RATE = 0.05
LASER_POWER = 4.0
LASER_DEPTH = 4.0
ORDERING_SPREAD = 0.08
TABLE_LOW = 0.2
TABLE_SPAN = 1.6
RADIX = 4
PAIRS = ((0, 3, 4), (3, 1, 5), (4, 5, 2))
VMEM = pl.BlockSpec(memory_space=pltpu.VMEM)
SMEM = pl.BlockSpec(memory_space=pltpu.SMEM)
PARAMS = pltpu.CompilerParams(vmem_limit_bytes=50 * 1024 * 1024)
F32 = jnp.float32
BF16 = jnp.bfloat16


def two_terms(table):
    table = np.asarray(table, np.float64)
    high = table.astype(np.float32).astype(ml_dtypes.bfloat16)
    low = (table - high.astype(np.float64)).astype(np.float32).astype(ml_dtypes.bfloat16)
    return (high, low)


def waves(products, length):
    angles = 2.0 * math.pi / length * (products % length)
    return (np.cos(angles), np.sin(angles))


def split(values):
    high = values.astype(BF16)
    low = (values - high.astype(F32)).astype(BF16)
    return (high, low)


def matmul(left, right):
    return lax.dot_general(left, right, (((1,), (0,)), ((), ())), preferred_element_type=F32)


def layer_tables(layers, strips, comps, order):
    count = 2 * layers
    owners = count // 2
    rows_in = comps * strips * layers
    if order == "whole":
        shape = (owners, 2, comps, 2, strips)
    else:
        shape = (2, owners, comps, 2, strips)
    index = np.indices(shape).reshape(5, -1)
    if order == "whole":
        owner, member, comp, part, strip = index
    else:
        member, owner, comp, part, strip = index
    freq = 2 * owner + member
    comp_in, strip_in, layer_in = np.indices((comps, strips, layers)).reshape(3, -1)
    same = (comp[:, None] == comp_in[None]) & (strip[:, None] == strip_in[None])
    cosine, sine = waves(freq[:, None] * layer_in[None], count)
    zero = part[:, None] == 0
    from_real = np.where(zero, cosine, -sine) * same
    from_imag = np.where(zero, sine, cosine) * same
    forward = np.concatenate([from_real, from_imag], 1)
    return forward, forward.T


def along_tables(points, devices):
    length = 2 * points
    span = length // RADIX
    sub = points // RADIX
    a = np.arange(sub)
    v = np.arange(span)
    forward = np.zeros((RADIX, sub, 2 * span))
    for b in range(RADIX):
        cosine, sine = waves(v[None, :] * (RADIX * a + b)[:, None], length)
        forward[b] = np.concatenate([cosine, -sine], 1)
    order = np.zeros((points, points), np.float32)
    for b in range(RADIX):
        order[RADIX * a + b, b * sub + a] = 1.0
    return forward, forward.transpose(0, 2, 1), order.astype(ml_dtypes.bfloat16)


def across_tables(points, groups, blocks, strips):
    length = 2 * points
    span = length // RADIX
    quarter, block, part, strip = np.indices((groups // RADIX, blocks, 2, strips)).reshape(4, -1)
    v = np.arange(span)
    forward = np.zeros((RADIX, 2 * span, quarter.size))
    for b in range(RADIX):
        y = groups * strips * block + groups * strip + RADIX * quarter + b
        cosine, sine = waves(v[:, None] * y[None, :], length)
        zero = part[None, :] == 0
        forward[b, :span] = np.where(zero, cosine, sine)
        forward[b, span:] = np.where(zero, -sine, cosine)
    return forward, forward.transpose(0, 2, 1)


def edges_kernel(heat, kind, factor, sides, rows):
    layers, count = 8, heat.shape[0] // 8
    lane = lax.broadcasted_iota(jnp.int32, (layers, 128), 1)
    packed = [jnp.zeros((layers, 128), F32), jnp.zeros((layers, 128), F32)]
    for y in range(count):
        theta = heat[pl.ds(y, layers, stride=count), :]
        which = kind[pl.ds(y, layers, stride=count), :]
        gain = jnp.zeros_like(theta)
        for grain in range(4):
            gain = gain + jnp.where(which == grain, factor[grain], 0.0)
        for at, value in enumerate((theta, gain)):
            turned = pltpu.roll(value, (2 + 4 * y) % 128, 1)
            packed[at] = jnp.where(lane // 4 == y, turned, packed[at])
            if y < 2:
                rows[0, at, y] = value
            if y >= count - 2:
                rows[1, at, y - count + 2] = value
    sides[0] = packed[0]
    sides[1] = packed[1]


def heat_kernel(
    heat, kind, moment, above, below, left, right, up_left, up_right, down_left, down_right,
    nodes, factor, threshold, spot_row, spot_col, place, warmed, scaled, *, total_rows, total_cols
):
    layers, count = 8, heat.shape[0] // 8
    width = 128
    col_base = place[0] * width
    row_base = place[1] * count
    lane = lax.broadcasted_iota(jnp.int32, (layers, width), 1)
    first = lane == 0
    last = lane == width - 1
    low = lane < width // 2
    depth = lax.broadcasted_iota(jnp.int32, (layers, width), 0)
    spacing = TABLE_SPAN / (nodes.shape[0] - 1)
    slopes = [(nodes[j + 1] - nodes[j]) * (1.0 / spacing) for j in range(nodes.shape[0] - 1)]

    def conductivity(theta, gain):
        absolute = theta + AMBIENT_HEAT
        total = jnp.zeros_like(theta) + nodes[0]
        for j, slope in enumerate(slopes):
            total = total + slope * jnp.clip(absolute - (TABLE_LOW + j * spacing), 0.0, spacing)
        return gain * total

    inside_top = (row_base > 0).astype(F32)
    inside_bottom = (row_base + count < total_rows).astype(F32)
    start = AMBIENT_HEAT
    main = {}
    gains = {}
    for y in range(count):
        which = kind[pl.ds(y, layers, stride=count), :]
        gain = jnp.zeros((layers, width), F32)
        for grain in range(4):
            gain = gain + jnp.where(which == grain, factor[grain], 0.0)
        gains[y] = gain
        main[y] = heat[pl.ds(y, layers, stride=count), :] - start
    for j in range(2):
        main[j - 2] = (above[0, j] - start) * inside_top
        gains[j - 2] = above[1, j] * inside_top
        main[count + j] = (below[0, j] - start) * inside_bottom
        gains[count + j] = below[1, j] * inside_bottom

    def side(at, y, to_left, to_right):
        turn = (128 - (2 + 4 * y)) % 128
        return jnp.where(low, pltpu.roll(to_right[at], turn, 1), pltpu.roll(to_left[at], turn, 1))

    flank = {}
    flank_gain = {}
    for y in range(count):
        flank[y] = side(0, y, left, right) - start
        flank_gain[y] = side(1, y, left, right)
    flank[-1] = (side(0, count - 1, up_left, up_right) - start) * inside_top
    flank_gain[-1] = side(1, count - 1, up_left, up_right) * inside_top
    flank[count] = (side(0, 0, down_left, down_right) - start) * inside_bottom
    flank_gain[count] = side(1, 0, down_left, down_right) * inside_bottom

    def heating(y, sweep, along):
        across = (row_base + y - spot_row[sweep]).astype(F32) * (1.0 / 32.0)
        across = jnp.full((layers, width), -0.5, F32) * (across * across)
        return along * jnp.exp(across)

    def along_of(columns, sweep):
        shifted = columns - spot_col[sweep] + total_cols // 2
        shifted = jnp.where(shifted < 0, shifted + total_cols, shifted)
        shifted = jnp.where(shifted >= total_cols, shifted - total_cols, shifted)
        offset = (shifted - total_cols // 2).astype(F32) * (1.0 / (0.5 * width))
        return jnp.exp(depth.astype(F32) * (-1.0 / LASER_DEPTH)) * jnp.exp(-0.5 * offset * offset)

    main_columns = col_base + lane
    flank_columns = jnp.where(low, lane + width, lane - width) + col_base
    flank_columns = jnp.where(flank_columns < 0, flank_columns + total_cols, flank_columns)
    flank_columns = jnp.where(
        flank_columns >= total_cols, flank_columns - total_cols, flank_columns
    )
    not_top = depth > 0
    not_bottom = depth < layers - 1

    def before(value, other):
        return jnp.where(first, pltpu.roll(other, 1, 1), pltpu.roll(value, 1, 1))

    def after(value, other):
        return jnp.where(last, pltpu.roll(other, width - 1, 1), pltpu.roll(value, width - 1, 1))

    def step(theta, k, sides, up, down, source):
        flux = jnp.zeros_like(theta)
        for other, other_k in sides + (up, down):
            flux = flux + (k + other_k) * (other - theta)
        below_flux = (k + pltpu.roll(k, layers - 1, 0)) * (pltpu.roll(theta, layers - 1, 0) - theta)
        above_flux = (k + pltpu.roll(k, 1, 0)) * (pltpu.roll(theta, 1, 0) - theta)
        flux = flux + jnp.where(not_bottom, below_flux, 0.0) + jnp.where(not_top, above_flux, 0.0)
        return theta + STEP_RATE * (0.5 * flux + LASER_POWER * source)

    def flanked(value, other):
        return before(value, other), after(value, other)

    for sweep in range(SWEEPS):
        reach = SWEEPS - 1 - sweep
        k_main = {y: conductivity(main[y], gains[y]) for y in range(-1 - reach, count + 1 + reach)}
        k_flank = {
            y: conductivity(flank[y], flank_gain[y]) for y in range(-reach, count + reach)
        }
        along_main = along_of(main_columns, sweep)
        along_flank = along_of(flank_columns, sweep)
        fresh = {}
        fresh_flank = {}
        for y in range(-reach, count + reach):
            lt, rt = flanked(main[y], flank[y])
            lk, rk = flanked(k_main[y], k_flank[y])
            value = step(
                main[y], k_main[y], ((lt, lk), (rt, rk)),
                (main[y - 1], k_main[y - 1]), (main[y + 1], k_main[y + 1]),
                heating(y, sweep, along_main),
            )
            if y < 0:
                value = value * inside_top
            if y >= count:
                value = value * inside_bottom
            fresh[y] = value
            if reach and 0 <= y < count:
                lt, rt = flanked(flank[y], main[y])
                lk, rk = flanked(k_flank[y], k_main[y])
                fresh_flank[y] = step(
                    flank[y], k_flank[y], ((lt, lk), (rt, rk)),
                    (flank[y - 1], k_flank[y - 1]), (flank[y + 1], k_flank[y + 1]),
                    heating(y, sweep, along_flank),
                )
        main, flank = fresh, fresh_flank

    groups = scaled.shape[0]
    for y in range(count):
        value = main[y] + AMBIENT_HEAT
        warmed[pl.ds(y, layers, stride=count), :] = value
        which = kind[pl.ds(y, layers, stride=count), :]
        limit = jnp.zeros((layers, width), F32)
        for grain in range(4):
            limit = limit + jnp.where(which == grain, threshold[grain], 0.0)
        fraction = 1.0 / (1.0 + jnp.exp((value - limit) * (1.0 / ORDERING_SPREAD)))
        strip, group = divmod(y, groups)
        for comp in range(3):
            source = moment[pl.ds(comp * layers * count + y, layers, stride=count), :]
            at = (comp * (count // groups) + strip) * layers
            scaled[group, at : at + layers, :] = source * fraction


def turns(t, sign):
    (ar, ai), (br, bi), (cr, ci), (dr, di) = t
    er, ei, fr, fi = ar + cr, ai + ci, ar - cr, ai - ci
    gr, gi, hr, hi = br + dr, bi + di, br - dr, bi - di
    minus = (fr + hi, fi - hr)
    plus = (fr - hi, fi + hr)
    one, three = (minus, plus) if sign < 0 else (plus, minus)
    return ((er + gr, ei + gi), one, (er - gr, ei - gi), three)


def rows_kernel(block, order, high, low, layer_high, layer_low, *outs):
    groups, lines, width = block.shape
    points = groups * width
    sub = points // RADIX
    span = high.shape[2] // 2
    values = jnp.concatenate([block[t] for t in range(groups)], 1)
    both = jnp.concatenate(split(values), 0)
    both = matmul(both, order[...]).astype(BF16)
    parts = []
    for b in range(RADIX):
        data = both[:, b * sub : (b + 1) * sub]
        total = matmul(data, high[b])
        total = total[:lines] + total[lines:] + matmul(data[:lines], low[b])
        parts.append((total[:, :span], total[:, span:]))
    slabs = span // width
    for u, (real, imag) in enumerate(turns(parts, -1)):
        data_high, data_low = split(jnp.concatenate([real, imag], 0))
        total = matmul(layer_high[...], data_high)
        total = total + matmul(layer_high[...], data_low)
        total = total + matmul(layer_low[...], data_high)
        each = total.shape[0] // len(outs)
        rows = each // groups
        blocks = RADIX * slabs
        for member, out in enumerate(outs):
            for t in range(groups):
                for slab in range(slabs):
                    out[t * blocks + u * slabs + slab] = total[
                        member * each + t * rows : member * each + (t + 1) * rows,
                        slab * width : (slab + 1) * width,
                    ]


def spectrum_kernel(data, tensor, high, low, back_high, back_low, out, sums, fields_high, fields_low):
    comps = 3
    senders, lines, width = data.shape
    blocks = 16
    quarters = senders // blocks // RADIX
    members = lines // (8 * comps)
    span = high.shape[1] // 2
    columns = comps * width
    for member in range(members):
        for b in range(RADIX):
            pieces = []
            for comp in range(comps):
                at = (member * comps + comp) * 8
                tall = [
                    data[(b + RADIX * q) * blocks : (b + RADIX * q + 1) * blocks, at : at + 8, :]
                    for q in range(quarters)
                ]
                pieces.append(jnp.concatenate(tall, 0).reshape(quarters * blocks * 8, width))
            data_high, data_low = split(jnp.concatenate(pieces, 1))
            total = matmul(high[b], data_high)
            total = total + matmul(high[b], data_low)
            total = total + matmul(low[b], data_high)
            sums[b] = total
        piece = 16

        def multiply(step, carry):
            at = pl.multiple_of(step * piece, piece)
            spectra = []
            for comp in range(comps):
                lanes = pl.ds(comp * width, width)
                t = [
                    (sums[b, pl.ds(at, piece), lanes], sums[b, pl.ds(span + at, piece), lanes])
                    for b in range(RADIX)
                ]
                spectra.append(turns(t, -1))
            field = [[None] * RADIX for _ in range(comps)]
            for u in range(RADIX):
                taps = [tensor[p, member, pl.ds(u * span + at, piece), :] for p in range(6)]
                for target in range(comps):
                    field[target][u] = tuple(
                        taps[PAIRS[target][0]] * spectra[0][u][part]
                        + taps[PAIRS[target][1]] * spectra[1][u][part]
                        + taps[PAIRS[target][2]] * spectra[2][u][part]
                        for part in range(2)
                    )
            for comp in range(comps):
                lanes = pl.ds(comp * width, width)
                for b, both in enumerate(turns(field[comp], 1)):
                    for part, value in enumerate(both):
                        data_high, data_low = split(value)
                        rows = pl.ds(part * span + at, piece)
                        fields_high[b, rows, lanes] = data_high
                        fields_low[b, rows, lanes] = data_low
            return carry

        lax.fori_loop(0, span // piece, multiply, 0)
        for b in range(RADIX):
            total = matmul(back_high[b], fields_high[b])
            total = total + matmul(back_high[b], fields_low[b])
            total = total + matmul(back_low[b], fields_high[b])
            for q in range(quarters):
                group = b + RADIX * q
                tall = total[q * blocks * 8 : (q + 1) * blocks * 8]
                for comp in range(comps):
                    at = (member * comps + comp) * 8
                    out[group * blocks : (group + 1) * blocks, at : at + 8, :] = tall[
                        :, comp * width : (comp + 1) * width
                    ].reshape(blocks, 8, width)


def cells_kernel(*refs, scale):
    *blocks_in, layer_high, layer_low, high, low, order, out = refs
    groups, lines, width = out.shape
    span = high.shape[1] // 2
    slabs = span // width
    blocks = RADIX * slabs
    pieces = []
    for u in range(RADIX):
        columns = []
        for slab in range(slabs):
            at = u * slabs + slab
            columns.append(
                jnp.concatenate([d[t * blocks + at] for d in blocks_in for t in range(groups)], 0)
            )
        data_high, data_low = split(jnp.concatenate(columns, 1))
        total = matmul(layer_high[...], data_high)
        total = total + matmul(layer_high[...], data_low)
        total = total + matmul(layer_low[...], data_high)
        pieces.append((total[:lines], total[lines:]))
    sorted_columns = []
    for b, both in enumerate(turns(pieces, 1)):
        data_high, data_low = split(jnp.concatenate(both, 1))
        total = matmul(data_high, high[b]) + matmul(data_low, high[b])
        sorted_columns.append(total + matmul(data_high, low[b]))
    values = jnp.concatenate(sorted_columns, 1) * scale
    data_high, data_mid = split(values)
    data_low = (values - data_high.astype(F32) - data_mid.astype(F32)).astype(BF16)
    total = matmul(jnp.concatenate([data_high, data_mid, data_low], 0), order[...])
    values = total[:lines] + total[lines : 2 * lines] + total[2 * lines :]
    for t in range(groups):
        out[t] = values[:, t * width : (t + 1) * width]


def place_kernel(block, out):
    groups, lines, width = block.shape
    layers = 8
    count = out.shape[0] // (3 * layers)
    strips = count // groups
    for comp in range(3):
        for y in range(count):
            strip, group = divmod(y, groups)
            at = (comp * strips + strip) * layers
            out[pl.ds(comp * layers * count + y, layers, stride=count), :] = block[
                group, at : at + layers, :
            ]


def call(kernel, out_shape, in_specs, scratch=(), flops=0, bytes_accessed=0):
    many = isinstance(out_shape, (list, tuple))
    return pl.pallas_call(
        kernel,
        out_shape=out_shape,
        in_specs=in_specs,
        out_specs=[VMEM] * len(out_shape) if many else VMEM,
        scratch_shapes=list(scratch),
        compiler_params=PARAMS,
        cost_estimate=pl.CostEstimate(
            flops=flops, bytes_accessed=bytes_accessed, transcendentals=0
        ),
    )


def local(
    tx, ty, order, heat, kind, moment, tensor, nodes, factor, threshold, spot_row, spot_col
):
    layers, count, width = heat.shape
    strips = count // tx
    comps = 3
    lines = comps * strips * layers
    points_x, points_y = tx * width, ty * count
    members = 2

    heat = heat.reshape(layers * count, width)
    kind = kind.reshape(layers * count, width)
    moment = moment.reshape(comps * layers * count, width)
    sides, rows = call(
        edges_kernel,
        [
            jax.ShapeDtypeStruct((2, layers, width), F32),
            jax.ShapeDtypeStruct((2, 2, 2, layers, width), F32),
        ],
        [VMEM, VMEM, SMEM],
    )(heat, kind, factor)

    def moved(value, step_x, step_y):
        pairs = []
        for x in range(tx):
            for y in range(ty):
                if 0 <= y + step_y < ty:
                    pairs.append((x * ty + y, (x + step_x) % tx * ty + y + step_y))
        return lax.ppermute(value, ("tx", "ty"), pairs)

    left = moved(sides, 1, 0)
    right = moved(sides, -1, 0)
    above = moved(rows[1], 0, 1)
    below = moved(rows[0], 0, -1)
    up_left = moved(sides, 1, 1)
    up_right = moved(sides, -1, 1)
    down_left = moved(sides, 1, -1)
    down_right = moved(sides, -1, -1)
    place = jnp.stack([lax.axis_index("tx"), lax.axis_index("ty")]).astype(jnp.int32)
    warmed, scaled = call(
        functools.partial(heat_kernel, total_rows=points_y, total_cols=points_x),
        [
            jax.ShapeDtypeStruct((layers * count, width), F32),
            jax.ShapeDtypeStruct((tx, lines, width), F32),
        ],
        [VMEM] * 11 + [SMEM] * 6,
    )(
        heat, kind, moment, above, below, left, right, up_left, up_right, down_left, down_right,
        nodes, factor, threshold, spot_row, spot_col, place,
    )
    block = lax.all_to_all(scaled, "tx", split_axis=0, concat_axis=0, tiled=True)

    layer, layer_back = layer_tables(layers, strips, comps, order)
    along, along_back, sort = along_tables(points_x, tx)
    across, across_back = across_tables(points_y, tx, ty, strips)
    senders = tx * ty
    chunks = 1 if order == "whole" else members
    message = members // chunks * comps * 2 * strips
    spectra = call(
        rows_kernel,
        [jax.ShapeDtypeStruct((senders, message, width), F32)] * chunks,
        [VMEM] * 6,
    )(block, sort, *two_terms(along), *two_terms(layer))
    fields = []
    for chunk, data in enumerate(spectra):
        data = lax.all_to_all(data, ("tx", "ty"), split_axis=0, concat_axis=0, tiled=True)
        taps = tensor if chunks == 1 else tensor[:, chunk : chunk + 1]
        span = 2 * points_y // RADIX
        field = call(
            spectrum_kernel,
            jax.ShapeDtypeStruct(data.shape, F32),
            [VMEM] * 6,
            [
                pltpu.VMEM((RADIX, 2 * span, comps * width), F32),
                pltpu.VMEM((RADIX, 2 * span, comps * width), BF16),
                pltpu.VMEM((RADIX, 2 * span, comps * width), BF16),
            ],
        )(data, taps, *two_terms(across), *two_terms(across_back))
        fields.append(
            lax.all_to_all(field, ("tx", "ty"), split_axis=0, concat_axis=0, tiled=True)
        )
    scale = -1.0 / (2 * layers * 2 * points_y * 2 * points_x)
    cells = call(
        functools.partial(cells_kernel, scale=scale),
        jax.ShapeDtypeStruct((tx, lines, width), F32),
        [VMEM] * (chunks + 5),
    )(
        *fields, *two_terms(layer_back), *two_terms(along_back), np.ascontiguousarray(sort.T)
    )
    cells = lax.all_to_all(cells, "tx", split_axis=0, concat_axis=0, tiled=True)
    demag = call(
        place_kernel, jax.ShapeDtypeStruct((comps * layers * count, width), F32), [VMEM]
    )(cells)
    return (
        warmed.reshape(layers, count, width),
        demag.reshape(comps, layers, count, width),
    )


def solution(mesh):
    in_specs = (
        P(None, "ty", "tx"),
        P(None, "ty", "tx"),
        P(None, None, "ty", "tx"),
        P(None, "tx", None, "ty"),
        P(),
        P(),
        P(),
        P(),
        P(),
    )
    out_specs = (P(None, "ty", "tx"), P(None, None, "ty", "tx"))
    body = functools.partial(local, mesh.shape["tx"], mesh.shape["ty"], "whole")
    return jax.shard_map(body, mesh=mesh, in_specs=in_specs, out_specs=out_specs, check_vma=False)
```

```python
import functools
import math

import jax
import jax.numpy as jnp
import ml_dtypes
import numpy as np
from jax import lax
from jax.experimental import pallas as pl
from jax.experimental.pallas import tpu as pltpu
from jax.sharding import PartitionSpec as P

SWEEPS = 2
AMBIENT_HEAT = 0.3
STEP_RATE = 0.05
LASER_POWER = 4.0
LASER_DEPTH = 4.0
ORDERING_SPREAD = 0.08
TABLE_LOW = 0.2
TABLE_SPAN = 1.6
RADIX = 4
PAIRS = ((0, 3, 4), (3, 1, 5), (4, 5, 2))
VMEM = pl.BlockSpec(memory_space=pltpu.VMEM)
ANY = pl.BlockSpec(memory_space=pl.ANY)
F32 = jnp.float32
BF16 = jnp.bfloat16


def two_terms(table):
    table = np.asarray(table, np.float64)
    high = table.astype(np.float32).astype(ml_dtypes.bfloat16)
    low = (table - high.astype(np.float64)).astype(np.float32).astype(ml_dtypes.bfloat16)
    return (high, low)


def waves(products, length):
    angles = 2.0 * math.pi / length * (products % length)
    return (np.cos(angles), np.sin(angles))


def split(values):
    high = values.astype(BF16)
    low = (values - high.astype(F32)).astype(BF16)
    return (high, low)


def matmul(left, right):
    return lax.dot_general(left, right, (((1,), (0,)), ((), ())), preferred_element_type=F32)


def layer_tables(layers, strips, comps, order):
    count = 2 * layers
    owners = count // 2
    rows_in = comps * strips * layers
    if order == "whole":
        shape = (owners, 2, comps, 2, strips)
    else:
        shape = (2, owners, comps, 2, strips)
    index = np.indices(shape).reshape(5, -1)
    if order == "whole":
        owner, member, comp, part, strip = index
    else:
        member, owner, comp, part, strip = index
    freq = 2 * owner + member
    comp_in, strip_in, layer_in = np.indices((comps, strips, layers)).reshape(3, -1)
    same = (comp[:, None] == comp_in[None]) & (strip[:, None] == strip_in[None])
    cosine, sine = waves(freq[:, None] * layer_in[None], count)
    zero = part[:, None] == 0
    from_real = np.where(zero, cosine, -sine) * same
    from_imag = np.where(zero, sine, cosine) * same
    forward = np.concatenate([from_real, from_imag], 1)
    return forward, forward.T


def along_tables(points, devices):
    length = 2 * points
    span = length // RADIX
    sub = points // RADIX
    a = np.arange(sub)
    v = np.arange(span)
    forward = np.zeros((RADIX, sub, 2 * span))
    for b in range(RADIX):
        cosine, sine = waves(v[None, :] * (RADIX * a + b)[:, None], length)
        forward[b] = np.concatenate([cosine, -sine], 1)
    order = np.zeros((points, points), np.float32)
    for b in range(RADIX):
        order[RADIX * a + b, b * sub + a] = 1.0
    return forward, forward.transpose(0, 2, 1), order.astype(ml_dtypes.bfloat16)


def across_tables(points, groups, blocks, strips):
    length = 2 * points
    span = length // RADIX
    quarter, block, part, strip = np.indices((groups // RADIX, blocks, 2, strips)).reshape(4, -1)
    v = np.arange(span)
    forward = np.zeros((RADIX, 2 * span, quarter.size))
    for b in range(RADIX):
        y = groups * strips * block + groups * strip + RADIX * quarter + b
        cosine, sine = waves(v[:, None] * y[None, :], length)
        zero = part[None, :] == 0
        forward[b, :span] = np.where(zero, cosine, sine)
        forward[b, span:] = np.where(zero, -sine, cosine)
    return forward, forward.transpose(0, 2, 1)


def fetch(pairs, sems):
    copies = [
        pltpu.make_async_copy(source, target, sems.at[at])
        for at, (source, target) in enumerate(pairs)
    ]
    for copy in copies:
        copy.start()
    return copies


def chosen(which, values):
    total = jnp.zeros(which.shape, F32)
    for grain in range(values.shape[0]):
        total = total + jnp.where(which == grain, values[grain], 0.0)
    return total


def edges_kernel(
    heat_in, kind_in, factor_in, threshold_in, heat, gains, limits, sides, rows,
    kind, factor, threshold, sems
):
    copies = fetch(
        [(factor_in, factor), (threshold_in, threshold), (kind_in, kind), (heat_in, heat)], sems
    )
    for copy in copies:
        copy.wait()
    layers, count = 8, heat.shape[0] // 8
    lane = lax.broadcasted_iota(jnp.int32, (layers, 128), 1)
    packed = [jnp.zeros((layers, 128), F32), jnp.zeros((layers, 128), F32)]
    for y in range(count):
        at_rows = pl.ds(y, layers, stride=count)
        theta = heat[at_rows, :]
        which = kind[at_rows, :]
        gain = chosen(which, factor)
        gains[at_rows, :] = gain
        limits[at_rows, :] = chosen(which, threshold)
        for at, value in enumerate((theta, gain)):
            turned = pltpu.roll(value, (2 + 4 * y) % 128, 1)
            packed[at] = jnp.where(lane // 4 == y, turned, packed[at])
            if y < 2:
                rows[0, 2 * at + y] = value
            if y >= count - 2:
                rows[1, 2 * at + y - count + 2] = value
    sides[0] = packed[0]
    sides[1] = packed[1]


def join_kernel(rows, left, right, upward, downward):
    for at, out in enumerate((upward, downward)):
        out[0:4] = rows[at]
        out[4:6] = left[...]
        out[6:8] = right[...]


def heat_kernel(
    heat, gains_in, limits, moment_in, above, below, left, right, nodes_in, spot_row_in, spot_col_in,
    warmed, scaled, moment, nodes, spot_row, spot_col, sems, *, total_rows, total_cols
):
    copies = fetch(
        [(nodes_in, nodes), (spot_row_in, spot_row), (spot_col_in, spot_col), (moment_in, moment)],
        sems,
    )
    layers, count = 8, heat.shape[0] // 8
    width = 128
    col_base = lax.axis_index("tx") * width
    row_base = lax.axis_index("ty") * count
    for copy in copies[:3]:
        copy.wait()
    lane = lax.broadcasted_iota(jnp.int32, (layers, width), 1)
    first = lane == 0
    last = lane == width - 1
    low = lane < width // 2
    depth = lax.broadcasted_iota(jnp.int32, (layers, width), 0)
    spacing = TABLE_SPAN / (nodes.shape[0] - 1)
    slopes = [(nodes[j + 1] - nodes[j]) * (1.0 / spacing) for j in range(nodes.shape[0] - 1)]

    def conductivity(theta, gain):
        absolute = theta + AMBIENT_HEAT
        total = jnp.zeros_like(theta) + nodes[0]
        for j, slope in enumerate(slopes):
            total = total + slope * jnp.clip(absolute - (TABLE_LOW + j * spacing), 0.0, spacing)
        return gain * total

    inside_top = jnp.where(row_base > 0, 1.0, 0.0)
    inside_bottom = jnp.where(row_base + count < total_rows, 1.0, 0.0)
    start = AMBIENT_HEAT
    main = {}
    gains = {}
    for y in range(count):
        gains[y] = gains_in[pl.ds(y, layers, stride=count), :]
        main[y] = heat[pl.ds(y, layers, stride=count), :] - start
    for j in range(2):
        main[j - 2] = (above[j] - start) * inside_top
        gains[j - 2] = above[2 + j] * inside_top
        main[count + j] = (below[j] - start) * inside_bottom
        gains[count + j] = below[2 + j] * inside_bottom

    def side(at, y, to_left, to_right, skip=(0, 0)):
        turn = (128 - (2 + 4 * y)) % 128
        return jnp.where(
            low,
            pltpu.roll(to_right[skip[1] + at], turn, 1),
            pltpu.roll(to_left[skip[0] + at], turn, 1),
        )

    flank = {}
    flank_gain = {}
    for y in range(count):
        flank[y] = side(0, y, left, right) - start
        flank_gain[y] = side(1, y, left, right)
    flank[-1] = (side(0, count - 1, above, above, (4, 6)) - start) * inside_top
    flank_gain[-1] = side(1, count - 1, above, above, (4, 6)) * inside_top
    flank[count] = (side(0, 0, below, below, (4, 6)) - start) * inside_bottom
    flank_gain[count] = side(1, 0, below, below, (4, 6)) * inside_bottom

    def heating(y, sweep, along):
        across = (row_base + y - spot_row[sweep]).astype(F32) * (1.0 / 32.0)
        across = jnp.full((layers, width), -0.5, F32) * (across * across)
        return along * jnp.exp(across)

    def along_of(columns, sweep):
        shifted = columns - spot_col[sweep] + total_cols // 2
        shifted = jnp.where(shifted < 0, shifted + total_cols, shifted)
        shifted = jnp.where(shifted >= total_cols, shifted - total_cols, shifted)
        offset = (shifted - total_cols // 2).astype(F32) * (1.0 / (0.5 * width))
        return jnp.exp(depth.astype(F32) * (-1.0 / LASER_DEPTH)) * jnp.exp(-0.5 * offset * offset)

    main_columns = col_base + lane
    flank_columns = jnp.where(low, lane + width, lane - width) + col_base
    flank_columns = jnp.where(flank_columns < 0, flank_columns + total_cols, flank_columns)
    flank_columns = jnp.where(
        flank_columns >= total_cols, flank_columns - total_cols, flank_columns
    )
    not_top = depth > 0
    not_bottom = depth < layers - 1

    def before(value, other):
        return jnp.where(first, pltpu.roll(other, 1, 1), pltpu.roll(value, 1, 1))

    def after(value, other):
        return jnp.where(last, pltpu.roll(other, width - 1, 1), pltpu.roll(value, width - 1, 1))

    def step(theta, k, sides, up, down, source):
        flux = jnp.zeros_like(theta)
        for other, other_k in sides + (up, down):
            flux = flux + (k + other_k) * (other - theta)
        below_flux = (k + pltpu.roll(k, layers - 1, 0)) * (pltpu.roll(theta, layers - 1, 0) - theta)
        above_flux = (k + pltpu.roll(k, 1, 0)) * (pltpu.roll(theta, 1, 0) - theta)
        flux = flux + jnp.where(not_bottom, below_flux, 0.0) + jnp.where(not_top, above_flux, 0.0)
        return theta + STEP_RATE * (0.5 * flux + LASER_POWER * source)

    def flanked(value, other):
        return before(value, other), after(value, other)

    for sweep in range(SWEEPS):
        reach = SWEEPS - 1 - sweep
        k_main = {y: conductivity(main[y], gains[y]) for y in range(-1 - reach, count + 1 + reach)}
        k_flank = {
            y: conductivity(flank[y], flank_gain[y]) for y in range(-reach, count + reach)
        }
        along_main = along_of(main_columns, sweep)
        along_flank = along_of(flank_columns, sweep)
        fresh = {}
        fresh_flank = {}
        for y in range(-reach, count + reach):
            lt, rt = flanked(main[y], flank[y])
            lk, rk = flanked(k_main[y], k_flank[y])
            value = step(
                main[y], k_main[y], ((lt, lk), (rt, rk)),
                (main[y - 1], k_main[y - 1]), (main[y + 1], k_main[y + 1]),
                heating(y, sweep, along_main),
            )
            if y < 0:
                value = value * inside_top
            if y >= count:
                value = value * inside_bottom
            fresh[y] = value
            if reach and 0 <= y < count:
                lt, rt = flanked(flank[y], main[y])
                lk, rk = flanked(k_flank[y], k_main[y])
                fresh_flank[y] = step(
                    flank[y], k_flank[y], ((lt, lk), (rt, rk)),
                    (flank[y - 1], k_flank[y - 1]), (flank[y + 1], k_flank[y + 1]),
                    heating(y, sweep, along_flank),
                )
        main, flank = fresh, fresh_flank

    groups = scaled.shape[0]
    copies[3].wait()
    for y in range(count):
        value = main[y] + AMBIENT_HEAT
        warmed[pl.ds(y, layers, stride=count), :] = value
        limit = limits[pl.ds(y, layers, stride=count), :]
        fraction = 1.0 / (1.0 + jnp.exp((value - limit) * (1.0 / ORDERING_SPREAD)))
        strip, group = divmod(y, groups)
        for comp in range(3):
            source = moment[pl.ds(comp * layers * count + y, layers, stride=count), :]
            at = (comp * (count // groups) + strip) * layers
            scaled[group, at : at + layers, :] = source * fraction


def turns(t, sign):
    (ar, ai), (br, bi), (cr, ci), (dr, di) = t
    er, ei, fr, fi = ar + cr, ai + ci, ar - cr, ai - ci
    gr, gi, hr, hi = br + dr, bi + di, br - dr, bi - di
    minus = (fr + hi, fi - hr)
    plus = (fr - hi, fi + hr)
    one, three = (minus, plus) if sign < 0 else (plus, minus)
    return ((er + gr, ei + gi), one, (er - gr, ei - gi), three)


def matmul_terms(left, right):
    left_high, left_low = left
    right_high, right_low = right
    return matmul(
        jnp.concatenate([left_high, left_high, left_low], 1),
        jnp.concatenate([right_high, right_low, right_high], 0),
    )


def rows_kernel(block, order_in, high_in, low_in, layer_in, out, order, high, low, layer, sems):
    copies = fetch(
        [(order_in, order)]
        + [pair for b in range(RADIX) for pair in ((high_in.at[b], high.at[b]), (low_in.at[b], low.at[b]))]
        + [(layer_in, layer)],
        sems,
    )
    groups, lines, width = block.shape
    points = groups * width
    sub = points // RADIX
    span = high.shape[2] // 2
    values = jnp.concatenate([block[t] for t in range(groups)], 1)
    both = jnp.concatenate(split(values), 0)
    copies[0].wait()
    both = matmul(both, order[...]).astype(BF16)
    parts = []
    for b in range(RADIX):
        data = both[:, b * sub : (b + 1) * sub]
        copies[1 + 2 * b].wait()
        copies[2 + 2 * b].wait()
        total = matmul_terms((data[:lines], data[lines:]), (high[b], low[b]))
        parts.append((total[:, :span], total[:, span:]))
    copies[-1].wait()
    slabs = span // width
    blocks = RADIX * slabs
    for u, (real, imag) in enumerate(turns(parts, -1)):
        data_high, data_low = split(jnp.concatenate([real, imag], 0))
        total = matmul(layer[...], jnp.concatenate([data_high, data_low, data_high], 0))
        rows = total.shape[0] // groups
        for t in range(groups):
            for slab in range(slabs):
                out[t * blocks + u * slabs + slab] = total[
                    t * rows : (t + 1) * rows, slab * width : (slab + 1) * width
                ]


def spectrum_kernel(
    data, tensor_in, high_in, low_in, back_high_in, back_low_in, out,
    tensor, high, low, back_high, back_low, sums, fields_high, fields_low, sems
):
    comps = 3
    senders, lines, width = data.shape
    blocks = 16
    quarters = senders // blocks // RADIX
    units = lines // 8
    members = units // comps
    span = high.shape[1] // 2
    pairs = []
    for b in range(RADIX):
        pairs += [(high_in.at[b], high.at[b]), (low_in.at[b], low.at[b])]
    pairs += [(tensor_in, tensor)]
    for b in range(RADIX):
        pairs += [(back_high_in.at[b], back_high.at[b]), (back_low_in.at[b], back_low.at[b])]
    copies = fetch(pairs, sems)
    for b in range(RADIX):
        pieces = []
        for unit in range(units):
            tall = [
                data[(b + RADIX * q) * blocks : (b + RADIX * q + 1) * blocks, unit * 8 : unit * 8 + 8, :]
                for q in range(quarters)
            ]
            pieces.append(jnp.concatenate(tall, 0).reshape(quarters * blocks * 8, width))
        copies[2 * b].wait()
        copies[2 * b + 1].wait()
        sums[b] = matmul_terms((high[b], low[b]), split(jnp.concatenate(pieces, 1)))
    copies[2 * RADIX].wait()
    piece = 16

    def multiply(step, carry):
        at = pl.multiple_of(step * piece, piece)
        for member in range(members):
            spectra = []
            for comp in range(comps):
                lanes = pl.ds((member * comps + comp) * width, width)
                t = [
                    (sums[b, pl.ds(at, piece), lanes], sums[b, pl.ds(span + at, piece), lanes])
                    for b in range(RADIX)
                ]
                spectra.append(turns(t, -1))
            field = [[None] * RADIX for _ in range(comps)]
            for u in range(RADIX):
                taps = [tensor[p, member, pl.ds(u * span + at, piece), :] for p in range(6)]
                for target in range(comps):
                    field[target][u] = tuple(
                        taps[PAIRS[target][0]] * spectra[0][u][part]
                        + taps[PAIRS[target][1]] * spectra[1][u][part]
                        + taps[PAIRS[target][2]] * spectra[2][u][part]
                        for part in range(2)
                    )
            for comp in range(comps):
                lanes = pl.ds((member * comps + comp) * width, width)
                for b, both in enumerate(turns(field[comp], 1)):
                    for part, value in enumerate(both):
                        data_high, data_low = split(value)
                        rows = pl.ds(part * span + at, piece)
                        fields_high[b, rows, lanes] = data_high
                        fields_low[b, rows, lanes] = data_low
        return carry

    lax.fori_loop(0, span // piece, multiply, 0)
    for b in range(RADIX):
        copies[2 * RADIX + 1 + 2 * b].wait()
        copies[2 * RADIX + 2 + 2 * b].wait()
        total = matmul_terms((back_high[b], back_low[b]), (fields_high[b], fields_low[b]))
        for q in range(quarters):
            group = b + RADIX * q
            tall = total[q * blocks * 8 : (q + 1) * blocks * 8]
            for unit in range(units):
                out[group * blocks : (group + 1) * blocks, unit * 8 : unit * 8 + 8, :] = tall[
                    :, unit * width : (unit + 1) * width
                ].reshape(blocks, 8, width)


def cells_kernel(data, layer_in, high_in, low_in, order_in, out, layer, high, low, order, sems, *, scale):
    copies = fetch(
        [(layer_in, layer)]
        + [pair for b in range(RADIX) for pair in ((high_in.at[b], high.at[b]), (low_in.at[b], low.at[b]))]
        + [(order_in, order)],
        sems,
    )
    groups, lines, width = out.shape
    span = high.shape[1] // 2
    slabs = span // width
    blocks = RADIX * slabs
    pieces = []
    copies[0].wait()
    for u in range(RADIX):
        columns = []
        for slab in range(slabs):
            at = u * slabs + slab
            columns.append(jnp.concatenate([data[t * blocks + at] for t in range(groups)], 0))
        data_high, data_low = split(jnp.concatenate(columns, 1))
        total = matmul(layer[...], jnp.concatenate([data_high, data_low, data_high], 0))
        pieces.append((total[:lines], total[lines:]))
    sorted_columns = []
    for b, both in enumerate(turns(pieces, 1)):
        copies[1 + 2 * b].wait()
        copies[2 + 2 * b].wait()
        sorted_columns.append(matmul_terms(split(jnp.concatenate(both, 1)), (high[b], low[b])))
    values = jnp.concatenate(sorted_columns, 1) * scale
    data_high, data_mid = split(values)
    data_low = (values - data_high.astype(F32) - data_mid.astype(F32)).astype(BF16)
    copies[-1].wait()
    total = matmul(jnp.concatenate([data_high, data_mid, data_low], 0), order[...])
    values = total[:lines] + total[lines : 2 * lines] + total[2 * lines :]
    for t in range(groups):
        out[t] = values[:, t * width : (t + 1) * width]


def place_kernel(block, out):
    groups, lines, width = block.shape
    layers = 8
    count = out.shape[0] // (3 * layers)
    strips = count // groups
    for comp in range(3):
        for y in range(count):
            strip, group = divmod(y, groups)
            at = (comp * strips + strip) * layers
            out[pl.ds(comp * layers * count + y, layers, stride=count), :] = block[
                group, at : at + layers, :
            ]


def near(shape, dtype):
    return pltpu.VMEM(shape, dtype)


def call(kernel, out_shape, in_specs, scratch=(), megabytes=16, flops=0, bytes_accessed=0):
    many = isinstance(out_shape, (list, tuple))
    return pl.pallas_call(
        kernel,
        out_shape=out_shape,
        in_specs=in_specs,
        out_specs=[VMEM] * len(out_shape) if many else VMEM,
        scratch_shapes=list(scratch),
        compiler_params=pltpu.CompilerParams(vmem_limit_bytes=megabytes * 1024 * 1024),
        cost_estimate=pl.CostEstimate(
            flops=flops, bytes_accessed=bytes_accessed, transcendentals=0
        ),
    )


def far(value):
    return pltpu.with_memory_space_constraint(value, pltpu.HBM)


def with_tables(kernel, out_shape, operand, tables, scratch=(), copies=0, megabytes=32):
    tables = [jnp.asarray(a) for a in tables]
    return call(
        kernel,
        out_shape,
        [VMEM] + [ANY] * len(tables),
        [pltpu.VMEM(a.shape, a.dtype) for a in tables]
        + list(scratch)
        + [pltpu.SemaphoreType.DMA((copies,))],
        megabytes=megabytes,
    )(operand, *[far(a) for a in tables])


def local(
    tx, ty, order, heat, kind, moment, tensor, nodes, factor, threshold, spot_row, spot_col
):
    layers, count, width = heat.shape
    strips = count // tx
    comps = 3
    lines = comps * strips * layers
    points_x, points_y = tx * width, ty * count
    members = 2
    cells = layers * count

    heat = heat.reshape(cells, width)
    kind = kind.reshape(cells, width)
    moment = moment.reshape(comps * cells, width)
    heat, gains, limits, sides, rows = call(
        edges_kernel,
        [near((cells, width), F32)] * 3
        + [near((2, layers, width), F32), near((2, 4, layers, width), F32)],
        [ANY] * 4,
        [
            pltpu.VMEM((cells, width), jnp.int32),
            pltpu.SMEM(factor.shape, F32),
            pltpu.SMEM(threshold.shape, F32),
            pltpu.SemaphoreType.DMA((4,)),
        ],
    )(far(heat), far(kind), far(factor), far(threshold))

    def moved(value, axis, step, wrap):
        size = tx if axis == "tx" else ty
        pairs = [(i, (i + step) % size) for i in range(size) if wrap or 0 <= i + step < size]
        return lax.ppermute(value, axis, pairs)

    left = moved(sides, "tx", 1, True)
    right = moved(sides, "tx", -1, True)
    upward, downward = call(join_kernel, [near((8, layers, width), F32)] * 2, [VMEM] * 3)(
        rows, left, right
    )
    above = moved(downward, "ty", 1, False)
    below = moved(upward, "ty", -1, False)
    warmed, scaled = call(
        functools.partial(heat_kernel, total_rows=points_y, total_cols=points_x),
        [
            jax.ShapeDtypeStruct((cells, width), F32),
            near((tx, lines, width), F32),
        ],
        [VMEM] * 3 + [ANY] + [VMEM] * 4 + [ANY] * 3,
        [
            pltpu.VMEM((comps * cells, width), F32),
            pltpu.SMEM(nodes.shape, F32),
            pltpu.SMEM(spot_row.shape, jnp.int32),
            pltpu.SMEM(spot_col.shape, jnp.int32),
            pltpu.SemaphoreType.DMA((4,)),
        ],
    )(
        heat, gains, limits, far(moment), above, below, left, right,
        far(nodes), far(spot_row), far(spot_col),
    )

    layer, layer_back = layer_tables(layers, strips, comps, order)
    along, along_back, sort = along_tables(points_x, tx)
    across, across_back = across_tables(points_y, tx, ty, strips)
    senders = tx * ty
    message = members * comps * 2 * strips
    span = 2 * points_y // RADIX

    def tripled(table):
        high, low = two_terms(table)
        return np.concatenate([high, high, low], 1)

    block = lax.all_to_all(scaled, "tx", split_axis=0, concat_axis=0, tiled=True)
    spectra = with_tables(
        rows_kernel,
        jax.ShapeDtypeStruct((senders, message, width), F32),
        block,
        [sort, *two_terms(along), tripled(layer)],
        copies=2 + 2 * RADIX,
    )
    data = lax.all_to_all(spectra, ("tx", "ty"), split_axis=0, concat_axis=0, tiled=True)
    columns = members * comps * width
    field = with_tables(
        spectrum_kernel,
        jax.ShapeDtypeStruct(data.shape, F32),
        data,
        [tensor, *two_terms(across), *two_terms(across_back)],
        [
            pltpu.VMEM((RADIX, 2 * span, columns), F32),
            pltpu.VMEM((RADIX, 2 * span, columns), BF16),
            pltpu.VMEM((RADIX, 2 * span, columns), BF16),
        ],
        copies=1 + 4 * RADIX,
        megabytes=44,
    )
    data = lax.all_to_all(field, ("tx", "ty"), split_axis=0, concat_axis=0, tiled=True)
    scale = -1.0 / (2 * layers * 2 * points_y * 2 * points_x)
    block = with_tables(
        functools.partial(cells_kernel, scale=scale),
        near((tx, lines, width), F32),
        data,
        [tripled(layer_back), *two_terms(along_back), np.ascontiguousarray(sort.T)],
        copies=2 + 2 * RADIX,
    )
    block = lax.all_to_all(block, "tx", split_axis=0, concat_axis=0, tiled=True)
    demag = call(place_kernel, jax.ShapeDtypeStruct((comps * cells, width), F32), [VMEM])(block)
    return (
        warmed.reshape(layers, count, width),
        demag.reshape(comps, layers, count, width),
    )


def solution(mesh):
    in_specs = (
        P(None, "ty", "tx"),
        P(None, "ty", "tx"),
        P(None, None, "ty", "tx"),
        P(None, "tx", None, "ty"),
        P(),
        P(),
        P(),
        P(),
        P(),
    )
    out_specs = (P(None, "ty", "tx"), P(None, None, "ty", "tx"))
    body = functools.partial(local, mesh.shape["tx"], mesh.shape["ty"], "whole")
    return jax.shard_map(body, mesh=mesh, in_specs=in_specs, out_specs=out_specs, check_vma=False)
```

```python
import functools
import math

import jax
import jax.numpy as jnp
import ml_dtypes
import numpy as np
from jax import lax
from jax.experimental import pallas as pl
from jax.experimental.pallas import tpu as pltpu
from jax.sharding import PartitionSpec as P

SWEEPS = 2
AMBIENT_HEAT = 0.3
STEP_RATE = 0.05
LASER_POWER = 4.0
LASER_DEPTH = 4.0
ORDERING_SPREAD = 0.08
TABLE_LOW = 0.2
TABLE_SPAN = 1.6
RADIX = 4
REACH = SWEEPS
PAIRS = ((0, 3, 4), (3, 1, 5), (4, 5, 2))
VMEM = pl.BlockSpec(memory_space=pltpu.VMEM)
ANY = pl.BlockSpec(memory_space=pl.ANY)
F32 = jnp.float32
BF16 = jnp.bfloat16


def two_terms(table):
    table = np.asarray(table, np.float64)
    high = table.astype(np.float32).astype(ml_dtypes.bfloat16)
    low = (table - high.astype(np.float64)).astype(np.float32).astype(ml_dtypes.bfloat16)
    return (high, low)


def waves(products, length):
    angles = 2.0 * math.pi / length * (products % length)
    return (np.cos(angles), np.sin(angles))


def split(values):
    high = values.astype(BF16)
    low = (values - high.astype(F32)).astype(BF16)
    return (high, low)


def matmul(left, right):
    return lax.dot_general(left, right, (((1,), (0,)), ((), ())), preferred_element_type=F32)


def layer_tables(layers, strips, comps, order):
    count = 2 * layers
    owners = count // 2
    rows_in = comps * strips * layers
    if order == "whole":
        shape = (owners, 2, comps, 2, strips)
    else:
        shape = (2, owners, comps, 2, strips)
    index = np.indices(shape).reshape(5, -1)
    if order == "whole":
        owner, member, comp, part, strip = index
    else:
        member, owner, comp, part, strip = index
    freq = 2 * owner + member
    comp_in, strip_in, layer_in = np.indices((comps, strips, layers)).reshape(3, -1)
    same = (comp[:, None] == comp_in[None]) & (strip[:, None] == strip_in[None])
    cosine, sine = waves(freq[:, None] * layer_in[None], count)
    zero = part[:, None] == 0
    from_real = np.where(zero, cosine, -sine) * same
    from_imag = np.where(zero, sine, cosine) * same
    forward = np.concatenate([from_real, from_imag], 1)
    return forward, forward.T


def along_tables(points, devices):
    length = 2 * points
    span = length // RADIX
    sub = points // RADIX
    a = np.arange(sub)
    v = np.arange(span)
    forward = np.zeros((RADIX, sub, 2 * span))
    for b in range(RADIX):
        cosine, sine = waves(v[None, :] * (RADIX * a + b)[:, None], length)
        forward[b] = np.concatenate([cosine, -sine], 1)
    order = np.zeros((points, points), np.float32)
    for b in range(RADIX):
        order[RADIX * a + b, b * sub + a] = 1.0
    return forward, forward.transpose(0, 2, 1), order.astype(ml_dtypes.bfloat16)


def across_tables(points, groups, blocks, strips):
    length = 2 * points
    span = length // RADIX
    part, group, block = np.indices((2, groups, blocks)).reshape(3, -1)
    v = np.arange(span)
    forward = np.zeros((RADIX, 2 * span, part.size))
    for b in range(RADIX):
        y = strips * (groups * block + group) + b
        cosine, sine = waves(v[:, None] * y[None, :], length)
        zero = part[None, :] == 0
        forward[b, :span] = np.where(zero, cosine, sine)
        forward[b, span:] = np.where(zero, -sine, cosine)
    return forward, forward.transpose(0, 2, 1)


def fetch(pairs, sems):
    copies = [
        pltpu.make_async_copy(source, target, sems.at[at])
        for at, (source, target) in enumerate(pairs)
    ]
    for copy in copies:
        copy.start()
    return copies


def chosen(which, values):
    total = jnp.zeros(which.shape, F32)
    for grain in range(values.shape[0]):
        total = total + jnp.where(which == grain, values[grain], 0.0)
    return total


def edges_kernel(heat_in, kind_in, moment_in, heat, kind, moment, rows, sems):
    copies = fetch([(heat_in, heat), (kind_in, kind), (moment_in, moment)], sems)
    layers, count = 8, heat.shape[0] // 8
    copies[0].wait()
    copies[1].wait()
    for side, first in enumerate((0, count - REACH)):
        for j in range(REACH):
            at = pl.ds(first + j, layers, stride=count)
            rows[side, j] = heat[at, :]
            rows[side, REACH + j] = kind[at, :].astype(F32)
    copies[2].wait()


def send_kernel(heat, kind, moment, above, below, out):
    layers, count = 8, heat.shape[0] // 8
    groups = out.shape[0]
    strips = count // groups
    tall = strips + 2 * REACH
    for group in range(groups):
        for i in range(tall):
            y = group * strips - REACH + i
            if y < 0:
                pair = (above[y + REACH], above[y + 2 * REACH])
            elif y >= count:
                pair = (below[y - count], below[y - count + REACH])
            else:
                at = pl.ds(y, layers, stride=count)
                pair = (heat[at, :], kind[at, :].astype(F32))
            for which, value in enumerate(pair):
                out[group, (which * tall + i) * layers : (which * tall + i + 1) * layers, :] = value
        for comp in range(3):
            for strip in range(strips):
                at = pl.ds(comp * layers * count + group * strips + strip, layers, stride=count)
                to = (2 * tall + comp * strips + strip) * layers
                out[group, to : to + layers, :] = moment[at, :]


def heat_rows(block, nodes, factor, threshold, spot_row, spot_col, total_rows):
    layers = 8
    groups, lines, width = block.shape
    total_cols = groups * width
    strips = (lines // layers - 4 * REACH) // 5
    tall = strips + 2 * REACH
    row_base = (lax.axis_index("ty") * groups + lax.axis_index("tx")) * strips - REACH
    shape = (layers, total_cols)
    column = lax.broadcasted_iota(jnp.int32, shape, 1)
    depth = lax.broadcasted_iota(jnp.int32, shape, 0)
    spacing = TABLE_SPAN / (nodes.shape[0] - 1)
    slopes = [(nodes[j + 1] - nodes[j]) * (1.0 / spacing) for j in range(nodes.shape[0] - 1)]

    def whole(index):
        at = index * layers
        return jnp.concatenate([block[t, at : at + layers, :] for t in range(groups)], 1)

    def chosen(which, values):
        total = jnp.zeros(which.shape, F32)
        for grain in range(values.shape[0]):
            total = total + jnp.where(which == float(grain), values[grain], 0.0)
        return total

    def conductivity(theta, gain):
        absolute = theta + AMBIENT_HEAT
        total = jnp.zeros_like(theta) + nodes[0]
        for j, slope in enumerate(slopes):
            total = total + slope * jnp.clip(absolute - (TABLE_LOW + j * spacing), 0.0, spacing)
        return gain * total

    inside = {}
    thetas = {}
    gains = {}
    for i in range(tall):
        y = row_base + i
        inside[i] = jnp.where((y >= 0) & (y < total_rows), 1.0, 0.0)
        thetas[i] = (whole(i) - AMBIENT_HEAT) * inside[i]
        gains[i] = chosen(whole(tall + i), factor) * inside[i]
    not_top = depth > 0
    not_bottom = depth < layers - 1
    for sweep in range(SWEEPS):
        shifted = column - spot_col[sweep] + total_cols // 2
        shifted = jnp.where(shifted < 0, shifted + total_cols, shifted)
        shifted = jnp.where(shifted >= total_cols, shifted - total_cols, shifted)
        offset = (shifted - total_cols // 2).astype(F32) * (1.0 / (0.5 * width))
        along = jnp.exp(depth.astype(F32) * (-1.0 / LASER_DEPTH)) * jnp.exp(-0.5 * offset * offset)
        k = {i: conductivity(thetas[i], gains[i]) for i in range(sweep, tall - sweep)}
        fresh = {}
        for i in range(sweep + 1, tall - sweep - 1):
            theta, own = thetas[i], k[i]
            flux = (own + k[i - 1]) * (thetas[i - 1] - theta)
            flux = flux + (own + k[i + 1]) * (thetas[i + 1] - theta)
            for turn in (1, total_cols - 1):
                flux = flux + (own + pltpu.roll(own, turn, 1)) * (pltpu.roll(theta, turn, 1) - theta)
            for turn, valid in ((1, not_top), (layers - 1, not_bottom)):
                part = (own + pltpu.roll(own, turn, 0)) * (pltpu.roll(theta, turn, 0) - theta)
                flux = flux + jnp.where(valid, part, 0.0)
            across = (row_base + i - spot_row[sweep]).astype(F32) * (1.0 / 32.0)
            across = jnp.exp(jnp.full((layers, width), -0.5, F32) * (across * across))
            source = along * jnp.concatenate([across] * groups, 1)
            value = theta + STEP_RATE * (0.5 * flux + LASER_POWER * source)
            fresh[i] = value * inside[i]
        thetas = fresh
    warmed = []
    fractions = []
    for strip in range(strips):
        value = thetas[REACH + strip] + AMBIENT_HEAT
        limit = chosen(whole(tall + REACH + strip), threshold)
        warmed.append(value)
        fractions.append(1.0 / (1.0 + jnp.exp((value - limit) * (1.0 / ORDERING_SPREAD))))
    scaled = []
    for comp in range(3):
        for strip in range(strips):
            scaled.append(whole(2 * tall + comp * strips + strip) * fractions[strip])
    return warmed, jnp.concatenate(scaled, 0)


def turns(t, sign):
    (ar, ai), (br, bi), (cr, ci), (dr, di) = t
    er, ei, fr, fi = ar + cr, ai + ci, ar - cr, ai - ci
    gr, gi, hr, hi = br + dr, bi + di, br - dr, bi - di
    minus = (fr + hi, fi - hr)
    plus = (fr - hi, fi + hr)
    one, three = (minus, plus) if sign < 0 else (plus, minus)
    return ((er + gr, ei + gi), one, (er - gr, ei - gi), three)


def matmul_terms(left, right):
    left_high, left_low = left
    right_high, right_low = right
    return matmul(
        jnp.concatenate([left_high, left_high, left_low], 1),
        jnp.concatenate([right_high, right_low, right_high], 0),
    )


def rows_kernel(
    block, order_in, high_in, low_in, layer_in, nodes_in, factor_in, threshold_in, spot_row_in, spot_col_in,
    out, warmed, order, high, low, layer, nodes, factor, threshold, spot_row, spot_col, sems, *, total_rows
):
    copies = fetch(
        [
            (nodes_in, nodes), (factor_in, factor), (threshold_in, threshold),
            (spot_row_in, spot_row), (spot_col_in, spot_col), (order_in, order),
        ]
        + [pair for b in range(RADIX) for pair in ((high_in.at[b], high.at[b]), (low_in.at[b], low.at[b]))]
        + [(layer_in, layer)],
        sems,
    )
    for copy in copies[:5]:
        copy.wait()
    copies = copies[5:]
    groups, _, width = block.shape
    points = groups * width
    sub = points // RADIX
    span = high.shape[2] // 2
    kept, values = heat_rows(block, nodes, factor, threshold, spot_row, spot_col, total_rows)
    lines = values.shape[0]
    for strip, value in enumerate(kept):
        for t in range(groups):
            warmed[t, strip * 8 : strip * 8 + 8, :] = value[:, t * width : (t + 1) * width]
    both = jnp.concatenate(split(values), 0)
    copies[0].wait()
    both = matmul(both, order[...]).astype(BF16)
    parts = []
    for b in range(RADIX):
        data = both[:, b * sub : (b + 1) * sub]
        copies[1 + 2 * b].wait()
        copies[2 + 2 * b].wait()
        total = matmul_terms((data[:lines], data[lines:]), (high[b], low[b]))
        parts.append((total[:, :span], total[:, span:]))
    copies[-1].wait()
    slabs = span // width
    blocks = RADIX * slabs
    for u, (real, imag) in enumerate(turns(parts, -1)):
        data_high, data_low = split(jnp.concatenate([real, imag], 0))
        total = matmul(layer[...], jnp.concatenate([data_high, data_low, data_high], 0))
        rows = total.shape[0] // groups
        for t in range(groups):
            for slab in range(slabs):
                out[t * blocks + u * slabs + slab] = total[
                    t * rows : (t + 1) * rows, slab * width : (slab + 1) * width
                ]


def spectrum_kernel(
    data, tensor_in, high_in, low_in, back_high_in, back_low_in, out,
    tensor, high, low, back_high, back_low, sums, fields_high, fields_low, sems
):
    comps = 3
    width = data.shape[1]
    senders = high.shape[2] // 2
    lines = data.shape[0] // senders
    units = lines // 8
    members = units // comps
    span = high.shape[1] // 2
    pairs = []
    for b in range(RADIX):
        pairs += [(high_in.at[b], high.at[b]), (low_in.at[b], low.at[b])]
    pairs += [(tensor_in, tensor)]
    for b in range(RADIX):
        pairs += [(back_high_in.at[b], back_high.at[b]), (back_low_in.at[b], back_low.at[b])]
    copies = fetch(pairs, sems)
    for b in range(RADIX):
        pieces = []
        for unit in range(units):
            both = [
                data[pl.ds(unit * 8 + part * RADIX + b, senders, stride=lines), :]
                for part in range(2)
            ]
            pieces.append(jnp.concatenate(both, 0))
        copies[2 * b].wait()
        copies[2 * b + 1].wait()
        sums[b] = matmul_terms((high[b], low[b]), split(jnp.concatenate(pieces, 1)))
    copies[2 * RADIX].wait()
    piece = 16

    def multiply(step, carry):
        at = pl.multiple_of(step * piece, piece)
        for member in range(members):
            spectra = []
            for comp in range(comps):
                lanes = pl.ds((member * comps + comp) * width, width)
                t = [
                    (sums[b, pl.ds(at, piece), lanes], sums[b, pl.ds(span + at, piece), lanes])
                    for b in range(RADIX)
                ]
                spectra.append(turns(t, -1))
            field = [[None] * RADIX for _ in range(comps)]
            for u in range(RADIX):
                taps = [tensor[p, member, pl.ds(u * span + at, piece), :] for p in range(6)]
                for target in range(comps):
                    field[target][u] = tuple(
                        taps[PAIRS[target][0]] * spectra[0][u][part]
                        + taps[PAIRS[target][1]] * spectra[1][u][part]
                        + taps[PAIRS[target][2]] * spectra[2][u][part]
                        for part in range(2)
                    )
            for comp in range(comps):
                lanes = pl.ds((member * comps + comp) * width, width)
                for b, both in enumerate(turns(field[comp], 1)):
                    for part, value in enumerate(both):
                        data_high, data_low = split(value)
                        rows = pl.ds(part * span + at, piece)
                        fields_high[b, rows, lanes] = data_high
                        fields_low[b, rows, lanes] = data_low
        return carry

    lax.fori_loop(0, span // piece, multiply, 0)
    for b in range(RADIX):
        copies[2 * RADIX + 1 + 2 * b].wait()
        copies[2 * RADIX + 2 + 2 * b].wait()
        total = matmul_terms((back_high[b], back_low[b]), (fields_high[b], fields_low[b]))
        for unit in range(units):
            for part in range(2):
                out[pl.ds(unit * 8 + part * RADIX + b, senders, stride=lines), :] = total[
                    part * senders : (part + 1) * senders, unit * width : (unit + 1) * width
                ]


def cells_kernel(data, kept, layer_in, high_in, low_in, order_in, out, layer, high, low, order, sems, *, scale):
    copies = fetch(
        [(layer_in, layer)]
        + [pair for b in range(RADIX) for pair in ((high_in.at[b], high.at[b]), (low_in.at[b], low.at[b]))]
        + [(order_in, order)],
        sems,
    )
    groups, _, width = out.shape
    lines = layer.shape[0] // 2
    span = high.shape[1] // 2
    slabs = span // width
    blocks = RADIX * slabs
    pieces = []
    copies[0].wait()
    for u in range(RADIX):
        columns = []
        for slab in range(slabs):
            at = u * slabs + slab
            columns.append(jnp.concatenate([data[t * blocks + at] for t in range(groups)], 0))
        data_high, data_low = split(jnp.concatenate(columns, 1))
        total = matmul(layer[...], jnp.concatenate([data_high, data_low, data_high], 0))
        pieces.append((total[:lines], total[lines:]))
    sorted_columns = []
    for b, both in enumerate(turns(pieces, 1)):
        copies[1 + 2 * b].wait()
        copies[2 + 2 * b].wait()
        sorted_columns.append(matmul_terms(split(jnp.concatenate(both, 1)), (high[b], low[b])))
    values = jnp.concatenate(sorted_columns, 1) * scale
    data_high, data_mid = split(values)
    data_low = (values - data_high.astype(F32) - data_mid.astype(F32)).astype(BF16)
    copies[-1].wait()
    total = matmul(jnp.concatenate([data_high, data_mid, data_low], 0), order[...])
    values = total[:lines] + total[lines : 2 * lines] + total[2 * lines :]
    for t in range(groups):
        out[t, :lines] = values[:, t * width : (t + 1) * width]
        out[t, lines:] = kept[t]


def place_kernel(block, field, warmed):
    groups, lines, width = block.shape
    layers = 8
    count = warmed.shape[0] // layers
    strips = count // groups
    for y in range(count):
        group, strip = divmod(y, strips)
        for comp in range(4):
            at = (comp * strips + strip) * layers
            value = block[group, at : at + layers, :]
            if comp < 3:
                field[pl.ds(comp * layers * count + y, layers, stride=count), :] = value
            else:
                warmed[pl.ds(y, layers, stride=count), :] = value


def near(shape, dtype):
    return pltpu.VMEM(shape, dtype)


def call(kernel, out_shape, in_specs, scratch=(), megabytes=16, flops=0, bytes_accessed=0):
    many = isinstance(out_shape, (list, tuple))
    return pl.pallas_call(
        kernel,
        out_shape=out_shape,
        in_specs=in_specs,
        out_specs=[VMEM] * len(out_shape) if many else VMEM,
        scratch_shapes=list(scratch),
        compiler_params=pltpu.CompilerParams(vmem_limit_bytes=megabytes * 1024 * 1024),
        cost_estimate=pl.CostEstimate(
            flops=flops, bytes_accessed=bytes_accessed, transcendentals=0
        ),
    )


def far(value):
    return pltpu.with_memory_space_constraint(value, pltpu.HBM)


def with_tables(
    kernel, out_shape, operands, tables, scalars=(), scratch=(), copies=0, megabytes=32
):
    tables = [jnp.asarray(a) for a in tables]
    return call(
        kernel,
        out_shape,
        [VMEM] * len(operands) + [ANY] * (len(tables) + len(scalars)),
        [pltpu.VMEM(a.shape, a.dtype) for a in tables]
        + [pltpu.SMEM(a.shape, a.dtype) for a in scalars]
        + list(scratch)
        + [pltpu.SemaphoreType.DMA((copies,))],
        megabytes=megabytes,
    )(*operands, *[far(a) for a in tables], *[far(a) for a in scalars])


def local(
    tx, ty, order, heat, kind, moment, tensor, nodes, factor, threshold, spot_row, spot_col
):
    layers, count, width = heat.shape
    strips = count // tx
    comps = 3
    lines = comps * strips * layers
    points_x, points_y = tx * width, ty * count
    members = 2
    cells = layers * count

    heat = heat.reshape(cells, width)
    kind = kind.reshape(cells, width)
    moment = moment.reshape(comps * cells, width)
    heat, kind, moment, rows = call(
        edges_kernel,
        [
            near((cells, width), F32),
            near((cells, width), jnp.int32),
            near((comps * cells, width), F32),
            near((2, 2 * REACH, layers, width), F32),
        ],
        [ANY] * 3,
        [pltpu.SemaphoreType.DMA((3,))],
    )(far(heat), far(kind), far(moment))

    def moved(value, step):
        pairs = [(i, i + step) for i in range(ty) if 0 <= i + step < ty]
        return lax.ppermute(value, "ty", pairs)

    above = moved(rows[1], 1)
    below = moved(rows[0], -1)
    tall = 2 * (strips + 2 * REACH) + comps * strips
    block = call(send_kernel, near((tx, tall * layers, width), F32), [VMEM] * 5)(
        heat, kind, moment, above, below
    )
    block = lax.all_to_all(block, "tx", split_axis=0, concat_axis=0, tiled=True)

    layer, layer_back = layer_tables(layers, strips, comps, order)
    along, along_back, sort = along_tables(points_x, tx)
    across, across_back = across_tables(points_y, tx, ty, strips)
    senders = tx * ty
    message = members * comps * 2 * strips
    span = 2 * points_y // RADIX

    def tripled(table):
        high, low = two_terms(table)
        return np.concatenate([high, high, low], 1)

    spectra, warmed = with_tables(
        functools.partial(rows_kernel, total_rows=points_y),
        [
            jax.ShapeDtypeStruct((senders, message, width), F32),
            near((tx, strips * layers, width), F32),
        ],
        [block],
        [sort, *two_terms(along), tripled(layer)],
        [nodes, factor, threshold, spot_row, spot_col],
        copies=7 + 2 * RADIX,
    )
    data = lax.all_to_all(spectra, ("tx", "ty"), split_axis=0, concat_axis=0, tiled=True)
    columns = members * comps * width
    field = with_tables(
        spectrum_kernel,
        jax.ShapeDtypeStruct((senders * message, width), F32),
        [data.reshape(senders * message, width)],
        [tensor, *two_terms(across), *two_terms(across_back)],
        (),
        [
            pltpu.VMEM((RADIX, 2 * span, columns), F32),
            pltpu.VMEM((RADIX, 2 * span, columns), BF16),
            pltpu.VMEM((RADIX, 2 * span, columns), BF16),
        ],
        copies=1 + 4 * RADIX,
        megabytes=44,
    )
    field = field.reshape(senders, message, width)
    data = lax.all_to_all(field, ("tx", "ty"), split_axis=0, concat_axis=0, tiled=True)
    scale = -1.0 / (2 * layers * 2 * points_y * 2 * points_x)
    block = with_tables(
        functools.partial(cells_kernel, scale=scale),
        near((tx, lines + strips * layers, width), F32),
        [data, warmed],
        [tripled(layer_back), *two_terms(along_back), np.ascontiguousarray(sort.T)],
        copies=2 + 2 * RADIX,
    )
    block = lax.all_to_all(block, "tx", split_axis=0, concat_axis=0, tiled=True)
    demag, warmed = call(
        place_kernel,
        [jax.ShapeDtypeStruct((comps * cells, width), F32), jax.ShapeDtypeStruct((cells, width), F32)],
        [VMEM],
    )(block)
    return (
        warmed.reshape(layers, count, width),
        demag.reshape(comps, layers, count, width),
    )


def solution(mesh):
    in_specs = (
        P(None, "ty", "tx"),
        P(None, "ty", "tx"),
        P(None, None, "ty", "tx"),
        P(None, "tx", None, "ty"),
        P(),
        P(),
        P(),
        P(),
        P(),
    )
    out_specs = (P(None, "ty", "tx"), P(None, None, "ty", "tx"))
    body = functools.partial(local, mesh.shape["tx"], mesh.shape["ty"], "whole")
    return jax.shard_map(body, mesh=mesh, in_specs=in_specs, out_specs=out_specs, check_vma=False)
```

```python
import functools
import math

import jax
import jax.numpy as jnp
import ml_dtypes
import numpy as np
from jax import lax
from jax.experimental import pallas as pl
from jax.experimental.pallas import tpu as pltpu
from jax.sharding import PartitionSpec as P

SWEEPS = 2
AMBIENT_HEAT = 0.3
STEP_RATE = 0.05
LASER_POWER = 4.0
LASER_DEPTH = 4.0
ORDERING_SPREAD = 0.08
TABLE_LOW = 0.2
TABLE_SPAN = 1.6
RADIX = 4
REACH = SWEEPS
PAIRS = ((0, 3, 4), (3, 1, 5), (4, 5, 2))
VMEM = pl.BlockSpec(memory_space=pltpu.VMEM)
ANY = pl.BlockSpec(memory_space=pl.ANY)
F32 = jnp.float32
BF16 = jnp.bfloat16


def two_terms(table):
    table = np.asarray(table, np.float64)
    high = table.astype(np.float32).astype(ml_dtypes.bfloat16)
    low = (table - high.astype(np.float64)).astype(np.float32).astype(ml_dtypes.bfloat16)
    return (high, low)


def waves(products, length):
    angles = 2.0 * math.pi / length * (products % length)
    return (np.cos(angles), np.sin(angles))


def split(values):
    high = values.astype(BF16)
    low = (values - high.astype(F32)).astype(BF16)
    return (high, low)


def matmul(left, right):
    return lax.dot_general(left, right, (((1,), (0,)), ((), ())), preferred_element_type=F32)


def layer_tables(layers, strips, comps, order):
    count = 2 * layers
    owners = count // 2
    rows_in = comps * strips * layers
    if order == "whole":
        shape = (owners, 2, comps, 2, strips)
    else:
        shape = (2, owners, comps, 2, strips)
    index = np.indices(shape).reshape(5, -1)
    if order == "whole":
        owner, member, comp, part, strip = index
    else:
        member, owner, comp, part, strip = index
    freq = 2 * owner + member
    comp_in, strip_in, layer_in = np.indices((comps, strips, layers)).reshape(3, -1)
    same = (comp[:, None] == comp_in[None]) & (strip[:, None] == strip_in[None])
    cosine, sine = waves(freq[:, None] * layer_in[None], count)
    zero = part[:, None] == 0
    from_real = np.where(zero, cosine, -sine) * same
    from_imag = np.where(zero, sine, cosine) * same
    forward = np.concatenate([from_real, from_imag], 1)
    return forward, forward.T


def along_tables(points, devices):
    length = 2 * points
    span = length // RADIX
    sub = points // RADIX
    a = np.arange(sub)
    v = np.arange(span)
    forward = np.zeros((RADIX, sub, 2 * span))
    for b in range(RADIX):
        cosine, sine = waves(v[None, :] * (RADIX * a + b)[:, None], length)
        forward[b] = np.concatenate([cosine, -sine], 1)
    order = np.zeros((points, points), np.float32)
    for b in range(RADIX):
        order[RADIX * a + b, b * sub + a] = 1.0
    return forward, forward.transpose(0, 2, 1), order.astype(ml_dtypes.bfloat16)


def across_tables(points, groups, blocks, strips):
    length = 2 * points
    span = length // RADIX
    part, group, block = np.indices((2, groups, blocks)).reshape(3, -1)
    v = np.arange(span)
    forward = np.zeros((RADIX, 2 * span, part.size))
    for b in range(RADIX):
        y = strips * (groups * block + group) + b
        cosine, sine = waves(v[:, None] * y[None, :], length)
        zero = part[None, :] == 0
        forward[b, :span] = np.where(zero, cosine, sine)
        forward[b, span:] = np.where(zero, -sine, cosine)
    return forward, forward.transpose(0, 2, 1)


def fetch(pairs, sems):
    copies = [
        pltpu.make_async_copy(source, target, sems.at[at])
        for at, (source, target) in enumerate(pairs)
    ]
    for copy in copies:
        copy.start()
    return copies


def chosen(which, values):
    total = jnp.zeros(which.shape, F32)
    for grain in range(values.shape[0]):
        total = total + jnp.where(which == grain, values[grain], 0.0)
    return total


def edges_kernel(heat_in, kind_in, moment_in, heat, kind, moment, rows, sems):
    copies = fetch([(heat_in, heat), (kind_in, kind), (moment_in, moment)], sems)
    layers, count = 8, heat.shape[0] // 8
    copies[0].wait()
    copies[1].wait()
    for side, first in enumerate((0, count - REACH)):
        for j in range(REACH):
            at = pl.ds(first + j, layers, stride=count)
            rows[side, j] = heat[at, :]
            rows[side, REACH + j] = kind[at, :].astype(F32)
    copies[2].wait()


def send_kernel(heat, kind, moment, above, below, out):
    layers, count = 8, heat.shape[0] // 8
    groups = out.shape[0]
    strips = count // groups
    tall = strips + 2 * REACH
    for group in range(groups):
        for i in range(tall):
            y = group * strips - REACH + i
            if y < 0:
                pair = (above[y + REACH], above[y + 2 * REACH])
            elif y >= count:
                pair = (below[y - count], below[y - count + REACH])
            else:
                at = pl.ds(y, layers, stride=count)
                pair = (heat[at, :], kind[at, :].astype(F32))
            for which, value in enumerate(pair):
                out[group, (which * tall + i) * layers : (which * tall + i + 1) * layers, :] = value
        for comp in range(3):
            for strip in range(strips):
                at = pl.ds(comp * layers * count + group * strips + strip, layers, stride=count)
                to = (2 * tall + comp * strips + strip) * layers
                out[group, to : to + layers, :] = moment[at, :]


def heat_rows(block, nodes, factor, threshold, spot_row, spot_col, total_rows):
    layers = 8
    groups, lines, width = block.shape
    total_cols = groups * width
    strips = (lines // layers - 4 * REACH) // 5
    tall = strips + 2 * REACH
    row_base = (lax.axis_index("ty") * groups + lax.axis_index("tx")) * strips - REACH
    shape = (layers, total_cols)
    column = lax.broadcasted_iota(jnp.int32, shape, 1)
    depth = lax.broadcasted_iota(jnp.int32, shape, 0)
    spacing = TABLE_SPAN / (nodes.shape[0] - 1)
    slopes = [(nodes[j + 1] - nodes[j]) * (1.0 / spacing) for j in range(nodes.shape[0] - 1)]

    def whole(index):
        at = index * layers
        return jnp.concatenate([block[t, at : at + layers, :] for t in range(groups)], 1)

    def chosen(which, values):
        total = jnp.zeros(which.shape, F32)
        for grain in range(values.shape[0]):
            total = total + jnp.where(which == float(grain), values[grain], 0.0)
        return total

    def conductivity(theta, gain):
        absolute = theta + AMBIENT_HEAT
        total = jnp.zeros_like(theta) + nodes[0]
        for j, slope in enumerate(slopes):
            total = total + slope * jnp.clip(absolute - (TABLE_LOW + j * spacing), 0.0, spacing)
        return gain * total

    inside = {}
    thetas = {}
    gains = {}
    for i in range(tall):
        y = row_base + i
        inside[i] = jnp.where((y >= 0) & (y < total_rows), 1.0, 0.0)
        thetas[i] = (whole(i) - AMBIENT_HEAT) * inside[i]
        gains[i] = chosen(whole(tall + i), factor) * inside[i]
    not_top = depth > 0
    not_bottom = depth < layers - 1
    for sweep in range(SWEEPS):
        shifted = column - spot_col[sweep] + total_cols // 2
        shifted = jnp.where(shifted < 0, shifted + total_cols, shifted)
        shifted = jnp.where(shifted >= total_cols, shifted - total_cols, shifted)
        offset = (shifted - total_cols // 2).astype(F32) * (1.0 / (0.5 * width))
        along = jnp.exp(depth.astype(F32) * (-1.0 / LASER_DEPTH)) * jnp.exp(-0.5 * offset * offset)
        k = {i: conductivity(thetas[i], gains[i]) for i in range(sweep, tall - sweep)}
        fresh = {}
        for i in range(sweep + 1, tall - sweep - 1):
            theta, own = thetas[i], k[i]
            flux = (own + k[i - 1]) * (thetas[i - 1] - theta)
            flux = flux + (own + k[i + 1]) * (thetas[i + 1] - theta)
            for turn in (1, total_cols - 1):
                flux = flux + (own + pltpu.roll(own, turn, 1)) * (pltpu.roll(theta, turn, 1) - theta)
            for turn, valid in ((1, not_top), (layers - 1, not_bottom)):
                part = (own + pltpu.roll(own, turn, 0)) * (pltpu.roll(theta, turn, 0) - theta)
                flux = flux + jnp.where(valid, part, 0.0)
            across = (row_base + i - spot_row[sweep]).astype(F32) * (1.0 / 32.0)
            across = jnp.exp(jnp.full((layers, width), -0.5, F32) * (across * across))
            source = along * jnp.concatenate([across] * groups, 1)
            value = theta + STEP_RATE * (0.5 * flux + LASER_POWER * source)
            fresh[i] = value * inside[i]
        thetas = fresh
    warmed = []
    fractions = []
    for strip in range(strips):
        value = thetas[REACH + strip] + AMBIENT_HEAT
        limit = chosen(whole(tall + REACH + strip), threshold)
        warmed.append(value)
        fractions.append(1.0 / (1.0 + jnp.exp((value - limit) * (1.0 / ORDERING_SPREAD))))
    scaled = []
    for comp in range(3):
        for strip in range(strips):
            scaled.append(whole(2 * tall + comp * strips + strip) * fractions[strip])
    return warmed, jnp.concatenate(scaled, 0)


def turns(t, sign):
    (ar, ai), (br, bi), (cr, ci), (dr, di) = t
    er, ei, fr, fi = ar + cr, ai + ci, ar - cr, ai - ci
    gr, gi, hr, hi = br + dr, bi + di, br - dr, bi - di
    minus = (fr + hi, fi - hr)
    plus = (fr - hi, fi + hr)
    one, three = (minus, plus) if sign < 0 else (plus, minus)
    return ((er + gr, ei + gi), one, (er - gr, ei - gi), three)


def matmul_terms(left, right):
    left_high, left_low = left
    right_high, right_low = right
    return matmul(
        jnp.concatenate([left_high, left_high, left_low], 1),
        jnp.concatenate([right_high, right_low, right_high], 0),
    )


def rows_kernel(
    block, order_in, high_in, low_in, layer_in, nodes_in, factor_in, threshold_in, spot_row_in, spot_col_in,
    out, warmed, order, high, low, layer, nodes, factor, threshold, spot_row, spot_col, sems, *, total_rows
):
    copies = fetch(
        [
            (nodes_in, nodes), (factor_in, factor), (threshold_in, threshold),
            (spot_row_in, spot_row), (spot_col_in, spot_col), (order_in, order),
        ]
        + [pair for b in range(RADIX) for pair in ((high_in.at[b], high.at[b]), (low_in.at[b], low.at[b]))]
        + [(layer_in, layer)],
        sems,
    )
    for copy in copies[:5]:
        copy.wait()
    copies = copies[5:]
    groups, _, width = block.shape
    points = groups * width
    sub = points // RADIX
    span = high.shape[2] // 2
    kept, values = heat_rows(block, nodes, factor, threshold, spot_row, spot_col, total_rows)
    lines = values.shape[0]
    for strip, value in enumerate(kept):
        for t in range(groups):
            warmed[t, strip * 8 : strip * 8 + 8, :] = value[:, t * width : (t + 1) * width]
    both = jnp.concatenate(split(values), 0)
    copies[0].wait()
    both = matmul(both, order[...]).astype(BF16)
    parts = []
    for copy in copies[1:]:
        copy.wait()
    for b in range(RADIX):
        data = both[:, b * sub : (b + 1) * sub]
        total = matmul_terms((data[:lines], data[lines:]), (high[b], low[b]))
        parts.append((total[:, :span], total[:, span:]))
    slabs = span // width
    blocks = RADIX * slabs
    for u, (real, imag) in enumerate(turns(parts, -1)):
        data_high, data_low = split(jnp.concatenate([real, imag], 0))
        total = matmul(layer[...], jnp.concatenate([data_high, data_low, data_high], 0))
        rows = total.shape[0] // groups
        for t in range(groups):
            for slab in range(slabs):
                out[t * blocks + u * slabs + slab] = total[
                    t * rows : (t + 1) * rows, slab * width : (slab + 1) * width
                ]


def spectrum_kernel(
    data, tensor_in, high_in, low_in, back_high_in, back_low_in, out,
    tensor, high, low, back_high, back_low, sums, fields_high, fields_low, sems
):
    comps = 3
    width = data.shape[1]
    senders = high.shape[2] // 2
    lines = data.shape[0] // senders
    units = lines // 8
    members = units // comps
    span = high.shape[1] // 2
    pairs = []
    for b in range(RADIX):
        pairs += [(high_in.at[b], high.at[b]), (low_in.at[b], low.at[b])]
    pairs += [(tensor_in, tensor)]
    for b in range(RADIX):
        pairs += [(back_high_in.at[b], back_high.at[b]), (back_low_in.at[b], back_low.at[b])]
    copies = fetch(pairs, sems)
    for copy in copies[: 2 * RADIX]:
        copy.wait()
    for b in range(RADIX):
        pieces = []
        for unit in range(units):
            both = [
                data[pl.ds(unit * 8 + part * RADIX + b, senders, stride=lines), :]
                for part in range(2)
            ]
            pieces.append(jnp.concatenate(both, 0))
        sums[b] = matmul_terms((high[b], low[b]), split(jnp.concatenate(pieces, 1)))
    copies[2 * RADIX].wait()
    piece = 16

    def multiply(step, carry):
        at = pl.multiple_of(step * piece, piece)
        for member in range(members):
            spectra = []
            for comp in range(comps):
                lanes = pl.ds((member * comps + comp) * width, width)
                t = [
                    (sums[b, pl.ds(at, piece), lanes], sums[b, pl.ds(span + at, piece), lanes])
                    for b in range(RADIX)
                ]
                spectra.append(turns(t, -1))
            field = [[None] * RADIX for _ in range(comps)]
            for u in range(RADIX):
                taps = [tensor[p, member, pl.ds(u * span + at, piece), :] for p in range(6)]
                for target in range(comps):
                    field[target][u] = tuple(
                        taps[PAIRS[target][0]] * spectra[0][u][part]
                        + taps[PAIRS[target][1]] * spectra[1][u][part]
                        + taps[PAIRS[target][2]] * spectra[2][u][part]
                        for part in range(2)
                    )
            for comp in range(comps):
                lanes = pl.ds((member * comps + comp) * width, width)
                for b, both in enumerate(turns(field[comp], 1)):
                    for part, value in enumerate(both):
                        data_high, data_low = split(value)
                        rows = pl.ds(part * span + at, piece)
                        fields_high[b, rows, lanes] = data_high
                        fields_low[b, rows, lanes] = data_low
        return carry

    lax.fori_loop(0, span // piece, multiply, 0, unroll=4)
    for copy in copies[2 * RADIX + 1 :]:
        copy.wait()
    for b in range(RADIX):
        total = matmul_terms((back_high[b], back_low[b]), (fields_high[b], fields_low[b]))
        for unit in range(units):
            for part in range(2):
                out[pl.ds(unit * 8 + part * RADIX + b, senders, stride=lines), :] = total[
                    part * senders : (part + 1) * senders, unit * width : (unit + 1) * width
                ]


def cells_kernel(data, kept, layer_in, high_in, low_in, order_in, out, layer, high, low, order, sems, *, scale):
    copies = fetch(
        [(layer_in, layer)]
        + [pair for b in range(RADIX) for pair in ((high_in.at[b], high.at[b]), (low_in.at[b], low.at[b]))]
        + [(order_in, order)],
        sems,
    )
    groups, _, width = out.shape
    lines = layer.shape[0] // 2
    span = high.shape[1] // 2
    slabs = span // width
    blocks = RADIX * slabs
    pieces = []
    copies[0].wait()
    for u in range(RADIX):
        columns = []
        for slab in range(slabs):
            at = u * slabs + slab
            columns.append(jnp.concatenate([data[t * blocks + at] for t in range(groups)], 0))
        data_high, data_low = split(jnp.concatenate(columns, 1))
        total = matmul(layer[...], jnp.concatenate([data_high, data_low, data_high], 0))
        pieces.append((total[:lines], total[lines:]))
    sorted_columns = []
    for copy in copies[1:]:
        copy.wait()
    for b, both in enumerate(turns(pieces, 1)):
        sorted_columns.append(matmul_terms(split(jnp.concatenate(both, 1)), (high[b], low[b])))
    values = jnp.concatenate(sorted_columns, 1) * scale
    data_high, data_mid = split(values)
    data_low = (values - data_high.astype(F32) - data_mid.astype(F32)).astype(BF16)
    total = matmul(jnp.concatenate([data_high, data_mid, data_low], 0), order[...])
    values = total[:lines] + total[lines : 2 * lines] + total[2 * lines :]
    for t in range(groups):
        out[t, :lines] = values[:, t * width : (t + 1) * width]
        out[t, lines:] = kept[t]


def place_kernel(block, field, warmed):
    groups, lines, width = block.shape
    layers = 8
    count = warmed.shape[0] // layers
    strips = count // groups
    for y in range(count):
        group, strip = divmod(y, strips)
        for comp in range(4):
            at = (comp * strips + strip) * layers
            value = block[group, at : at + layers, :]
            if comp < 3:
                field[pl.ds(comp * layers * count + y, layers, stride=count), :] = value
            else:
                warmed[pl.ds(y, layers, stride=count), :] = value


def near(shape, dtype):
    return pltpu.VMEM(shape, dtype)


def call(kernel, out_shape, in_specs, scratch=(), megabytes=16, flops=0, bytes_accessed=0):
    many = isinstance(out_shape, (list, tuple))
    return pl.pallas_call(
        kernel,
        out_shape=out_shape,
        in_specs=in_specs,
        out_specs=[VMEM] * len(out_shape) if many else VMEM,
        scratch_shapes=list(scratch),
        compiler_params=pltpu.CompilerParams(vmem_limit_bytes=megabytes * 1024 * 1024),
        cost_estimate=pl.CostEstimate(
            flops=flops, bytes_accessed=bytes_accessed, transcendentals=0
        ),
    )


def far(value):
    return pltpu.with_memory_space_constraint(value, pltpu.HBM)


def with_tables(
    kernel, out_shape, operands, tables, scalars=(), scratch=(), copies=0, megabytes=32
):
    tables = [jnp.asarray(a) for a in tables]
    return call(
        kernel,
        out_shape,
        [VMEM] * len(operands) + [ANY] * (len(tables) + len(scalars)),
        [pltpu.VMEM(a.shape, a.dtype) for a in tables]
        + [pltpu.SMEM(a.shape, a.dtype) for a in scalars]
        + list(scratch)
        + [pltpu.SemaphoreType.DMA((copies,))],
        megabytes=megabytes,
    )(*operands, *[far(a) for a in tables], *[far(a) for a in scalars])


def local(
    tx, ty, order, heat, kind, moment, tensor, nodes, factor, threshold, spot_row, spot_col
):
    layers, count, width = heat.shape
    strips = count // tx
    comps = 3
    lines = comps * strips * layers
    points_x, points_y = tx * width, ty * count
    members = 2
    cells = layers * count

    heat = heat.reshape(cells, width)
    kind = kind.reshape(cells, width)
    moment = moment.reshape(comps * cells, width)
    heat, kind, moment, rows = call(
        edges_kernel,
        [
            near((cells, width), F32),
            near((cells, width), jnp.int32),
            near((comps * cells, width), F32),
            near((2, 2 * REACH, layers, width), F32),
        ],
        [ANY] * 3,
        [pltpu.SemaphoreType.DMA((3,))],
    )(far(heat), far(kind), far(moment))

    def moved(value, step):
        return lax.ppermute(value, "ty", [(i, (i + step) % ty) for i in range(ty)])

    above = moved(rows[1], 1)
    below = moved(rows[0], -1)
    tall = 2 * (strips + 2 * REACH) + comps * strips
    block = call(send_kernel, near((tx, tall * layers, width), F32), [VMEM] * 5)(
        heat, kind, moment, above, below
    )
    block = lax.all_to_all(block, "tx", split_axis=0, concat_axis=0, tiled=True)

    layer, layer_back = layer_tables(layers, strips, comps, order)
    along, along_back, sort = along_tables(points_x, tx)
    across, across_back = across_tables(points_y, tx, ty, strips)
    senders = tx * ty
    message = members * comps * 2 * strips
    span = 2 * points_y // RADIX

    def tripled(table):
        high, low = two_terms(table)
        return np.concatenate([high, high, low], 1)

    spectra, warmed = with_tables(
        functools.partial(rows_kernel, total_rows=points_y),
        [
            jax.ShapeDtypeStruct((senders, message, width), F32),
            near((tx, strips * layers, width), F32),
        ],
        [block],
        [sort, *two_terms(along), tripled(layer)],
        [nodes, factor, threshold, spot_row, spot_col],
        copies=7 + 2 * RADIX,
    )
    data = lax.all_to_all(spectra, ("tx", "ty"), split_axis=0, concat_axis=0, tiled=True)
    columns = members * comps * width
    field = with_tables(
        spectrum_kernel,
        jax.ShapeDtypeStruct((senders * message, width), F32),
        [data.reshape(senders * message, width)],
        [tensor, *two_terms(across), *two_terms(across_back)],
        (),
        [
            pltpu.VMEM((RADIX, 2 * span, columns), F32),
            pltpu.VMEM((RADIX, 2 * span, columns), BF16),
            pltpu.VMEM((RADIX, 2 * span, columns), BF16),
        ],
        copies=1 + 4 * RADIX,
        megabytes=44,
    )
    field = field.reshape(senders, message, width)
    data = lax.all_to_all(field, ("tx", "ty"), split_axis=0, concat_axis=0, tiled=True)
    scale = -1.0 / (2 * layers * 2 * points_y * 2 * points_x)
    block = with_tables(
        functools.partial(cells_kernel, scale=scale),
        near((tx, lines + strips * layers, width), F32),
        [data, warmed],
        [tripled(layer_back), *two_terms(along_back), np.ascontiguousarray(sort.T)],
        copies=2 + 2 * RADIX,
    )
    block = lax.all_to_all(block, "tx", split_axis=0, concat_axis=0, tiled=True)
    demag, warmed = call(
        place_kernel,
        [jax.ShapeDtypeStruct((comps * cells, width), F32), jax.ShapeDtypeStruct((cells, width), F32)],
        [VMEM],
    )(block)
    return (
        warmed.reshape(layers, count, width),
        demag.reshape(comps, layers, count, width),
    )


def solution(mesh):
    in_specs = (
        P(None, "ty", "tx"),
        P(None, "ty", "tx"),
        P(None, None, "ty", "tx"),
        P(None, "tx", None, "ty"),
        P(),
        P(),
        P(),
        P(),
        P(),
    )
    out_specs = (P(None, "ty", "tx"), P(None, None, "ty", "tx"))
    body = functools.partial(local, mesh.shape["tx"], mesh.shape["ty"], "whole")
    return jax.shard_map(body, mesh=mesh, in_specs=in_specs, out_specs=out_specs, check_vma=False)
```

```python
import functools
import math

import jax
import jax.numpy as jnp
import ml_dtypes
import numpy as np
from jax import lax
from jax.experimental import pallas as pl
from jax.experimental.pallas import tpu as pltpu
from jax.sharding import PartitionSpec as P

SWEEPS = 2
AMBIENT_HEAT = 0.3
STEP_RATE = 0.05
LASER_POWER = 4.0
LASER_DEPTH = 4.0
ORDERING_SPREAD = 0.08
TABLE_LOW = 0.2
TABLE_SPAN = 1.6
RADIX = 4
REACH = SWEEPS
PAIRS = ((0, 3, 4), (3, 1, 5), (4, 5, 2))
VMEM = pl.BlockSpec(memory_space=pltpu.VMEM)
ANY = pl.BlockSpec(memory_space=pl.ANY)
F32 = jnp.float32
BF16 = jnp.bfloat16


def two_terms(table):
    table = np.asarray(table, np.float64)
    high = table.astype(np.float32).astype(ml_dtypes.bfloat16)
    low = (table - high.astype(np.float64)).astype(np.float32).astype(ml_dtypes.bfloat16)
    return (high, low)


def waves(products, length):
    angles = 2.0 * math.pi / length * (products % length)
    return (np.cos(angles), np.sin(angles))


def split(values):
    high = values.astype(BF16)
    low = (values - high.astype(F32)).astype(BF16)
    return (high, low)


def matmul(left, right):
    return lax.dot_general(left, right, (((1,), (0,)), ((), ())), preferred_element_type=F32)


def along_tables(points):
    length = 2 * points
    span = length // RADIX
    a = np.arange(points // RADIX)
    b = np.arange(RADIX)
    v = np.arange(span)
    cosine, sine = waves(v[None, :] * (RADIX * a)[:, None], length)
    forward = np.concatenate([cosine, -sine], 1)
    turn = np.stack(waves(v[None, :] * b[:, None], length), 1).reshape(2 * RADIX, span)
    half = points // 2
    order = np.zeros((half, half), np.float32)
    x = np.arange(half)
    order[x, x % RADIX * (half // RADIX) + x // RADIX] = 1.0
    return forward, turn.astype(np.float32), order.astype(ml_dtypes.bfloat16)


def across_tables(points, groups, blocks, strips):
    length = 2 * points
    span = length // RADIX
    part, group, block = np.indices((2, groups, blocks)).reshape(3, -1)
    v = np.arange(span)
    forward = np.zeros((RADIX, 2 * span, part.size))
    for b in range(RADIX):
        y = strips * (groups * block + group) + b
        cosine, sine = waves(v[:, None] * y[None, :], length)
        zero = part[None, :] == 0
        forward[b, :span] = np.where(zero, cosine, sine)
        forward[b, span:] = np.where(zero, -sine, cosine)
    return forward[:, :span], forward.transpose(0, 2, 1)[:, : part.size // 2]


def fetch(pairs, sems):
    copies = [
        pltpu.make_async_copy(source, target, sems.at[at])
        for at, (source, target) in enumerate(pairs)
    ]
    for copy in copies:
        copy.start()
    return copies


def chosen(which, values):
    total = jnp.zeros(which.shape, F32)
    for grain in range(values.shape[0]):
        total = total + jnp.where(which == grain, values[grain], 0.0)
    return total


def edges_kernel(heat_in, kind_in, moment_in, heat, kind, moment, rows, sems):
    copies = fetch([(heat_in, heat), (kind_in, kind), (moment_in, moment)], sems)
    layers, count = 8, heat.shape[0] // 8
    copies[0].wait()
    copies[1].wait()
    for side, first in enumerate((0, count - REACH)):
        for j in range(REACH):
            at = pl.ds(first + j, layers, stride=count)
            rows[side, j] = heat[at, :]
            rows[side, REACH + j] = kind[at, :].astype(F32)
    copies[2].wait()


def send_kernel(heat, kind, moment, above, below, out):
    layers, count = 8, heat.shape[0] // 8
    groups = out.shape[0]
    strips = count // groups
    tall = strips + 2 * REACH
    for group in range(groups):
        for i in range(tall):
            y = group * strips - REACH + i
            if y < 0:
                pair = (above[y + REACH], above[y + 2 * REACH])
            elif y >= count:
                pair = (below[y - count], below[y - count + REACH])
            else:
                at = pl.ds(y, layers, stride=count)
                pair = (heat[at, :], kind[at, :].astype(F32))
            for which, value in enumerate(pair):
                out[group, (which * tall + i) * layers : (which * tall + i + 1) * layers, :] = value
        for comp in range(3):
            for strip in range(strips):
                at = pl.ds(comp * layers * count + group * strips + strip, layers, stride=count)
                to = (2 * tall + comp * strips + strip) * layers
                out[group, to : to + layers, :] = moment[at, :]


def heat_rows(block, nodes, factor, threshold, spot_row, spot_col, total_rows):
    layers = 8
    groups, lines, width = block.shape
    total_cols = groups * width
    strips = (lines // layers - 4 * REACH) // 5
    tall = strips + 2 * REACH
    row_base = (lax.axis_index("ty") * groups + lax.axis_index("tx")) * strips - REACH
    shape = (layers, total_cols)
    column = lax.broadcasted_iota(jnp.int32, shape, 1)
    depth = lax.broadcasted_iota(jnp.int32, shape, 0)
    spacing = TABLE_SPAN / (nodes.shape[0] - 1)
    slopes = [(nodes[j + 1] - nodes[j]) * (1.0 / spacing) for j in range(nodes.shape[0] - 1)]

    def whole(index):
        at = index * layers
        return jnp.concatenate([block[t, at : at + layers, :] for t in range(groups)], 1)

    def chosen(which, values):
        total = jnp.zeros(which.shape, F32)
        for grain in range(values.shape[0]):
            total = total + jnp.where(which == float(grain), values[grain], 0.0)
        return total

    def conductivity(theta, gain):
        absolute = theta + AMBIENT_HEAT
        total = jnp.zeros_like(theta) + nodes[0]
        for j, slope in enumerate(slopes):
            total = total + slope * jnp.clip(absolute - (TABLE_LOW + j * spacing), 0.0, spacing)
        return gain * total

    inside = {}
    thetas = {}
    gains = {}
    for i in range(tall):
        y = row_base + i
        inside[i] = jnp.where((y >= 0) & (y < total_rows), 1.0, 0.0)
        thetas[i] = (whole(i) - AMBIENT_HEAT) * inside[i]
        gains[i] = chosen(whole(tall + i), factor) * inside[i]
    not_top = depth > 0
    not_bottom = depth < layers - 1
    for sweep in range(SWEEPS):
        shifted = column - spot_col[sweep] + total_cols // 2
        shifted = jnp.where(shifted < 0, shifted + total_cols, shifted)
        shifted = jnp.where(shifted >= total_cols, shifted - total_cols, shifted)
        offset = (shifted - total_cols // 2).astype(F32) * (1.0 / (0.5 * width))
        along = jnp.exp(depth.astype(F32) * (-1.0 / LASER_DEPTH)) * jnp.exp(-0.5 * offset * offset)
        k = {i: conductivity(thetas[i], gains[i]) for i in range(sweep, tall - sweep)}
        fresh = {}
        for i in range(sweep + 1, tall - sweep - 1):
            theta, own = thetas[i], k[i]
            flux = (own + k[i - 1]) * (thetas[i - 1] - theta)
            flux = flux + (own + k[i + 1]) * (thetas[i + 1] - theta)
            for turn in (1, total_cols - 1):
                flux = flux + (own + pltpu.roll(own, turn, 1)) * (pltpu.roll(theta, turn, 1) - theta)
            for turn, valid in ((1, not_top), (layers - 1, not_bottom)):
                part = (own + pltpu.roll(own, turn, 0)) * (pltpu.roll(theta, turn, 0) - theta)
                flux = flux + jnp.where(valid, part, 0.0)
            across = (row_base + i - spot_row[sweep]).astype(F32) * (1.0 / 32.0)
            across = jnp.exp(jnp.full((layers, width), -0.5, F32) * (across * across))
            source = along * jnp.concatenate([across] * groups, 1)
            value = theta + STEP_RATE * (0.5 * flux + LASER_POWER * source)
            fresh[i] = value * inside[i]
        thetas = fresh
    warmed = []
    fractions = []
    for strip in range(strips):
        value = thetas[REACH + strip] + AMBIENT_HEAT
        limit = chosen(whole(tall + REACH + strip), threshold)
        warmed.append(value)
        fractions.append(1.0 / (1.0 + jnp.exp((value - limit) * (1.0 / ORDERING_SPREAD))))
    scaled = []
    for comp in range(3):
        for strip in range(strips):
            scaled.append(whole(2 * tall + comp * strips + strip) * fractions[strip])
    return warmed, jnp.concatenate(scaled, 0)


def turns(t, sign):
    (ar, ai), (br, bi), (cr, ci), (dr, di) = t
    er, ei, fr, fi = ar + cr, ai + ci, ar - cr, ai - ci
    gr, gi, hr, hi = br + dr, bi + di, br - dr, bi - di
    minus = (fr + hi, fi - hr)
    plus = (fr - hi, fi + hr)
    one, three = (minus, plus) if sign < 0 else (plus, minus)
    return ((er + gr, ei + gi), one, (er - gr, ei - gi), three)


def matmul_terms(left, right):
    left_high, left_low = left
    right_high, right_low = right
    return matmul(
        jnp.concatenate([left_high, left_high, left_low], 1),
        jnp.concatenate([right_high, right_low, right_high], 0),
    )


def eight(x, sign):
    even, odd = turns(x[0::2], sign), turns(x[1::2], sign)
    root = math.sqrt(0.5)
    first, second = [], []
    for k in range(4):
        (er, ei), (ar, ai) = even[k], odd[k]
        if k == 1:
            ar, ai = (ar - sign * ai) * root, (ai + sign * ar) * root
        elif k == 2:
            ar, ai = -sign * ai, sign * ar
        elif k == 3:
            ar, ai = (-ar - sign * ai) * root, (-ai + sign * ar) * root
        first.append((er + ar, ei + ai))
        second.append((er - ar, ei - ai))
    return first + second


def layer_turn(value, layer, layers, high_half, sign):
    if layer == 0:
        return value
    real, imag = value
    angle = math.pi * layer / layers
    cosine = jnp.where(high_half, math.cos(angle), 1.0)
    sine = jnp.where(high_half, sign * math.sin(angle), 0.0)
    return real * cosine - imag * sine, imag * cosine + real * sine


def halves(values):
    middle = values.shape[1] // 2
    return values[:, :middle], values[:, middle:]


def rows_kernel(
    block, order_in, high_in, low_in, turn_in, nodes_in, factor_in, threshold_in, spot_row_in, spot_col_in,
    out, warmed, order, high, low, turn, nodes, factor, threshold, spot_row, spot_col, scaled, sems, *, total_rows
):
    copies = fetch(
        [
            (nodes_in, nodes), (factor_in, factor), (threshold_in, threshold),
            (spot_row_in, spot_row), (spot_col_in, spot_col),
            (order_in, order), (high_in, high), (low_in, low), (turn_in, turn),
        ],
        sems,
    )
    for copy in copies[:5]:
        copy.wait()
    groups, _, width = block.shape
    span = high.shape[1] // 2
    kept, values = heat_rows(block, nodes, factor, threshold, spot_row, spot_col, total_rows)
    layers = 8
    lines = values.shape[0]
    strips = len(kept)
    columns = []
    for t in range(groups):
        scaled[t] = values[:, t * width : (t + 1) * width]
        rows = [
            scaled[t, pl.ds(comp * strips * layers + layer, strips, stride=layers), :]
            for comp in range(3)
            for layer in range(layers)
        ]
        columns.append(jnp.concatenate(rows, 0))
    values = jnp.concatenate(columns, 1)
    for strip, value in enumerate(kept):
        for t in range(groups):
            warmed[t, strip * 8 : strip * 8 + 8, :] = value[:, t * width : (t + 1) * width]
    for copy in copies[5:]:
        copy.wait()
    both = jnp.concatenate(split(values), 0)
    both = [matmul(half, order[...]).astype(BF16) for half in halves(both)]
    piece = both[0].shape[1] // RADIX
    sorted_rows = [
        jnp.concatenate(
            [
                jnp.concatenate([half[term, b * piece : (b + 1) * piece] for half in both], 1)
                for b in range(RADIX)
            ],
            0,
        )
        for term in (slice(0, lines), slice(lines, 2 * lines))
    ]
    total = matmul_terms(sorted_rows, (high[...], low[...]))
    parts = []
    for b in range(RADIX):
        real, imag = halves(total[b * lines : (b + 1) * lines])
        if b:
            cosine, sine = turn[2 * b : 2 * b + 1, :], turn[2 * b + 1 : 2 * b + 2, :]
            real, imag = real * cosine + imag * sine, imag * cosine - real * sine
        parts.append((real, imag))
    slabs = span // width
    blocks = RADIX * slabs
    wide = slabs * width
    high_half = lax.broadcasted_iota(jnp.int32, (2 * strips, wide), 0) >= strips
    for u, spectra in enumerate(turns(parts, -1)):
        for comp in range(3):
            layered = []
            for layer in range(layers):
                at = (comp * layers + layer // 2 * 2) * strips
                tiles = [value[at : at + 2 * strips] for value in spectra]
                moved = [pltpu.roll(tile, strips, 0) for tile in tiles]
                if layer % 2:
                    tiles, moved = moved, tiles
                both = [
                    jnp.where(high_half, other, tile)
                    for tile, other in zip(tiles, moved, strict=True)
                ]
                layered.append(layer_turn(both, layer, layers, high_half, -1))
            for t, value in enumerate(eight(layered, -1)):
                for part in range(2):
                    at = (comp * 2 + part) * 2 * strips
                    for slab in range(slabs):
                        out[t * blocks + u * slabs + slab, at : at + 2 * strips, :] = value[part][
                            :, slab * width : (slab + 1) * width
                        ]


def complex_table(half):
    split_at = half.shape[1] // 2
    turned = jnp.concatenate([-half[:, split_at:], half[:, :split_at]], 1)
    return jnp.concatenate([half, turned], 0)


def spectrum_kernel(
    data, tensor_in, high_in, low_in, back_high_in, back_low_in, out,
    tensor, high, low, back_high, back_low, sums, fields_high, fields_low, sems
):
    comps = 3
    width = data.shape[1]
    senders = high.shape[2] // 2
    lines = data.shape[0] // senders
    units = lines // 8
    members = units // comps
    span = high.shape[1]

    def row_of(unit, part, b):
        member, comp = divmod(unit, comps)
        return ((comp * 2 + part) * members + member) * RADIX + b

    copies = fetch(
        [
            (high_in, high), (low_in, low), (tensor_in, tensor),
            (back_high_in, back_high), (back_low_in, back_low),
        ],
        sems,
    )
    for b in range(RADIX):
        for unit in range(units):
            both = [
                data[pl.ds(row_of(unit, part, b), senders, stride=lines), :] for part in range(2)
            ]
            data_high, data_low = split(jnp.concatenate(both, 0))
            lanes = slice(unit * width, (unit + 1) * width)
            fields_high[b, : 2 * senders, lanes] = data_high
            fields_low[b, : 2 * senders, lanes] = data_low
    copies[0].wait()
    copies[1].wait()
    for b in range(RADIX):
        sums[b] = matmul_terms(
            (complex_table(high[b]), complex_table(low[b])),
            (fields_high[b, : 2 * senders], fields_low[b, : 2 * senders]),
        )
    copies[2].wait()
    piece = 16

    def multiply(step, carry):
        at = pl.multiple_of(step * piece, piece)
        for member in range(members):
            spectra = []
            for comp in range(comps):
                lanes = pl.ds((member * comps + comp) * width, width)
                t = [
                    (sums[b, pl.ds(at, piece), lanes], sums[b, pl.ds(span + at, piece), lanes])
                    for b in range(RADIX)
                ]
                spectra.append(turns(t, -1))
            field = [[None] * RADIX for _ in range(comps)]
            for u in range(RADIX):
                taps = [tensor[p, member, pl.ds(u * span + at, piece), :] for p in range(6)]
                for target in range(comps):
                    field[target][u] = tuple(
                        taps[PAIRS[target][0]] * spectra[0][u][part]
                        + taps[PAIRS[target][1]] * spectra[1][u][part]
                        + taps[PAIRS[target][2]] * spectra[2][u][part]
                        for part in range(2)
                    )
            for comp in range(comps):
                lanes = pl.ds((member * comps + comp) * width, width)
                for b, both in enumerate(turns(field[comp], 1)):
                    for part, value in enumerate(both):
                        data_high, data_low = split(value)
                        rows = pl.ds(part * span + at, piece)
                        fields_high[b, rows, lanes] = data_high
                        fields_low[b, rows, lanes] = data_low
        return carry

    lax.fori_loop(0, span // piece, multiply, 0, unroll=4)
    copies[3].wait()
    copies[4].wait()
    for b in range(RADIX):
        total = matmul_terms(
            (complex_table(back_high[b]), complex_table(back_low[b])),
            (fields_high[b], fields_low[b]),
        )
        for unit in range(units):
            for part in range(2):
                out[pl.ds(row_of(unit, part, b), senders, stride=lines), :] = total[
                    part * senders : (part + 1) * senders, unit * width : (unit + 1) * width
                ]


def cells_kernel(
    data, kept, high_in, low_in, turn_in, order_in, out, high, low, turn, order, sems, *, scale
):
    copies = fetch(
        [(high_in, high), (low_in, low), (turn_in, turn), (order_in, order)],
        sems,
    )
    groups, _, width = out.shape
    layers = 8
    strips = kept.shape[1] // layers
    lines = 3 * layers * strips
    span = high.shape[0] // 2
    slabs = span // width
    blocks = RADIX * slabs
    pieces = []
    high_half = lax.broadcasted_iota(jnp.int32, (2 * strips, slabs * width), 0) >= strips
    for u in range(RADIX):
        columns = []
        for comp in range(3):
            spectra = []
            for t in range(groups):
                both = []
                for part in range(2):
                    at = (comp * 2 + part) * 2 * strips
                    both.append(
                        jnp.concatenate(
                            [
                                data[t * blocks + u * slabs + slab, at : at + 2 * strips, :]
                                for slab in range(slabs)
                            ],
                            1,
                        )
                    )
                spectra.append(both)
            layered = []
            for layer, value in enumerate(eight(spectra, 1)):
                value = layer_turn(value, layer, layers, high_half, 1)
                layered.append([part + pltpu.roll(part, strips, 0) for part in value])
            for layer in range(0, layers, 2):
                columns.append(
                    [
                        jnp.where(high_half, other, own)
                        for own, other in zip(layered[layer], layered[layer + 1], strict=True)
                    ]
                )
        pieces.append(tuple(jnp.concatenate([c[part] for c in columns], 0) for part in range(2)))
    for copy in copies:
        copy.wait()
    rows = []
    for b, (real, imag) in enumerate(turns(pieces, 1)):
        if b:
            cosine, sine = turn[2 * b : 2 * b + 1, :], turn[2 * b + 1 : 2 * b + 2, :]
            real, imag = real * cosine - imag * sine, imag * cosine + real * sine
        rows.append(jnp.concatenate([real, imag], 1))
    total = matmul_terms(split(jnp.concatenate(rows, 0)), (high[...], low[...])) * scale
    sorted_halves = []
    for half in halves(total):
        values = jnp.concatenate([half[b * lines : (b + 1) * lines] for b in range(RADIX)], 1)
        data_high, data_mid = split(values)
        data_low = (values - data_high.astype(F32) - data_mid.astype(F32)).astype(BF16)
        values = matmul(jnp.concatenate([data_high, data_mid, data_low], 0), order[...])
        sorted_halves.append(values[:lines] + values[lines : 2 * lines] + values[2 * lines :])
    values = jnp.concatenate(sorted_halves, 1)
    for t in range(groups):
        out[t, :lines] = values[:, t * width : (t + 1) * width]
        out[t, lines:] = kept[t]


def place_kernel(block, field, warmed):
    groups, lines, width = block.shape
    layers = 8
    count = warmed.shape[0] // layers
    strips = count // groups
    for y in range(count):
        group, strip = divmod(y, strips)
        for comp in range(4):
            if comp < 3:
                at = pl.ds(comp * strips * layers + strip, layers, stride=strips)
                field[pl.ds(comp * layers * count + y, layers, stride=count), :] = block[group, at, :]
            else:
                at = (comp * strips + strip) * layers
                warmed[pl.ds(y, layers, stride=count), :] = block[group, at : at + layers, :]


def near(shape, dtype):
    return pltpu.VMEM(shape, dtype)


def call(kernel, out_shape, in_specs, scratch=(), megabytes=16, flops=0, bytes_accessed=0):
    many = isinstance(out_shape, (list, tuple))
    return pl.pallas_call(
        kernel,
        out_shape=out_shape,
        in_specs=in_specs,
        out_specs=[VMEM] * len(out_shape) if many else VMEM,
        scratch_shapes=list(scratch),
        compiler_params=pltpu.CompilerParams(vmem_limit_bytes=megabytes * 1024 * 1024),
        cost_estimate=pl.CostEstimate(
            flops=flops, bytes_accessed=bytes_accessed, transcendentals=0
        ),
    )


def far(value):
    return pltpu.with_memory_space_constraint(value, pltpu.HBM)


def with_tables(
    kernel, out_shape, operands, tables, scalars=(), scratch=(), copies=0, megabytes=32
):
    tables = [jnp.asarray(a) for a in tables]
    return call(
        kernel,
        out_shape,
        [VMEM] * len(operands) + [ANY] * (len(tables) + len(scalars)),
        [pltpu.VMEM(a.shape, a.dtype) for a in tables]
        + [pltpu.SMEM(a.shape, a.dtype) for a in scalars]
        + list(scratch)
        + [pltpu.SemaphoreType.DMA((copies,))],
        megabytes=megabytes,
    )(*operands, *[far(a) for a in tables], *[far(a) for a in scalars])


def local(
    tx, ty, heat, kind, moment, tensor, nodes, factor, threshold, spot_row, spot_col
):
    layers, count, width = heat.shape
    strips = count // tx
    comps = 3
    lines = comps * strips * layers
    points_x, points_y = tx * width, ty * count
    members = 2
    cells = layers * count

    heat = heat.reshape(cells, width)
    kind = kind.reshape(cells, width)
    moment = moment.reshape(comps * cells, width)
    heat, kind, moment, rows = call(
        edges_kernel,
        [
            near((cells, width), F32),
            near((cells, width), jnp.int32),
            near((comps * cells, width), F32),
            near((2, 2 * REACH, layers, width), F32),
        ],
        [ANY] * 3,
        [pltpu.SemaphoreType.DMA((3,))],
    )(far(heat), far(kind), far(moment))

    def moved(value, step):
        return lax.ppermute(value, "ty", [(i, (i + step) % ty) for i in range(ty)])

    above = moved(rows[1], 1)
    below = moved(rows[0], -1)
    tall = 2 * (strips + 2 * REACH) + comps * strips
    block = call(send_kernel, near((tx, tall * layers, width), F32), [VMEM] * 5)(
        heat, kind, moment, above, below
    )
    block = lax.all_to_all(block, "tx", split_axis=0, concat_axis=0, tiled=True)

    along, turn, sort = along_tables(points_x)
    across, across_back = across_tables(points_y, tx, ty, strips)
    senders = tx * ty
    message = members * comps * 2 * strips
    span = 2 * points_y // RADIX

    spectra, warmed = with_tables(
        functools.partial(rows_kernel, total_rows=points_y),
        [
            jax.ShapeDtypeStruct((senders, message, width), F32),
            near((tx, strips * layers, width), F32),
        ],
        [block],
        [sort, *two_terms(along), turn],
        [nodes, factor, threshold, spot_row, spot_col],
        [pltpu.VMEM((tx, lines, width), F32)],
        copies=9,
    )
    data = lax.all_to_all(spectra, ("tx", "ty"), split_axis=0, concat_axis=0, tiled=True)
    columns = members * comps * width
    field = with_tables(
        spectrum_kernel,
        jax.ShapeDtypeStruct((senders * message, width), F32),
        [data.reshape(senders * message, width)],
        [tensor, *two_terms(across), *two_terms(across_back)],
        (),
        [
            pltpu.VMEM((RADIX, 2 * span, columns), F32),
            pltpu.VMEM((RADIX, 2 * span, columns), BF16),
            pltpu.VMEM((RADIX, 2 * span, columns), BF16),
        ],
        copies=5,
        megabytes=44,
    )
    field = field.reshape(senders, message, width)
    data = lax.all_to_all(field, ("tx", "ty"), split_axis=0, concat_axis=0, tiled=True)
    scale = -1.0 / (2 * layers * 2 * points_y * 2 * points_x)
    block = with_tables(
        functools.partial(cells_kernel, scale=scale),
        near((tx, lines + strips * layers, width), F32),
        [data, warmed],
        [*two_terms(along.T), turn, np.ascontiguousarray(sort.T)],
        copies=4,
    )
    block = lax.all_to_all(block, "tx", split_axis=0, concat_axis=0, tiled=True)
    demag, warmed = call(
        place_kernel,
        [jax.ShapeDtypeStruct((comps * cells, width), F32), jax.ShapeDtypeStruct((cells, width), F32)],
        [VMEM],
    )(block)
    return (
        warmed.reshape(layers, count, width),
        demag.reshape(comps, layers, count, width),
    )


def solution(mesh):
    in_specs = (
        P(None, "ty", "tx"),
        P(None, "ty", "tx"),
        P(None, None, "ty", "tx"),
        P(None, "tx", None, "ty"),
        P(),
        P(),
        P(),
        P(),
        P(),
    )
    out_specs = (P(None, "ty", "tx"), P(None, None, "ty", "tx"))
    body = functools.partial(local, mesh.shape["tx"], mesh.shape["ty"])
    return jax.shard_map(body, mesh=mesh, in_specs=in_specs, out_specs=out_specs, check_vma=False)
```

```python
import functools
import math

import jax
import jax.numpy as jnp
import ml_dtypes
import numpy as np
from jax import lax
from jax.experimental import pallas as pl
from jax.experimental.pallas import tpu as pltpu
from jax.sharding import PartitionSpec as P

SWEEPS = 2
AMBIENT_HEAT = 0.3
STEP_RATE = 0.05
LASER_POWER = 4.0
LASER_DEPTH = 4.0
ORDERING_SPREAD = 0.08
TABLE_LOW = 0.2
TABLE_SPAN = 1.6
RADIX = 4
REACH = SWEEPS
OUTER, INNER = 2, 4
TX = ("tx_outer", "tx_inner")
PAIRS = ((0, 3, 4), (3, 1, 5), (4, 5, 2))
VMEM = pl.BlockSpec(memory_space=pltpu.VMEM)
ANY = pl.BlockSpec(memory_space=pl.ANY)
F32 = jnp.float32
BF16 = jnp.bfloat16


def two_terms(table):
    table = np.asarray(table, np.float64)
    high = table.astype(np.float32).astype(ml_dtypes.bfloat16)
    low = (table - high.astype(np.float64)).astype(np.float32).astype(ml_dtypes.bfloat16)
    return (high, low)


def waves(products, length):
    angles = 2.0 * math.pi / length * (products % length)
    return (np.cos(angles), np.sin(angles))


def split(values):
    high = values.astype(BF16)
    low = (values - high.astype(F32)).astype(BF16)
    return (high, low)


def matmul(left, right):
    return lax.dot_general(left, right, (((1,), (0,)), ((), ())), preferred_element_type=F32)


def along_tables(points):
    length = 2 * points
    span = length // RADIX
    a = np.arange(points // RADIX)
    b = np.arange(RADIX)
    v = np.arange(span)
    cosine, sine = waves(v[None, :] * (RADIX * a)[:, None], length)
    forward = np.concatenate([cosine, -sine], 1)
    turn = np.stack(waves(v[None, :] * b[:, None], length), 1).reshape(2 * RADIX, span)
    half = points // 2
    order = np.zeros((half, half), np.float32)
    x = np.arange(half)
    order[x, x % RADIX * (half // RADIX) + x // RADIX] = 1.0
    return forward, turn.astype(np.float32), order.astype(ml_dtypes.bfloat16)


def across_tables(points, groups, blocks, strips):
    length = 2 * points
    span = length // RADIX
    part, block, group = np.indices((2, blocks, groups)).reshape(3, -1)
    v = np.arange(span)
    forward = np.zeros((RADIX, 2 * span, part.size))
    for b in range(RADIX):
        y = strips * (groups * block + group) + b
        cosine, sine = waves(v[:, None] * y[None, :], length)
        zero = part[None, :] == 0
        forward[b, :span] = np.where(zero, cosine, sine)
        forward[b, span:] = np.where(zero, -sine, cosine)
    return forward[:, :span], forward.transpose(0, 2, 1)[:, : part.size // 2]


def fetch(pairs, sems):
    copies = [
        pltpu.make_async_copy(source, target, sems.at[at])
        for at, (source, target) in enumerate(pairs)
    ]
    for copy in copies:
        copy.start()
    return copies


def chosen(which, values):
    total = jnp.zeros(which.shape, F32)
    for grain in range(values.shape[0]):
        total = total + jnp.where(which == grain, values[grain], 0.0)
    return total


def rank(t):
    outer, inner = divmod(t, INNER)
    return inner * OUTER + outer


def edges_kernel(heat_in, kind_in, moment_in, heat, kind, moment, rows, sems):
    copies = fetch([(heat_in, heat), (kind_in, kind), (moment_in, moment)], sems)
    layers, count = 8, heat.shape[0] // 8
    copies[0].wait()
    copies[1].wait()
    for side, first in enumerate((0, count - REACH)):
        for j in range(REACH):
            at = pl.ds(first + j, layers, stride=count)
            rows[side, j] = heat[at, :]
            rows[side, REACH + j] = kind[at, :].astype(F32)
    copies[2].wait()


def send_kernel(heat, kind, moment, above, below, out):
    layers, count = 8, heat.shape[0] // 8
    groups = out.shape[0]
    strips = count // groups
    tall = strips + 2 * REACH
    for group in range(groups):
        for i in range(tall):
            y = group * strips - REACH + i
            if y < 0:
                pair = (above[y + REACH], above[y + 2 * REACH])
            elif y >= count:
                pair = (below[y - count], below[y - count + REACH])
            else:
                at = pl.ds(y, layers, stride=count)
                pair = (heat[at, :], kind[at, :].astype(F32))
            for which, value in enumerate(pair):
                at = (which * tall + i) * layers
                out[rank(group), at : at + layers, :] = value
        for comp in range(3):
            for strip in range(strips):
                at = pl.ds(comp * layers * count + group * strips + strip, layers, stride=count)
                to = (2 * tall + comp * strips + strip) * layers
                out[rank(group), to : to + layers, :] = moment[at, :]


def heat_rows(block, nodes, factor, threshold, spot_row, spot_col, total_rows):
    layers = 8
    groups, lines, width = block.shape
    total_cols = groups * width
    strips = (lines // layers - 4 * REACH) // 5
    tall = strips + 2 * REACH
    place = lax.axis_index("ty") * groups + lax.axis_index(TX[0]) * INNER + lax.axis_index(TX[1])
    row_base = place * strips - REACH
    shape = (layers, total_cols)
    column = lax.broadcasted_iota(jnp.int32, shape, 1)
    depth = lax.broadcasted_iota(jnp.int32, shape, 0)
    spacing = TABLE_SPAN / (nodes.shape[0] - 1)
    slopes = [(nodes[j + 1] - nodes[j]) * (1.0 / spacing) for j in range(nodes.shape[0] - 1)]

    def whole(index):
        at = index * layers
        return jnp.concatenate(
            [block[rank(t), at : at + layers, :] for t in range(groups)], 1
        )

    def chosen(which, values):
        total = jnp.zeros(which.shape, F32)
        for grain in range(values.shape[0]):
            total = total + jnp.where(which == float(grain), values[grain], 0.0)
        return total

    def conductivity(theta, gain):
        absolute = theta + AMBIENT_HEAT
        total = jnp.zeros_like(theta) + nodes[0]
        for j, slope in enumerate(slopes):
            total = total + slope * jnp.clip(absolute - (TABLE_LOW + j * spacing), 0.0, spacing)
        return gain * total

    inside = {}
    thetas = {}
    gains = {}
    for i in range(tall):
        y = row_base + i
        inside[i] = jnp.where((y >= 0) & (y < total_rows), 1.0, 0.0)
        thetas[i] = (whole(i) - AMBIENT_HEAT) * inside[i]
        gains[i] = chosen(whole(tall + i), factor) * inside[i]
    not_top = depth > 0
    not_bottom = depth < layers - 1
    for sweep in range(SWEEPS):
        shifted = column - spot_col[sweep] + total_cols // 2
        shifted = jnp.where(shifted < 0, shifted + total_cols, shifted)
        shifted = jnp.where(shifted >= total_cols, shifted - total_cols, shifted)
        offset = (shifted - total_cols // 2).astype(F32) * (1.0 / (0.5 * width))
        along = jnp.exp(depth.astype(F32) * (-1.0 / LASER_DEPTH)) * jnp.exp(-0.5 * offset * offset)
        k = {i: conductivity(thetas[i], gains[i]) for i in range(sweep, tall - sweep)}
        fresh = {}
        for i in range(sweep + 1, tall - sweep - 1):
            theta, own = thetas[i], k[i]
            flux = (own + k[i - 1]) * (thetas[i - 1] - theta)
            flux = flux + (own + k[i + 1]) * (thetas[i + 1] - theta)
            for turn in (1, total_cols - 1):
                flux = flux + (own + pltpu.roll(own, turn, 1)) * (pltpu.roll(theta, turn, 1) - theta)
            for turn, valid in ((1, not_top), (layers - 1, not_bottom)):
                part = (own + pltpu.roll(own, turn, 0)) * (pltpu.roll(theta, turn, 0) - theta)
                flux = flux + jnp.where(valid, part, 0.0)
            across = (row_base + i - spot_row[sweep]).astype(F32) * (1.0 / 32.0)
            across = jnp.exp(jnp.full((layers, width), -0.5, F32) * (across * across))
            source = along * jnp.concatenate([across] * groups, 1)
            value = theta + STEP_RATE * (0.5 * flux + LASER_POWER * source)
            fresh[i] = value * inside[i]
        thetas = fresh
    warmed = []
    fractions = []
    for strip in range(strips):
        value = thetas[REACH + strip] + AMBIENT_HEAT
        limit = chosen(whole(tall + REACH + strip), threshold)
        warmed.append(value)
        fractions.append(1.0 / (1.0 + jnp.exp((value - limit) * (1.0 / ORDERING_SPREAD))))
    scaled = []
    for comp in range(3):
        for strip in range(strips):
            scaled.append(whole(2 * tall + comp * strips + strip) * fractions[strip])
    return warmed, jnp.concatenate(scaled, 0)


def turns(t, sign):
    (ar, ai), (br, bi), (cr, ci), (dr, di) = t
    er, ei, fr, fi = ar + cr, ai + ci, ar - cr, ai - ci
    gr, gi, hr, hi = br + dr, bi + di, br - dr, bi - di
    minus = (fr + hi, fi - hr)
    plus = (fr - hi, fi + hr)
    one, three = (minus, plus) if sign < 0 else (plus, minus)
    return ((er + gr, ei + gi), one, (er - gr, ei - gi), three)


def matmul_terms(left, right):
    left_high, left_low = left
    right_high, right_low = right
    return matmul(
        jnp.concatenate([left_high, left_high, left_low], 1),
        jnp.concatenate([right_high, right_low, right_high], 0),
    )


def eight(x, sign):
    even, odd = turns(x[0::2], sign), turns(x[1::2], sign)
    root = math.sqrt(0.5)
    first, second = [], []
    for k in range(4):
        (er, ei), (ar, ai) = even[k], odd[k]
        if k == 1:
            ar, ai = (ar - sign * ai) * root, (ai + sign * ar) * root
        elif k == 2:
            ar, ai = -sign * ai, sign * ar
        elif k == 3:
            ar, ai = (-ar - sign * ai) * root, (-ai + sign * ar) * root
        first.append((er + ar, ei + ai))
        second.append((er - ar, ei - ai))
    return first + second


def layer_turn(value, layer, layers, high_half, sign):
    if layer == 0:
        return value
    real, imag = value
    angle = math.pi * layer / layers
    cosine = jnp.where(high_half, math.cos(angle), 1.0)
    sine = jnp.where(high_half, sign * math.sin(angle), 0.0)
    return real * cosine - imag * sine, imag * cosine + real * sine


def halves(values):
    middle = values.shape[1] // 2
    return values[:, :middle], values[:, middle:]


def rows_kernel(
    block, order_in, high_in, low_in, turn_in, nodes_in, factor_in, threshold_in, spot_row_in, spot_col_in,
    out, warmed, order, high, low, turn, nodes, factor, threshold, spot_row, spot_col, scaled, sems, *, total_rows
):
    copies = fetch(
        [
            (nodes_in, nodes), (factor_in, factor), (threshold_in, threshold),
            (spot_row_in, spot_row), (spot_col_in, spot_col),
            (order_in, order), (high_in, high), (low_in, low), (turn_in, turn),
        ],
        sems,
    )
    for copy in copies[:5]:
        copy.wait()
    groups, _, width = block.shape
    span = high.shape[1] // 2
    kept, values = heat_rows(block, nodes, factor, threshold, spot_row, spot_col, total_rows)
    layers = 8
    lines = values.shape[0]
    strips = len(kept)
    columns = []
    for t in range(groups):
        scaled[t] = values[:, t * width : (t + 1) * width]
        rows = [
            scaled[t, pl.ds(comp * strips * layers + layer, strips, stride=layers), :]
            for comp in range(3)
            for layer in range(layers)
        ]
        columns.append(jnp.concatenate(rows, 0))
    values = jnp.concatenate(columns, 1)
    for strip, value in enumerate(kept):
        for t in range(groups):
            warmed[t, strip * 8 : strip * 8 + 8, :] = value[:, t * width : (t + 1) * width]
    for copy in copies[5:]:
        copy.wait()
    both = jnp.concatenate(split(values), 0)
    both = [matmul(half, order[...]).astype(BF16) for half in halves(both)]
    piece = both[0].shape[1] // RADIX
    sorted_rows = [
        jnp.concatenate(
            [
                jnp.concatenate([half[term, b * piece : (b + 1) * piece] for half in both], 1)
                for b in range(RADIX)
            ],
            0,
        )
        for term in (slice(0, lines), slice(lines, 2 * lines))
    ]
    total = matmul_terms(sorted_rows, (high[...], low[...]))
    parts = []
    for b in range(RADIX):
        real, imag = halves(total[b * lines : (b + 1) * lines])
        if b:
            cosine, sine = turn[2 * b : 2 * b + 1, :], turn[2 * b + 1 : 2 * b + 2, :]
            real, imag = real * cosine + imag * sine, imag * cosine - real * sine
        parts.append((real, imag))
    slabs = span // width
    wide = slabs * width
    high_half = lax.broadcasted_iota(jnp.int32, (2 * strips, wide), 0) >= strips
    for u, spectra in enumerate(turns(parts, -1)):
        for comp in range(3):
            layered = []
            for layer in range(layers):
                at = (comp * layers + layer // 2 * 2) * strips
                tiles = [value[at : at + 2 * strips] for value in spectra]
                moved = [pltpu.roll(tile, strips, 0) for tile in tiles]
                if layer % 2:
                    tiles, moved = moved, tiles
                both = [
                    jnp.where(high_half, other, tile)
                    for tile, other in zip(tiles, moved, strict=True)
                ]
                layered.append(layer_turn(both, layer, layers, high_half, -1))
            for t, value in enumerate(eight(layered, -1)):
                for part in range(2):
                    at = (comp * 2 + part) * 2 * strips
                    for slab in range(slabs):
                        out[(u * slabs + slab) * groups + t, at : at + 2 * strips, :] = value[part][
                            :, slab * width : (slab + 1) * width
                        ]


def complex_table(half):
    split_at = half.shape[1] // 2
    turned = jnp.concatenate([-half[:, split_at:], half[:, :split_at]], 1)
    return jnp.concatenate([half, turned], 0)


def spectrum_kernel(
    data, tensor_in, high_in, low_in, back_high_in, back_low_in, out,
    tensor, high, low, back_high, back_low, sums, fields_high, fields_low, sems
):
    comps = 3
    width = data.shape[1]
    senders = high.shape[2] // 2
    lines = data.shape[0] // senders
    units = lines // 8
    members = units // comps
    span = high.shape[1]

    def row_of(unit, part, b):
        member, comp = divmod(unit, comps)
        return ((comp * 2 + part) * members + member) * RADIX + b

    copies = fetch(
        [
            (high_in, high), (low_in, low), (tensor_in, tensor),
            (back_high_in, back_high), (back_low_in, back_low),
        ],
        sems,
    )
    for b in range(RADIX):
        for unit in range(units):
            both = [
                data[pl.ds(row_of(unit, part, b), senders, stride=lines), :] for part in range(2)
            ]
            data_high, data_low = split(jnp.concatenate(both, 0))
            lanes = slice(unit * width, (unit + 1) * width)
            fields_high[b, : 2 * senders, lanes] = data_high
            fields_low[b, : 2 * senders, lanes] = data_low
    copies[0].wait()
    copies[1].wait()
    for b in range(RADIX):
        sums[b] = matmul_terms(
            (complex_table(high[b]), complex_table(low[b])),
            (fields_high[b, : 2 * senders], fields_low[b, : 2 * senders]),
        )
    copies[2].wait()
    piece = 16

    def multiply(step, carry):
        at = pl.multiple_of(step * piece, piece)
        for member in range(members):
            spectra = []
            for comp in range(comps):
                lanes = pl.ds((member * comps + comp) * width, width)
                t = [
                    (sums[b, pl.ds(at, piece), lanes], sums[b, pl.ds(span + at, piece), lanes])
                    for b in range(RADIX)
                ]
                spectra.append(turns(t, -1))
            field = [[None] * RADIX for _ in range(comps)]
            for u in range(RADIX):
                taps = [tensor[p, member, pl.ds(u * span + at, piece), :] for p in range(6)]
                for target in range(comps):
                    field[target][u] = tuple(
                        taps[PAIRS[target][0]] * spectra[0][u][part]
                        + taps[PAIRS[target][1]] * spectra[1][u][part]
                        + taps[PAIRS[target][2]] * spectra[2][u][part]
                        for part in range(2)
                    )
            for comp in range(comps):
                lanes = pl.ds((member * comps + comp) * width, width)
                for b, both in enumerate(turns(field[comp], 1)):
                    for part, value in enumerate(both):
                        data_high, data_low = split(value)
                        rows = pl.ds(part * span + at, piece)
                        fields_high[b, rows, lanes] = data_high
                        fields_low[b, rows, lanes] = data_low
        return carry

    lax.fori_loop(0, span // piece, multiply, 0, unroll=4)
    copies[3].wait()
    copies[4].wait()
    for b in range(RADIX):
        total = matmul_terms(
            (complex_table(back_high[b]), complex_table(back_low[b])),
            (fields_high[b], fields_low[b]),
        )
        for unit in range(units):
            for part in range(2):
                out[pl.ds(row_of(unit, part, b), senders, stride=lines), :] = total[
                    part * senders : (part + 1) * senders, unit * width : (unit + 1) * width
                ]


def cells_kernel(
    data, kept, high_in, low_in, turn_in, order_in, out, high, low, turn, order, sems, *, scale
):
    copies = fetch(
        [(high_in, high), (low_in, low), (turn_in, turn), (order_in, order)],
        sems,
    )
    groups, _, width = out.shape
    layers = 8
    strips = kept.shape[1] // layers
    lines = 3 * layers * strips
    span = high.shape[0] // 2
    slabs = span // width
    pieces = []
    high_half = lax.broadcasted_iota(jnp.int32, (2 * strips, slabs * width), 0) >= strips
    for u in range(RADIX):
        columns = []
        for comp in range(3):
            spectra = []
            for t in range(groups):
                both = []
                for part in range(2):
                    at = (comp * 2 + part) * 2 * strips
                    both.append(
                        jnp.concatenate(
                            [
                                data[(u * slabs + slab) * groups + t, at : at + 2 * strips, :]
                                for slab in range(slabs)
                            ],
                            1,
                        )
                    )
                spectra.append(both)
            layered = []
            for layer, value in enumerate(eight(spectra, 1)):
                value = layer_turn(value, layer, layers, high_half, 1)
                layered.append([part + pltpu.roll(part, strips, 0) for part in value])
            for layer in range(0, layers, 2):
                columns.append(
                    [
                        jnp.where(high_half, other, own)
                        for own, other in zip(layered[layer], layered[layer + 1], strict=True)
                    ]
                )
        pieces.append(tuple(jnp.concatenate([c[part] for c in columns], 0) for part in range(2)))
    for copy in copies:
        copy.wait()
    rows = []
    for b, (real, imag) in enumerate(turns(pieces, 1)):
        if b:
            cosine, sine = turn[2 * b : 2 * b + 1, :], turn[2 * b + 1 : 2 * b + 2, :]
            real, imag = real * cosine - imag * sine, imag * cosine + real * sine
        rows.append(jnp.concatenate([real, imag], 1))
    total = matmul_terms(split(jnp.concatenate(rows, 0)), (high[...], low[...])) * scale
    sorted_halves = []
    for half in halves(total):
        values = jnp.concatenate([half[b * lines : (b + 1) * lines] for b in range(RADIX)], 1)
        data_high, data_mid = split(values)
        data_low = (values - data_high.astype(F32) - data_mid.astype(F32)).astype(BF16)
        values = matmul(jnp.concatenate([data_high, data_mid, data_low], 0), order[...])
        sorted_halves.append(values[:lines] + values[lines : 2 * lines] + values[2 * lines :])
    values = jnp.concatenate(sorted_halves, 1)
    for t in range(groups):
        out[t, :lines] = values[:, t * width : (t + 1) * width]
        out[t, lines:] = kept[t]


def place_kernel(block, field, warmed):
    groups, lines, width = block.shape
    layers = 8
    count = warmed.shape[0] // layers
    strips = count // groups
    for y in range(count):
        group, strip = divmod(y, strips)
        for comp in range(4):
            if comp < 3:
                at = pl.ds(comp * strips * layers + strip, layers, stride=strips)
                field[pl.ds(comp * layers * count + y, layers, stride=count), :] = block[group, at, :]
            else:
                at = (comp * strips + strip) * layers
                warmed[pl.ds(y, layers, stride=count), :] = block[group, at : at + layers, :]


def near(shape, dtype):
    return pltpu.VMEM(shape, dtype)


def call(kernel, out_shape, in_specs, scratch=(), megabytes=16, flops=0, bytes_accessed=0):
    many = isinstance(out_shape, (list, tuple))
    return pl.pallas_call(
        kernel,
        out_shape=out_shape,
        in_specs=in_specs,
        out_specs=[VMEM] * len(out_shape) if many else VMEM,
        scratch_shapes=list(scratch),
        compiler_params=pltpu.CompilerParams(vmem_limit_bytes=megabytes * 1024 * 1024),
        cost_estimate=pl.CostEstimate(
            flops=flops, bytes_accessed=bytes_accessed, transcendentals=0
        ),
    )


def far(value):
    return pltpu.with_memory_space_constraint(value, pltpu.HBM)


def with_tables(
    kernel, out_shape, operands, tables, scalars=(), scratch=(), copies=0, megabytes=32
):
    tables = [jnp.asarray(a) for a in tables]
    return call(
        kernel,
        out_shape,
        [VMEM] * len(operands) + [ANY] * (len(tables) + len(scalars)),
        [pltpu.VMEM(a.shape, a.dtype) for a in tables]
        + [pltpu.SMEM(a.shape, a.dtype) for a in scalars]
        + list(scratch)
        + [pltpu.SemaphoreType.DMA((copies,))],
        megabytes=megabytes,
    )(*operands, *[far(a) for a in tables], *[far(a) for a in scalars])


def local(
    tx, ty, heat, kind, moment, tensor, nodes, factor, threshold, spot_row, spot_col
):
    layers, count, width = heat.shape
    strips = count // tx
    comps = 3
    lines = comps * strips * layers
    points_x, points_y = tx * width, ty * count
    members = 2
    cells = layers * count

    heat = heat.reshape(cells, width)
    kind = kind.reshape(cells, width)
    moment = moment.reshape(comps * cells, width)
    heat, kind, moment, rows = call(
        edges_kernel,
        [
            near((cells, width), F32),
            near((cells, width), jnp.int32),
            near((comps * cells, width), F32),
            near((2, 2 * REACH, layers, width), F32),
        ],
        [ANY] * 3,
        [pltpu.SemaphoreType.DMA((3,))],
    )(far(heat), far(kind), far(moment))

    def moved(value, step):
        return lax.ppermute(value, "ty", [(i, (i + step) % ty) for i in range(ty)])

    above = moved(rows[1], 1)
    below = moved(rows[0], -1)
    tall = 2 * (strips + 2 * REACH) + comps * strips
    block = call(send_kernel, near((tx, tall * layers, width), F32), [VMEM] * 5)(
        heat, kind, moment, above, below
    )
    block = lax.all_to_all(block, TX[::-1], split_axis=0, concat_axis=0, tiled=True)

    along, turn, sort = along_tables(points_x)
    across, across_back = across_tables(points_y, tx, ty, strips)
    senders = tx * ty
    message = members * comps * 2 * strips
    span = 2 * points_y // RADIX

    spectra, warmed = with_tables(
        functools.partial(rows_kernel, total_rows=points_y),
        [
            jax.ShapeDtypeStruct((senders, message, width), F32),
            near((tx, strips * layers, width), F32),
        ],
        [block],
        [sort, *two_terms(along), turn],
        [nodes, factor, threshold, spot_row, spot_col],
        [pltpu.VMEM((tx, lines, width), F32)],
        copies=9,
    )
    data = lax.all_to_all(spectra, ("ty", *TX), split_axis=0, concat_axis=0, tiled=True)
    columns = members * comps * width
    field = with_tables(
        spectrum_kernel,
        jax.ShapeDtypeStruct((senders * message, width), F32),
        [data.reshape(senders * message, width)],
        [tensor, *two_terms(across), *two_terms(across_back)],
        (),
        [
            pltpu.VMEM((RADIX, 2 * span, columns), F32),
            pltpu.VMEM((RADIX, 2 * span, columns), BF16),
            pltpu.VMEM((RADIX, 2 * span, columns), BF16),
        ],
        copies=5,
        megabytes=44,
    )
    field = field.reshape(senders, message, width)
    data = lax.all_to_all(field, ("ty", *TX), split_axis=0, concat_axis=0, tiled=True)
    scale = -1.0 / (2 * layers * 2 * points_y * 2 * points_x)
    block = with_tables(
        functools.partial(cells_kernel, scale=scale),
        near((tx, lines + strips * layers, width), F32),
        [data, warmed],
        [*two_terms(along.T), turn, np.ascontiguousarray(sort.T)],
        copies=4,
    )
    block = lax.all_to_all(block, TX, split_axis=0, concat_axis=0, tiled=True)
    demag, warmed = call(
        place_kernel,
        [jax.ShapeDtypeStruct((comps * cells, width), F32), jax.ShapeDtypeStruct((cells, width), F32)],
        [VMEM],
    )(block)
    return (
        warmed.reshape(layers, count, width),
        demag.reshape(comps, layers, count, width),
    )


def solution(mesh):
    tx, ty = mesh.shape["tx"], mesh.shape["ty"]
    parts = jax.sharding.Mesh(mesh.devices.reshape(OUTER, tx // OUTER, ty), (*TX, "ty"))
    in_specs = (
        P(None, "ty", TX),
        P(None, "ty", TX),
        P(None, None, "ty", TX),
        P(None, TX, None, "ty"),
        P(),
        P(),
        P(),
        P(),
        P(),
    )
    out_specs = (P(None, "ty", TX), P(None, None, "ty", TX))
    body = functools.partial(local, tx, ty)
    return jax.shard_map(body, mesh=parts, in_specs=in_specs, out_specs=out_specs, check_vma=False)
```

```python
import functools
import math

import jax
import jax.numpy as jnp
import ml_dtypes
import numpy as np
from jax import lax
from jax.experimental import pallas as pl
from jax.experimental.pallas import tpu as pltpu
from jax.sharding import PartitionSpec as P

SWEEPS = 2
AMBIENT_HEAT = 0.3
STEP_RATE = 0.05
LASER_POWER = 4.0
LASER_DEPTH = 4.0
ORDERING_SPREAD = 0.08
TABLE_LOW = 0.2
TABLE_SPAN = 1.6
RADIX = 4
REACH = SWEEPS
PARTS = {"x_hi": 2, "z": 4, "x_lo": 2, "y": 4, "core": 2}
TX, TY = ("x_hi", "z"), ("x_lo", "y", "core")
OUTWARD = ("x_lo", "y", "core", "x_hi", "z")
INWARD = ("y", "z", "x_lo", "x_hi", "core")
PAIRS = ((0, 3, 4), (3, 1, 5), (4, 5, 2))
VMEM = pl.BlockSpec(memory_space=pltpu.VMEM)
ANY = pl.BlockSpec(memory_space=pl.ANY)
F32 = jnp.float32
BF16 = jnp.bfloat16


def two_terms(table):
    table = np.asarray(table, np.float64)
    high = table.astype(np.float32).astype(ml_dtypes.bfloat16)
    low = (table - high.astype(np.float64)).astype(np.float32).astype(ml_dtypes.bfloat16)
    return (high, low)


def waves(products, length):
    angles = 2.0 * math.pi / length * (products % length)
    return (np.cos(angles), np.sin(angles))


def ranks(order, axes):
    sizes = [PARTS[axis] for axis in axes]
    place = dict(zip(axes, np.indices(sizes).reshape(len(axes), -1), strict=True))
    rank = np.zeros(math.prod(sizes), np.int64)
    for axis in order:
        rank = rank * PARTS[axis] + place[axis]
    return [int(r) for r in rank]


def index_of(axes):
    at = 0
    for axis in axes:
        at = at * PARTS[axis] + lax.axis_index(axis)
    return at


def split(values):
    high = values.astype(BF16)
    low = (values - high.astype(F32)).astype(BF16)
    return (high, low)


def matmul(left, right):
    return lax.dot_general(left, right, (((1,), (0,)), ((), ())), preferred_element_type=F32)


def along_tables(points):
    length = 2 * points
    span = length // RADIX
    a = np.arange(points // RADIX)
    b = np.arange(RADIX)
    v = np.arange(span)
    cosine, sine = waves(v[None, :] * (RADIX * a)[:, None], length)
    forward = np.concatenate([cosine, -sine], 1)
    turn = np.stack(waves(v[None, :] * b[:, None], length), 1).reshape(2 * RADIX, span)
    half = points // 2
    order = np.zeros((half, half), np.float32)
    x = np.arange(half)
    order[x, x % RADIX * (half // RADIX) + x // RADIX] = 1.0
    return forward, turn.astype(np.float32), order.astype(ml_dtypes.bfloat16)


def across_tables(points, groups, blocks, strips):
    length = 2 * points
    span = length // RADIX
    group, block = np.indices((groups, blocks)).reshape(2, -1)
    v = np.arange(span)
    tables = []
    for order in (OUTWARD, INWARD):
        y = np.zeros(groups * blocks, np.int64)
        y[ranks(order, TX + TY)] = strips * (groups * block + group)
        tables.append([waves(v[:, None] * (y + b)[None, :], length) for b in range(RADIX)])
    forward = np.stack([np.concatenate([c, s], 1) for c, s in tables[0]])
    back = np.stack([np.concatenate([c.T, -s.T], 1) for c, s in tables[1]])
    return forward, back


def fetch(pairs, sems):
    copies = [
        pltpu.make_async_copy(source, target, sems.at[at])
        for at, (source, target) in enumerate(pairs)
    ]
    for copy in copies:
        copy.start()
    return copies


def chosen(which, values):
    total = jnp.zeros(which.shape, F32)
    for grain in range(values.shape[0]):
        total = total + jnp.where(which == grain, values[grain], 0.0)
    return total


def edges_kernel(heat_in, kind_in, moment_in, heat, kind, moment, rows, sems):
    copies = fetch([(heat_in, heat), (kind_in, kind), (moment_in, moment)], sems)
    layers, count = 8, heat.shape[0] // 8
    copies[0].wait()
    copies[1].wait()
    for side, first in enumerate((0, count - REACH)):
        for j in range(REACH):
            at = pl.ds(first + j, layers, stride=count)
            rows[side, j] = heat[at, :]
            rows[side, REACH + j] = kind[at, :].astype(F32)
    copies[2].wait()


def send_kernel(heat, kind, moment, above, below, out):
    layers, count = 8, heat.shape[0] // 8
    groups = out.shape[0]
    strips = count // groups
    tall = strips + 2 * REACH
    for group in range(groups):
        for i in range(tall):
            y = group * strips - REACH + i
            if y < 0:
                pair = (above[y + REACH], above[y + 2 * REACH])
            elif y >= count:
                pair = (below[y - count], below[y - count + REACH])
            else:
                at = pl.ds(y, layers, stride=count)
                pair = (heat[at, :], kind[at, :].astype(F32))
            for which, value in enumerate(pair):
                at = (which * tall + i) * layers
                out[ranks(TX[::-1], TX)[group], at : at + layers, :] = value
        for comp in range(3):
            for strip in range(strips):
                at = pl.ds(comp * layers * count + group * strips + strip, layers, stride=count)
                to = (2 * tall + comp * strips + strip) * layers
                out[ranks(TX[::-1], TX)[group], to : to + layers, :] = moment[at, :]


def heat_rows(block, nodes, factor, threshold, spot_row, spot_col, total_rows):
    layers = 8
    groups, lines, width = block.shape
    total_cols = groups * width
    strips = (lines // layers - 4 * REACH) // 5
    tall = strips + 2 * REACH
    place = index_of(TY) * groups + index_of(TX)
    row_base = place * strips - REACH
    shape = (layers, total_cols)
    column = lax.broadcasted_iota(jnp.int32, shape, 1)
    depth = lax.broadcasted_iota(jnp.int32, shape, 0)
    spacing = TABLE_SPAN / (nodes.shape[0] - 1)
    slopes = [(nodes[j + 1] - nodes[j]) * (1.0 / spacing) for j in range(nodes.shape[0] - 1)]
    bases = [nodes[j] - slope * (TABLE_LOW + j * spacing) for j, slope in enumerate(slopes)]

    def whole(index):
        at = index * layers
        return jnp.concatenate(
            [block[t, at : at + layers, :] for t in ranks(TX[::-1], TX)], 1
        )

    def chosen(which, values):
        total = jnp.zeros(which.shape, F32)
        for grain in range(values.shape[0]):
            total = total + jnp.where(which == float(grain), values[grain], 0.0)
        return total

    def conductivity(theta, gain):
        absolute = jnp.clip(theta + AMBIENT_HEAT, TABLE_LOW, TABLE_LOW + TABLE_SPAN)
        base = jnp.full_like(theta, bases[0])
        slope = jnp.full_like(theta, slopes[0])
        for j in range(1, len(slopes)):
            beyond = absolute >= TABLE_LOW + j * spacing
            base = jnp.where(beyond, bases[j], base)
            slope = jnp.where(beyond, slopes[j], slope)
        return gain * (base + slope * absolute)

    inside = {}
    thetas = {}
    gains = {}
    for i in range(tall):
        y = row_base + i
        inside[i] = jnp.where((y >= 0) & (y < total_rows), 1.0, 0.0)
        thetas[i] = (whole(i) - AMBIENT_HEAT) * inside[i]
        gains[i] = chosen(whole(tall + i), factor) * inside[i]
    not_top = depth > 0
    not_bottom = depth < layers - 1
    for sweep in range(SWEEPS):
        shifted = column - spot_col[sweep] + total_cols // 2
        shifted = jnp.where(shifted < 0, shifted + total_cols, shifted)
        shifted = jnp.where(shifted >= total_cols, shifted - total_cols, shifted)
        offset = (shifted - total_cols // 2).astype(F32) * (1.0 / (0.5 * width))
        along = jnp.exp(depth.astype(F32) * (-1.0 / LASER_DEPTH)) * jnp.exp(-0.5 * offset * offset)
        k = {i: conductivity(thetas[i], gains[i]) for i in range(sweep, tall - sweep)}
        fresh = {}
        for i in range(sweep + 1, tall - sweep - 1):
            theta, own = thetas[i], k[i]
            flux = (own + k[i - 1]) * (thetas[i - 1] - theta)
            flux = flux + (own + k[i + 1]) * (thetas[i + 1] - theta)
            for turn in (1, total_cols - 1):
                flux = flux + (own + pltpu.roll(own, turn, 1)) * (pltpu.roll(theta, turn, 1) - theta)
            for turn, valid in ((1, not_top), (layers - 1, not_bottom)):
                part = (own + pltpu.roll(own, turn, 0)) * (pltpu.roll(theta, turn, 0) - theta)
                flux = flux + jnp.where(valid, part, 0.0)
            across = (row_base + i - spot_row[sweep]).astype(F32) * (1.0 / 32.0)
            across = jnp.exp(jnp.full((layers, width), -0.5, F32) * (across * across))
            source = along * jnp.concatenate([across] * groups, 1)
            value = theta + STEP_RATE * (0.5 * flux + LASER_POWER * source)
            fresh[i] = value * inside[i]
        thetas = fresh
    warmed = []
    fractions = []
    for strip in range(strips):
        value = thetas[REACH + strip] + AMBIENT_HEAT
        limit = chosen(whole(tall + REACH + strip), threshold)
        warmed.append(value)
        fractions.append(1.0 / (1.0 + jnp.exp((value - limit) * (1.0 / ORDERING_SPREAD))))
    scaled = []
    for comp in range(3):
        for strip in range(strips):
            scaled.append(whole(2 * tall + comp * strips + strip) * fractions[strip])
    return warmed, jnp.concatenate(scaled, 0)


def turns(t, sign):
    (ar, ai), (br, bi), (cr, ci), (dr, di) = t
    er, ei, fr, fi = ar + cr, ai + ci, ar - cr, ai - ci
    gr, gi, hr, hi = br + dr, bi + di, br - dr, bi - di
    minus = (fr + hi, fi - hr)
    plus = (fr - hi, fi + hr)
    one, three = (minus, plus) if sign < 0 else (plus, minus)
    return ((er + gr, ei + gi), one, (er - gr, ei - gi), three)


def matmul_terms(left, right):
    left_high, left_low = left
    right_high, right_low = right
    return matmul(
        jnp.concatenate([left_high, left_high, left_low], 1),
        jnp.concatenate([right_high, right_low, right_high], 0),
    )


def eight(x, sign):
    even, odd = turns(x[0::2], sign), turns(x[1::2], sign)
    root = math.sqrt(0.5)
    first, second = [], []
    for k in range(4):
        (er, ei), (ar, ai) = even[k], odd[k]
        if k == 1:
            ar, ai = (ar - sign * ai) * root, (ai + sign * ar) * root
        elif k == 2:
            ar, ai = -sign * ai, sign * ar
        elif k == 3:
            ar, ai = (-ar - sign * ai) * root, (-ai + sign * ar) * root
        first.append((er + ar, ei + ai))
        second.append((er - ar, ei - ai))
    return first + second


def layer_turn(value, layer, layers, high_half, sign):
    if layer == 0:
        return value
    real, imag = value
    angle = math.pi * layer / layers
    cosine = jnp.where(high_half, math.cos(angle), 1.0)
    sine = jnp.where(high_half, sign * math.sin(angle), 0.0)
    return real * cosine - imag * sine, imag * cosine + real * sine


def halves(values):
    middle = values.shape[1] // 2
    return values[:, :middle], values[:, middle:]


def rows_kernel(
    block, order_in, high_in, low_in, turn_in, nodes_in, factor_in, threshold_in, spot_row_in, spot_col_in,
    out, warmed, order, high, low, turn, nodes, factor, threshold, spot_row, spot_col, scaled, sems, *, total_rows
):
    copies = fetch(
        [
            (nodes_in, nodes), (factor_in, factor), (threshold_in, threshold),
            (spot_row_in, spot_row), (spot_col_in, spot_col),
            (order_in, order), (high_in, high), (low_in, low), (turn_in, turn),
        ],
        sems,
    )
    for copy in copies[:5]:
        copy.wait()
    groups, _, width = block.shape
    span = high.shape[1] // 2
    kept, values = heat_rows(block, nodes, factor, threshold, spot_row, spot_col, total_rows)
    layers = 8
    lines = values.shape[0]
    strips = len(kept)
    columns = []
    for t in range(groups):
        scaled[t] = values[:, t * width : (t + 1) * width]
        rows = [
            scaled[t, pl.ds(comp * strips * layers + layer, strips, stride=layers), :]
            for comp in range(3)
            for layer in range(layers)
        ]
        columns.append(jnp.concatenate(rows, 0))
    values = jnp.concatenate(columns, 1)
    for strip, value in enumerate(kept):
        for t in range(groups):
            warmed[t, strip * 8 : strip * 8 + 8, :] = value[:, t * width : (t + 1) * width]
    for copy in copies[5:]:
        copy.wait()
    both = jnp.concatenate(split(values), 0)
    both = [matmul(half, order[...]).astype(BF16) for half in halves(both)]
    piece = both[0].shape[1] // RADIX
    sorted_rows = [
        jnp.concatenate(
            [
                jnp.concatenate([half[term, b * piece : (b + 1) * piece] for half in both], 1)
                for b in range(RADIX)
            ],
            0,
        )
        for term in (slice(0, lines), slice(lines, 2 * lines))
    ]
    total = matmul_terms(sorted_rows, (high[...], low[...]))
    parts = []
    for b in range(RADIX):
        real, imag = halves(total[b * lines : (b + 1) * lines])
        if b:
            cosine, sine = turn[2 * b : 2 * b + 1, :], turn[2 * b + 1 : 2 * b + 2, :]
            real, imag = real * cosine + imag * sine, imag * cosine - real * sine
        parts.append((real, imag))
    slabs = span // width
    wide = slabs * width
    blocks = RADIX * slabs
    go = ranks(OUTWARD, TX + TY)
    high_half = lax.broadcasted_iota(jnp.int32, (2 * strips, wide), 0) >= strips
    for u, spectra in enumerate(turns(parts, -1)):
        for comp in range(3):
            layered = []
            for layer in range(layers):
                at = (comp * layers + layer // 2 * 2) * strips
                tiles = [value[at : at + 2 * strips] for value in spectra]
                moved = [pltpu.roll(tile, strips, 0) for tile in tiles]
                if layer % 2:
                    tiles, moved = moved, tiles
                both = [
                    jnp.where(high_half, other, tile)
                    for tile, other in zip(tiles, moved, strict=True)
                ]
                layered.append(layer_turn(both, layer, layers, high_half, -1))
            for t, value in enumerate(eight(layered, -1)):
                for part in range(2):
                    at = (comp * 2 + part) * 2 * strips
                    for slab in range(slabs):
                        out[go[t * blocks + u * slabs + slab], at : at + 2 * strips, :] = value[part][
                            :, slab * width : (slab + 1) * width
                        ]


def complex_table(half):
    split_at = half.shape[1] // 2
    turned = jnp.concatenate([-half[:, split_at:], half[:, :split_at]], 1)
    return jnp.concatenate([half, turned], 0)


def spectrum_kernel(
    data, tensor_in, high_in, low_in, back_high_in, back_low_in, out,
    tensor, high, low, back_high, back_low, sums, fields_high, fields_low, sems
):
    comps = 3
    width = data.shape[1]
    senders = high.shape[2] // 2
    lines = data.shape[0] // senders
    units = lines // 8
    members = units // comps
    span = high.shape[1]

    def row_of(unit, part, b):
        member, comp = divmod(unit, comps)
        return ((comp * 2 + part) * members + member) * RADIX + b

    copies = fetch(
        [
            (high_in, high), (low_in, low), (tensor_in, tensor),
            (back_high_in, back_high), (back_low_in, back_low),
        ],
        sems,
    )
    for b in range(RADIX):
        for unit in range(units):
            both = [
                data[pl.ds(row_of(unit, part, b), senders, stride=lines), :] for part in range(2)
            ]
            data_high, data_low = split(jnp.concatenate(both, 0))
            lanes = slice(unit * width, (unit + 1) * width)
            fields_high[b, : 2 * senders, lanes] = data_high
            fields_low[b, : 2 * senders, lanes] = data_low
    copies[0].wait()
    copies[1].wait()
    for b in range(RADIX):
        sums[b] = matmul_terms(
            (complex_table(high[b]), complex_table(low[b])),
            (fields_high[b, : 2 * senders], fields_low[b, : 2 * senders]),
        )
    copies[2].wait()
    piece = 16

    def multiply(step, carry):
        at = pl.multiple_of(step * piece, piece)
        for member in range(members):
            spectra = []
            for comp in range(comps):
                lanes = pl.ds((member * comps + comp) * width, width)
                t = [
                    (sums[b, pl.ds(at, piece), lanes], sums[b, pl.ds(span + at, piece), lanes])
                    for b in range(RADIX)
                ]
                spectra.append(turns(t, -1))
            field = [[None] * RADIX for _ in range(comps)]
            for u in range(RADIX):
                taps = [tensor[p, member, pl.ds(u * span + at, piece), :] for p in range(6)]
                for target in range(comps):
                    field[target][u] = tuple(
                        taps[PAIRS[target][0]] * spectra[0][u][part]
                        + taps[PAIRS[target][1]] * spectra[1][u][part]
                        + taps[PAIRS[target][2]] * spectra[2][u][part]
                        for part in range(2)
                    )
            for comp in range(comps):
                lanes = pl.ds((member * comps + comp) * width, width)
                for b, both in enumerate(turns(field[comp], 1)):
                    for part, value in enumerate(both):
                        data_high, data_low = split(value)
                        rows = pl.ds(part * span + at, piece)
                        fields_high[b, rows, lanes] = data_high
                        fields_low[b, rows, lanes] = data_low
        return carry

    lax.fori_loop(0, span // piece, multiply, 0, unroll=4)
    copies[3].wait()
    copies[4].wait()
    for b in range(RADIX):
        total = matmul_terms(
            (complex_table(back_high[b]), complex_table(back_low[b])),
            (fields_high[b], fields_low[b]),
        )
        for unit in range(units):
            for part in range(2):
                out[pl.ds(row_of(unit, part, b), senders, stride=lines), :] = total[
                    part * senders : (part + 1) * senders, unit * width : (unit + 1) * width
                ]


def cells_kernel(
    data, kept, high_in, low_in, turn_in, order_in, out, high, low, turn, order, sems, *, scale
):
    copies = fetch(
        [(high_in, high), (low_in, low), (turn_in, turn), (order_in, order)],
        sems,
    )
    groups, _, width = out.shape
    layers = 8
    strips = kept.shape[1] // layers
    lines = 3 * layers * strips
    span = high.shape[0] // 2
    slabs = span // width
    blocks = RADIX * slabs
    back = ranks(INWARD, TX + TY)
    pieces = []
    high_half = lax.broadcasted_iota(jnp.int32, (2 * strips, slabs * width), 0) >= strips
    for u in range(RADIX):
        columns = []
        for comp in range(3):
            spectra = []
            for t in range(groups):
                both = []
                for part in range(2):
                    at = (comp * 2 + part) * 2 * strips
                    both.append(
                        jnp.concatenate(
                            [
                                data[back[t * blocks + u * slabs + slab], at : at + 2 * strips, :]
                                for slab in range(slabs)
                            ],
                            1,
                        )
                    )
                spectra.append(both)
            layered = []
            for layer, value in enumerate(eight(spectra, 1)):
                value = layer_turn(value, layer, layers, high_half, 1)
                layered.append([part + pltpu.roll(part, strips, 0) for part in value])
            for layer in range(0, layers, 2):
                columns.append(
                    [
                        jnp.where(high_half, other, own)
                        for own, other in zip(layered[layer], layered[layer + 1], strict=True)
                    ]
                )
        pieces.append(tuple(jnp.concatenate([c[part] for c in columns], 0) for part in range(2)))
    for copy in copies:
        copy.wait()
    rows = []
    for b, (real, imag) in enumerate(turns(pieces, 1)):
        if b:
            cosine, sine = turn[2 * b : 2 * b + 1, :], turn[2 * b + 1 : 2 * b + 2, :]
            real, imag = real * cosine - imag * sine, imag * cosine + real * sine
        rows.append(jnp.concatenate([real, imag], 1))
    total = matmul_terms(split(jnp.concatenate(rows, 0)), (high[...], low[...])) * scale
    sorted_halves = []
    for half in halves(total):
        values = jnp.concatenate([half[b * lines : (b + 1) * lines] for b in range(RADIX)], 1)
        data_high, data_mid = split(values)
        data_low = (values - data_high.astype(F32) - data_mid.astype(F32)).astype(BF16)
        values = matmul(jnp.concatenate([data_high, data_mid, data_low], 0), order[...])
        sorted_halves.append(values[:lines] + values[lines : 2 * lines] + values[2 * lines :])
    values = jnp.concatenate(sorted_halves, 1)
    for t in range(groups):
        out[t, :lines] = values[:, t * width : (t + 1) * width]
        out[t, lines:] = kept[t]


def place_kernel(block, field, warmed):
    groups, lines, width = block.shape
    layers = 8
    count = warmed.shape[0] // layers
    strips = count // groups
    for y in range(count):
        group, strip = divmod(y, strips)
        for comp in range(4):
            if comp < 3:
                at = pl.ds(comp * strips * layers + strip, layers, stride=strips)
                field[pl.ds(comp * layers * count + y, layers, stride=count), :] = block[group, at, :]
            else:
                at = (comp * strips + strip) * layers
                warmed[pl.ds(y, layers, stride=count), :] = block[group, at : at + layers, :]


def near(shape, dtype):
    return pltpu.VMEM(shape, dtype)


def call(kernel, out_shape, in_specs, scratch=(), megabytes=16, flops=0, bytes_accessed=0):
    many = isinstance(out_shape, (list, tuple))
    return pl.pallas_call(
        kernel,
        out_shape=out_shape,
        in_specs=in_specs,
        out_specs=[VMEM] * len(out_shape) if many else VMEM,
        scratch_shapes=list(scratch),
        compiler_params=pltpu.CompilerParams(vmem_limit_bytes=megabytes * 1024 * 1024),
        cost_estimate=pl.CostEstimate(
            flops=flops, bytes_accessed=bytes_accessed, transcendentals=0
        ),
    )


def far(value):
    return pltpu.with_memory_space_constraint(value, pltpu.HBM)


def with_tables(
    kernel, out_shape, operands, tables, scalars=(), scratch=(), copies=0, megabytes=32
):
    tables = [jnp.asarray(a) for a in tables]
    return call(
        kernel,
        out_shape,
        [VMEM] * len(operands) + [ANY] * (len(tables) + len(scalars)),
        [pltpu.VMEM(a.shape, a.dtype) for a in tables]
        + [pltpu.SMEM(a.shape, a.dtype) for a in scalars]
        + list(scratch)
        + [pltpu.SemaphoreType.DMA((copies,))],
        megabytes=megabytes,
    )(*operands, *[far(a) for a in tables], *[far(a) for a in scalars])


def local(
    tx, ty, heat, kind, moment, tensor, nodes, factor, threshold, spot_row, spot_col
):
    layers, count, width = heat.shape
    strips = count // tx
    comps = 3
    lines = comps * strips * layers
    points_x, points_y = tx * width, ty * count
    members = 2
    cells = layers * count

    heat = heat.reshape(cells, width)
    kind = kind.reshape(cells, width)
    moment = moment.reshape(comps * cells, width)
    heat, kind, moment, rows = call(
        edges_kernel,
        [
            near((cells, width), F32),
            near((cells, width), jnp.int32),
            near((comps * cells, width), F32),
            near((2, 2 * REACH, layers, width), F32),
        ],
        [ANY] * 3,
        [pltpu.SemaphoreType.DMA((3,))],
    )(far(heat), far(kind), far(moment))

    def moved(value, step):
        return lax.ppermute(value, TY, [(i, (i + step) % ty) for i in range(ty)])

    above = moved(rows[1], 1)
    below = moved(rows[0], -1)
    tall = 2 * (strips + 2 * REACH) + comps * strips
    block = call(send_kernel, near((tx, tall * layers, width), F32), [VMEM] * 5)(
        heat, kind, moment, above, below
    )
    block = lax.all_to_all(block, TX[::-1], split_axis=0, concat_axis=0, tiled=True)

    along, turn, sort = along_tables(points_x)
    across, across_back = across_tables(points_y, tx, ty, strips)
    senders = tx * ty
    message = members * comps * 2 * strips
    span = 2 * points_y // RADIX

    spectra, warmed = with_tables(
        functools.partial(rows_kernel, total_rows=points_y),
        [
            jax.ShapeDtypeStruct((senders, message, width), F32),
            near((tx, strips * layers, width), F32),
        ],
        [block],
        [sort, *two_terms(along), turn],
        [nodes, factor, threshold, spot_row, spot_col],
        [pltpu.VMEM((tx, lines, width), F32)],
        copies=9,
    )
    data = lax.all_to_all(spectra, OUTWARD, split_axis=0, concat_axis=0, tiled=True)
    columns = members * comps * width
    field = with_tables(
        spectrum_kernel,
        jax.ShapeDtypeStruct((senders * message, width), F32),
        [data.reshape(senders * message, width)],
        [tensor, *two_terms(across), *two_terms(across_back)],
        (),
        [
            pltpu.VMEM((RADIX, 2 * span, columns), F32),
            pltpu.VMEM((RADIX, 2 * span, columns), BF16),
            pltpu.VMEM((RADIX, 2 * span, columns), BF16),
        ],
        copies=5,
        megabytes=44,
    )
    field = field.reshape(senders, message, width)
    data = lax.all_to_all(field, INWARD, split_axis=0, concat_axis=0, tiled=True)
    scale = -1.0 / (2 * layers * 2 * points_y * 2 * points_x)
    block = with_tables(
        functools.partial(cells_kernel, scale=scale),
        near((tx, lines + strips * layers, width), F32),
        [data, warmed],
        [*two_terms(along.T), turn, np.ascontiguousarray(sort.T)],
        copies=4,
    )
    block = lax.all_to_all(block, TX, split_axis=0, concat_axis=0, tiled=True)
    demag, warmed = call(
        place_kernel,
        [jax.ShapeDtypeStruct((comps * cells, width), F32), jax.ShapeDtypeStruct((cells, width), F32)],
        [VMEM],
    )(block)
    return (
        warmed.reshape(layers, count, width),
        demag.reshape(comps, layers, count, width),
    )


def solution(mesh):
    tx, ty = mesh.shape["tx"], mesh.shape["ty"]
    parts = jax.sharding.Mesh(mesh.devices.reshape(*PARTS.values()), tuple(PARTS))
    in_specs = (
        P(None, TY, TX),
        P(None, TY, TX),
        P(None, None, TY, TX),
        P(None, TX, None, TY),
        P(),
        P(),
        P(),
        P(),
        P(),
    )
    out_specs = (P(None, TY, TX), P(None, None, TY, TX))
    body = functools.partial(local, tx, ty)
    return jax.shard_map(body, mesh=parts, in_specs=in_specs, out_specs=out_specs, check_vma=False)
```

```python
import functools
import math

import jax
import jax.numpy as jnp
import ml_dtypes
import numpy as np
from jax import lax
from jax.experimental import pallas as pl
from jax.experimental.pallas import tpu as pltpu
from jax.sharding import PartitionSpec as P

SWEEPS = 2
AMBIENT_HEAT = 0.3
STEP_RATE = 0.05
LASER_POWER = 4.0
LASER_DEPTH = 4.0
ORDERING_SPREAD = 0.08
TABLE_LOW = 0.2
TABLE_SPAN = 1.6
RADIX = 4
REACH = SWEEPS
PARTS = {"x_hi": 2, "z": 4, "x_lo": 2, "y": 4, "core": 2}
TX, TY = ("x_hi", "z"), ("x_lo", "y", "core")
OUTWARD = ("x_lo", "y", "core", "x_hi", "z")
INWARD = ("y", "z", "x_lo", "x_hi", "core")
PAIRS = ((0, 3, 4), (3, 1, 5), (4, 5, 2))
VMEM = pl.BlockSpec(memory_space=pltpu.VMEM)
ANY = pl.BlockSpec(memory_space=pl.ANY)
F32 = jnp.float32
BF16 = jnp.bfloat16


def two_terms(table):
    table = np.asarray(table, np.float64)
    high = table.astype(np.float32).astype(ml_dtypes.bfloat16)
    low = (table - high.astype(np.float64)).astype(np.float32).astype(ml_dtypes.bfloat16)
    return (high, low)


def waves(products, length):
    angles = 2.0 * math.pi / length * (products % length)
    return (np.cos(angles), np.sin(angles))


def ranks(order, axes):
    sizes = [PARTS[axis] for axis in axes]
    place = dict(zip(axes, np.indices(sizes).reshape(len(axes), -1), strict=True))
    rank = np.zeros(math.prod(sizes), np.int64)
    for axis in order:
        rank = rank * PARTS[axis] + place[axis]
    return [int(r) for r in rank]


def index_of(axes):
    at = 0
    for axis in axes:
        at = at * PARTS[axis] + lax.axis_index(axis)
    return at


def split(values):
    high = values.astype(BF16)
    low = (values - high.astype(F32)).astype(BF16)
    return (high, low)


def matmul(left, right):
    return lax.dot_general(left, right, (((1,), (0,)), ((), ())), preferred_element_type=F32)


def along_tables(points):
    length = 2 * points
    span = length // RADIX
    a = np.arange(points // RADIX)
    b = np.arange(RADIX)
    v = np.arange(span)
    cosine, sine = waves(v[None, :] * (RADIX * a)[:, None], length)
    forward = np.concatenate([cosine, -sine], 1)
    turn = np.stack(waves(v[None, :] * b[:, None], length), 1).reshape(2 * RADIX, span)
    half = points // 2
    order = np.zeros((half, half), np.float32)
    x = np.arange(half)
    order[x, x % RADIX * (half // RADIX) + x // RADIX] = 1.0
    return forward, turn.astype(np.float32), order.astype(ml_dtypes.bfloat16)


def across_tables(points, groups, blocks, strips):
    length = 2 * points
    span = length // RADIX
    group, block = np.indices((groups, blocks)).reshape(2, -1)
    v = np.arange(span)
    tables = []
    for order in (OUTWARD, INWARD):
        y = np.zeros(groups * blocks, np.int64)
        y[ranks(order, TX + TY)] = strips * (groups * block + group)
        tables.append([waves(v[:, None] * (y + b)[None, :], length) for b in range(RADIX)])
    forward = np.stack([np.concatenate([c, s], 1) for c, s in tables[0]])
    back = np.stack([np.concatenate([c.T, -s.T], 1) for c, s in tables[1]])
    return forward, back


def fetch(pairs, sems):
    copies = [
        pltpu.make_async_copy(source, target, sems.at[at])
        for at, (source, target) in enumerate(pairs)
    ]
    for copy in copies:
        copy.start()
    return copies


def chosen(which, values):
    total = jnp.zeros(which.shape, F32)
    for grain in range(values.shape[0]):
        total = total + jnp.where(which == grain, values[grain], 0.0)
    return total


def edges_kernel(heat_in, kind_in, moment_in, heat, kind, moment, rows, sems):
    copies = fetch([(heat_in, heat), (kind_in, kind), (moment_in, moment)], sems)
    layers, count = 8, heat.shape[0] // 8
    copies[0].wait()
    copies[1].wait()
    for side, first in enumerate((0, count - REACH)):
        for j in range(REACH):
            at = pl.ds(first + j, layers, stride=count)
            rows[side, j] = heat[at, :]
            rows[side, REACH + j] = kind[at, :].astype(F32)
    copies[2].wait()


def send_kernel(heat, kind, moment, above, below, out):
    layers, count = 8, heat.shape[0] // 8
    groups = out.shape[0]
    strips = count // groups
    tall = strips + 2 * REACH
    for group in range(groups):
        for i in range(tall):
            y = group * strips - REACH + i
            if y < 0:
                pair = (above[y + REACH], above[y + 2 * REACH])
            elif y >= count:
                pair = (below[y - count], below[y - count + REACH])
            else:
                at = pl.ds(y, layers, stride=count)
                pair = (heat[at, :], kind[at, :].astype(F32))
            for which, value in enumerate(pair):
                at = (which * tall + i) * layers
                out[ranks(TX[::-1], TX)[group], at : at + layers, :] = value
        for comp in range(3):
            for strip in range(strips):
                at = pl.ds(comp * layers * count + group * strips + strip, layers, stride=count)
                to = (2 * tall + comp * strips + strip) * layers
                out[ranks(TX[::-1], TX)[group], to : to + layers, :] = moment[at, :]


def heat_rows(block, nodes, factor, threshold, spot_row, spot_col, total_rows):
    layers = 8
    groups, lines, width = block.shape
    total_cols = groups * width
    strips = (lines // layers - 4 * REACH) // 5
    tall = strips + 2 * REACH
    place = index_of(TY) * groups + index_of(TX)
    row_base = place * strips - REACH
    shape = (layers, total_cols)
    column = lax.broadcasted_iota(jnp.int32, shape, 1)
    depth = lax.broadcasted_iota(jnp.int32, shape, 0)
    spacing = TABLE_SPAN / (nodes.shape[0] - 1)
    slopes = [(nodes[j + 1] - nodes[j]) * (1.0 / spacing) for j in range(nodes.shape[0] - 1)]
    bases = [nodes[j] - slope * (TABLE_LOW + j * spacing) for j, slope in enumerate(slopes)]

    def whole(index):
        at = index * layers
        return jnp.concatenate(
            [block[t, at : at + layers, :] for t in ranks(TX[::-1], TX)], 1
        )

    def chosen(which, values):
        total = jnp.full(which.shape, values[0], F32)
        for grain in range(1, values.shape[0]):
            total = jnp.where(which == float(grain), values[grain], total)
        return total

    def conductivity(theta, gain):
        absolute = jnp.clip(theta + AMBIENT_HEAT, TABLE_LOW, TABLE_LOW + TABLE_SPAN)
        base = jnp.full_like(theta, bases[0])
        slope = jnp.full_like(theta, slopes[0])
        for j in range(1, len(slopes)):
            beyond = absolute >= TABLE_LOW + j * spacing
            base = jnp.where(beyond, bases[j], base)
            slope = jnp.where(beyond, slopes[j], slope)
        return gain * (base + slope * absolute)

    inside = {}
    thetas = {}
    gains = {}
    for i in range(tall):
        y = row_base + i
        inside[i] = jnp.where((y >= 0) & (y < total_rows), 1.0, 0.0)
        thetas[i] = (whole(i) - AMBIENT_HEAT) * inside[i]
        gains[i] = chosen(whole(tall + i), factor) * inside[i]
    not_bottom = depth < layers - 1
    for sweep in range(SWEEPS):
        shifted = column - spot_col[sweep] + total_cols // 2
        shifted = jnp.where(shifted < 0, shifted + total_cols, shifted)
        shifted = jnp.where(shifted >= total_cols, shifted - total_cols, shifted)
        offset = (shifted - total_cols // 2).astype(F32) * (1.0 / (0.5 * width))
        along = jnp.exp(depth.astype(F32) * (-1.0 / LASER_DEPTH)) * jnp.exp(-0.5 * offset * offset)
        k = {i: conductivity(thetas[i], gains[i]) for i in range(sweep, tall - sweep)}
        between = {
            i: (k[i] + k[i + 1]) * (thetas[i + 1] - thetas[i]) for i in range(sweep, tall - sweep - 1)
        }
        fresh = {}
        for i in range(sweep + 1, tall - sweep - 1):
            theta, own = thetas[i], k[i]
            right = (own + pltpu.roll(own, total_cols - 1, 1)) * (
                pltpu.roll(theta, total_cols - 1, 1) - theta
            )
            down = (own + pltpu.roll(own, layers - 1, 0)) * (pltpu.roll(theta, layers - 1, 0) - theta)
            down = jnp.where(not_bottom, down, 0.0)
            flux = (between[i] - between[i - 1]) + (right - pltpu.roll(right, 1, 1))
            flux = flux + (down - pltpu.roll(down, 1, 0))
            across = (row_base + i - spot_row[sweep]).astype(F32) * (1.0 / 32.0)
            across = jnp.exp(jnp.full((layers, width), -0.5, F32) * (across * across))
            source = along * jnp.concatenate([across] * groups, 1)
            value = theta + STEP_RATE * (0.5 * flux + LASER_POWER * source)
            fresh[i] = value * inside[i]
        thetas = fresh
    warmed = []
    fractions = []
    for strip in range(strips):
        value = thetas[REACH + strip] + AMBIENT_HEAT
        limit = chosen(whole(tall + REACH + strip), threshold)
        warmed.append(value)
        fractions.append(1.0 / (1.0 + jnp.exp((value - limit) * (1.0 / ORDERING_SPREAD))))
    scaled = []
    for comp in range(3):
        for strip in range(strips):
            scaled.append(whole(2 * tall + comp * strips + strip) * fractions[strip])
    return warmed, jnp.concatenate(scaled, 0)


def turns(t, sign):
    (ar, ai), (br, bi), (cr, ci), (dr, di) = t
    er, ei, fr, fi = ar + cr, ai + ci, ar - cr, ai - ci
    gr, gi, hr, hi = br + dr, bi + di, br - dr, bi - di
    minus = (fr + hi, fi - hr)
    plus = (fr - hi, fi + hr)
    one, three = (minus, plus) if sign < 0 else (plus, minus)
    return ((er + gr, ei + gi), one, (er - gr, ei - gi), three)


def matmul_terms(left, right):
    left_high, left_low = left
    right_high, right_low = right
    return matmul(
        jnp.concatenate([left_high, left_high, left_low], 1),
        jnp.concatenate([right_high, right_low, right_high], 0),
    )


def eight(x, sign):
    even, odd = turns(x[0::2], sign), turns(x[1::2], sign)
    root = math.sqrt(0.5)
    first, second = [], []
    for k in range(4):
        (er, ei), (ar, ai) = even[k], odd[k]
        if k == 1:
            ar, ai = (ar - sign * ai) * root, (ai + sign * ar) * root
        elif k == 2:
            ar, ai = -sign * ai, sign * ar
        elif k == 3:
            ar, ai = (-ar - sign * ai) * root, (-ai + sign * ar) * root
        first.append((er + ar, ei + ai))
        second.append((er - ar, ei - ai))
    return first + second


def layer_turn(value, layer, layers, high_half, sign):
    if layer == 0:
        return value
    real, imag = value
    angle = math.pi * layer / layers
    cosine = jnp.where(high_half, math.cos(angle), 1.0)
    sine = jnp.where(high_half, sign * math.sin(angle), 0.0)
    return real * cosine - imag * sine, imag * cosine + real * sine


def halves(values):
    middle = values.shape[1] // 2
    return values[:, :middle], values[:, middle:]


def rows_kernel(
    block, order_in, high_in, low_in, turn_in, nodes_in, factor_in, threshold_in, spot_row_in, spot_col_in,
    out, warmed, order, high, low, turn, nodes, factor, threshold, spot_row, spot_col, scaled, sems, *, total_rows
):
    copies = fetch(
        [
            (nodes_in, nodes), (factor_in, factor), (threshold_in, threshold),
            (spot_row_in, spot_row), (spot_col_in, spot_col),
            (order_in, order), (high_in, high), (low_in, low), (turn_in, turn),
        ],
        sems,
    )
    for copy in copies[:5]:
        copy.wait()
    groups, _, width = block.shape
    span = high.shape[1] // 2
    kept, values = heat_rows(block, nodes, factor, threshold, spot_row, spot_col, total_rows)
    layers = 8
    lines = values.shape[0]
    strips = len(kept)
    columns = []
    for t in range(groups):
        scaled[t] = values[:, t * width : (t + 1) * width]
        rows = [
            scaled[t, pl.ds(comp * strips * layers + layer, strips, stride=layers), :]
            for comp in range(3)
            for layer in range(layers)
        ]
        columns.append(jnp.concatenate(rows, 0))
    values = jnp.concatenate(columns, 1)
    for strip, value in enumerate(kept):
        for t in range(groups):
            warmed[t, strip * 8 : strip * 8 + 8, :] = value[:, t * width : (t + 1) * width]
    for copy in copies[5:]:
        copy.wait()
    both = jnp.concatenate(split(values), 0)
    both = [matmul(half, order[...]).astype(BF16) for half in halves(both)]
    piece = both[0].shape[1] // RADIX
    sorted_rows = [
        jnp.concatenate(
            [
                jnp.concatenate([half[term, b * piece : (b + 1) * piece] for half in both], 1)
                for b in range(RADIX)
            ],
            0,
        )
        for term in (slice(0, lines), slice(lines, 2 * lines))
    ]
    total = matmul_terms(sorted_rows, (high[...], low[...]))
    parts = []
    for b in range(RADIX):
        real, imag = halves(total[b * lines : (b + 1) * lines])
        if b:
            cosine, sine = turn[2 * b : 2 * b + 1, :], turn[2 * b + 1 : 2 * b + 2, :]
            real, imag = real * cosine + imag * sine, imag * cosine - real * sine
        parts.append((real, imag))
    slabs = span // width
    wide = slabs * width
    blocks = RADIX * slabs
    go = ranks(OUTWARD, TX + TY)
    high_half = lax.broadcasted_iota(jnp.int32, (2 * strips, wide), 0) >= strips
    for u, spectra in enumerate(turns(parts, -1)):
        for comp in range(3):
            layered = []
            for layer in range(layers):
                at = (comp * layers + layer // 2 * 2) * strips
                tiles = [value[at : at + 2 * strips] for value in spectra]
                moved = [pltpu.roll(tile, strips, 0) for tile in tiles]
                if layer % 2:
                    tiles, moved = moved, tiles
                both = [
                    jnp.where(high_half, other, tile)
                    for tile, other in zip(tiles, moved, strict=True)
                ]
                layered.append(layer_turn(both, layer, layers, high_half, -1))
            for t, value in enumerate(eight(layered, -1)):
                for part in range(2):
                    at = (comp * 2 + part) * 2 * strips
                    for slab in range(slabs):
                        out[go[t * blocks + u * slabs + slab], at : at + 2 * strips, :] = value[part][
                            :, slab * width : (slab + 1) * width
                        ]


def complex_table(half):
    split_at = half.shape[1] // 2
    turned = jnp.concatenate([-half[:, split_at:], half[:, :split_at]], 1)
    return jnp.concatenate([half, turned], 0)


def spectrum_kernel(
    data, tensor_in, high_in, low_in, back_high_in, back_low_in, out,
    tensor, high, low, back_high, back_low, sums, fields_high, fields_low, sems
):
    comps = 3
    width = data.shape[1]
    senders = high.shape[2] // 2
    lines = data.shape[0] // senders
    units = lines // 8
    members = units // comps
    span = high.shape[1]

    def row_of(unit, part, b):
        member, comp = divmod(unit, comps)
        return ((comp * 2 + part) * members + member) * RADIX + b

    copies = fetch(
        [
            (high_in, high), (low_in, low), (tensor_in, tensor),
            (back_high_in, back_high), (back_low_in, back_low),
        ],
        sems,
    )
    for b in range(RADIX):
        for unit in range(units):
            both = [
                data[pl.ds(row_of(unit, part, b), senders, stride=lines), :] for part in range(2)
            ]
            data_high, data_low = split(jnp.concatenate(both, 0))
            lanes = slice(unit * width, (unit + 1) * width)
            fields_high[b, : 2 * senders, lanes] = data_high
            fields_low[b, : 2 * senders, lanes] = data_low
    copies[0].wait()
    copies[1].wait()
    for b in range(RADIX):
        sums[b] = matmul_terms(
            (complex_table(high[b]), complex_table(low[b])),
            (fields_high[b, : 2 * senders], fields_low[b, : 2 * senders]),
        )
    copies[2].wait()
    piece = 16

    def multiply(step, carry):
        at = pl.multiple_of(step * piece, piece)
        for member in range(members):
            spectra = []
            for comp in range(comps):
                lanes = pl.ds((member * comps + comp) * width, width)
                t = [
                    (sums[b, pl.ds(at, piece), lanes], sums[b, pl.ds(span + at, piece), lanes])
                    for b in range(RADIX)
                ]
                spectra.append(turns(t, -1))
            field = [[None] * RADIX for _ in range(comps)]
            for u in range(RADIX):
                taps = [tensor[p, member, pl.ds(u * span + at, piece), :] for p in range(6)]
                for target in range(comps):
                    field[target][u] = tuple(
                        taps[PAIRS[target][0]] * spectra[0][u][part]
                        + taps[PAIRS[target][1]] * spectra[1][u][part]
                        + taps[PAIRS[target][2]] * spectra[2][u][part]
                        for part in range(2)
                    )
            for comp in range(comps):
                lanes = pl.ds((member * comps + comp) * width, width)
                for b, both in enumerate(turns(field[comp], 1)):
                    for part, value in enumerate(both):
                        data_high, data_low = split(value)
                        rows = pl.ds(part * span + at, piece)
                        fields_high[b, rows, lanes] = data_high
                        fields_low[b, rows, lanes] = data_low
        return carry

    lax.fori_loop(0, span // piece, multiply, 0, unroll=4)
    copies[3].wait()
    copies[4].wait()
    for b in range(RADIX):
        total = matmul_terms(
            (complex_table(back_high[b]), complex_table(back_low[b])),
            (fields_high[b], fields_low[b]),
        )
        for unit in range(units):
            for part in range(2):
                out[pl.ds(row_of(unit, part, b), senders, stride=lines), :] = total[
                    part * senders : (part + 1) * senders, unit * width : (unit + 1) * width
                ]


def cells_kernel(
    data, kept, high_in, low_in, turn_in, order_in, out, high, low, turn, order, sems, *, scale
):
    copies = fetch(
        [(high_in, high), (low_in, low), (turn_in, turn), (order_in, order)],
        sems,
    )
    groups, _, width = out.shape
    layers = 8
    strips = kept.shape[1] // layers
    lines = 3 * layers * strips
    span = high.shape[0] // 2
    slabs = span // width
    blocks = RADIX * slabs
    back = ranks(INWARD, TX + TY)
    pieces = []
    high_half = lax.broadcasted_iota(jnp.int32, (2 * strips, slabs * width), 0) >= strips
    for u in range(RADIX):
        columns = []
        for comp in range(3):
            spectra = []
            for t in range(groups):
                both = []
                for part in range(2):
                    at = (comp * 2 + part) * 2 * strips
                    both.append(
                        jnp.concatenate(
                            [
                                data[back[t * blocks + u * slabs + slab], at : at + 2 * strips, :]
                                for slab in range(slabs)
                            ],
                            1,
                        )
                    )
                spectra.append(both)
            layered = []
            for layer, value in enumerate(eight(spectra, 1)):
                value = layer_turn(value, layer, layers, high_half, 1)
                layered.append([part + pltpu.roll(part, strips, 0) for part in value])
            for layer in range(0, layers, 2):
                columns.append(
                    [
                        jnp.where(high_half, other, own)
                        for own, other in zip(layered[layer], layered[layer + 1], strict=True)
                    ]
                )
        pieces.append(tuple(jnp.concatenate([c[part] for c in columns], 0) for part in range(2)))
    for copy in copies:
        copy.wait()
    rows = []
    for b, (real, imag) in enumerate(turns(pieces, 1)):
        if b:
            cosine, sine = turn[2 * b : 2 * b + 1, :], turn[2 * b + 1 : 2 * b + 2, :]
            real, imag = real * cosine - imag * sine, imag * cosine + real * sine
        rows.append(jnp.concatenate([real, imag], 1))
    total = matmul_terms(split(jnp.concatenate(rows, 0)), (high[...], low[...])) * scale
    sorted_halves = []
    for half in halves(total):
        values = jnp.concatenate([half[b * lines : (b + 1) * lines] for b in range(RADIX)], 1)
        data_high, data_mid = split(values)
        data_low = (values - data_high.astype(F32) - data_mid.astype(F32)).astype(BF16)
        values = matmul(jnp.concatenate([data_high, data_mid, data_low], 0), order[...])
        sorted_halves.append(values[:lines] + values[lines : 2 * lines] + values[2 * lines :])
    values = jnp.concatenate(sorted_halves, 1)
    for t in range(groups):
        out[t, :lines] = values[:, t * width : (t + 1) * width]
        out[t, lines:] = kept[t]


def place_kernel(block, field, warmed):
    groups, lines, width = block.shape
    layers = 8
    count = warmed.shape[0] // layers
    strips = count // groups
    for y in range(count):
        group, strip = divmod(y, strips)
        for comp in range(4):
            if comp < 3:
                at = pl.ds(comp * strips * layers + strip, layers, stride=strips)
                field[pl.ds(comp * layers * count + y, layers, stride=count), :] = block[group, at, :]
            else:
                at = (comp * strips + strip) * layers
                warmed[pl.ds(y, layers, stride=count), :] = block[group, at : at + layers, :]


def near(shape, dtype):
    return pltpu.VMEM(shape, dtype)


def call(kernel, out_shape, in_specs, scratch=(), megabytes=16, flops=0, bytes_accessed=0):
    many = isinstance(out_shape, (list, tuple))
    return pl.pallas_call(
        kernel,
        out_shape=out_shape,
        in_specs=in_specs,
        out_specs=[VMEM] * len(out_shape) if many else VMEM,
        scratch_shapes=list(scratch),
        compiler_params=pltpu.CompilerParams(vmem_limit_bytes=megabytes * 1024 * 1024),
        cost_estimate=pl.CostEstimate(
            flops=flops, bytes_accessed=bytes_accessed, transcendentals=0
        ),
    )


def far(value):
    return pltpu.with_memory_space_constraint(value, pltpu.HBM)


def with_tables(
    kernel, out_shape, operands, tables, scalars=(), scratch=(), copies=0, megabytes=32
):
    tables = [jnp.asarray(a) for a in tables]
    return call(
        kernel,
        out_shape,
        [VMEM] * len(operands) + [ANY] * (len(tables) + len(scalars)),
        [pltpu.VMEM(a.shape, a.dtype) for a in tables]
        + [pltpu.SMEM(a.shape, a.dtype) for a in scalars]
        + list(scratch)
        + [pltpu.SemaphoreType.DMA((copies,))],
        megabytes=megabytes,
    )(*operands, *[far(a) for a in tables], *[far(a) for a in scalars])


def local(
    tx, ty, heat, kind, moment, tensor, nodes, factor, threshold, spot_row, spot_col
):
    layers, count, width = heat.shape
    strips = count // tx
    comps = 3
    lines = comps * strips * layers
    points_x, points_y = tx * width, ty * count
    members = 2
    cells = layers * count

    heat = heat.reshape(cells, width)
    kind = kind.reshape(cells, width)
    moment = moment.reshape(comps * cells, width)
    heat, kind, moment, rows = call(
        edges_kernel,
        [
            near((cells, width), F32),
            near((cells, width), jnp.int32),
            near((comps * cells, width), F32),
            near((2, 2 * REACH, layers, width), F32),
        ],
        [ANY] * 3,
        [pltpu.SemaphoreType.DMA((3,))],
    )(far(heat), far(kind), far(moment))

    def moved(value, step):
        return lax.ppermute(value, TY, [(i, (i + step) % ty) for i in range(ty)])

    above = moved(rows[1], 1)
    below = moved(rows[0], -1)
    tall = 2 * (strips + 2 * REACH) + comps * strips
    block = call(send_kernel, near((tx, tall * layers, width), F32), [VMEM] * 5)(
        heat, kind, moment, above, below
    )
    block = lax.all_to_all(block, TX[::-1], split_axis=0, concat_axis=0, tiled=True)

    along, turn, sort = along_tables(points_x)
    across, across_back = across_tables(points_y, tx, ty, strips)
    senders = tx * ty
    message = members * comps * 2 * strips
    span = 2 * points_y // RADIX

    spectra, warmed = with_tables(
        functools.partial(rows_kernel, total_rows=points_y),
        [
            jax.ShapeDtypeStruct((senders, message, width), F32),
            near((tx, strips * layers, width), F32),
        ],
        [block],
        [sort, *two_terms(along), turn],
        [nodes, factor, threshold, spot_row, spot_col],
        [pltpu.VMEM((tx, lines, width), F32)],
        copies=9,
    )
    data = lax.all_to_all(spectra, OUTWARD, split_axis=0, concat_axis=0, tiled=True)
    columns = members * comps * width
    field = with_tables(
        spectrum_kernel,
        jax.ShapeDtypeStruct((senders * message, width), F32),
        [data.reshape(senders * message, width)],
        [tensor, *two_terms(across), *two_terms(across_back)],
        (),
        [
            pltpu.VMEM((RADIX, 2 * span, columns), F32),
            pltpu.VMEM((RADIX, 2 * span, columns), BF16),
            pltpu.VMEM((RADIX, 2 * span, columns), BF16),
        ],
        copies=5,
        megabytes=44,
    )
    field = field.reshape(senders, message, width)
    data = lax.all_to_all(field, INWARD, split_axis=0, concat_axis=0, tiled=True)
    scale = -1.0 / (2 * layers * 2 * points_y * 2 * points_x)
    block = with_tables(
        functools.partial(cells_kernel, scale=scale),
        near((tx, lines + strips * layers, width), F32),
        [data, warmed],
        [*two_terms(along.T), turn, np.ascontiguousarray(sort.T)],
        copies=4,
    )
    block = lax.all_to_all(block, TX, split_axis=0, concat_axis=0, tiled=True)
    demag, warmed = call(
        place_kernel,
        [jax.ShapeDtypeStruct((comps * cells, width), F32), jax.ShapeDtypeStruct((cells, width), F32)],
        [VMEM],
    )(block)
    return (
        warmed.reshape(layers, count, width),
        demag.reshape(comps, layers, count, width),
    )


def solution(mesh):
    tx, ty = mesh.shape["tx"], mesh.shape["ty"]
    parts = jax.sharding.Mesh(mesh.devices.reshape(*PARTS.values()), tuple(PARTS))
    in_specs = (
        P(None, TY, TX),
        P(None, TY, TX),
        P(None, None, TY, TX),
        P(None, TX, None, TY),
        P(),
        P(),
        P(),
        P(),
        P(),
    )
    out_specs = (P(None, TY, TX), P(None, None, TY, TX))
    body = functools.partial(local, tx, ty)
    return jax.shard_map(body, mesh=parts, in_specs=in_specs, out_specs=out_specs, check_vma=False)
```
